32 devices in a mesh: dp: 8 (over y, x, core), ffn: 4 (over z).
Axes of the slice: x: 2, y: 2, z: 4, core: 2. Of those that a mesh axis runs over, the one named last changes fastest.
Arguments:
- block_input: bfloat16 [32768, 1024], P(('dp', 'ffn')), may hold values from -6 to 6
- cotangent: bfloat16 [32768, 1024], P(('dp', 'ffn')), may hold values from -6 to 6
- w_qkv: float32 [1024, 3072], P(None, ('dp', 'ffn')), may hold values from -0.1875 to 0.1875
- w_out: float32 [1024, 1024], P(None, ('dp', 'ffn')), may hold values from -0.5 to 0.5
- w_up: float32 [1024, 4096], P(None, ('dp', 'ffn')), may hold values from -0.1875 to 0.1875
- w_down: float32 [4096, 1024], P(('dp', 'ffn')), may hold values from -0.09375 to 0.09375
- vectors: float32 [8, 1024], P(None, ('dp', 'ffn')), may hold values from -0.6 to 1.6
- b_up: float32 [4096], P(('dp', 'ffn')), may hold values from -1.8 to 1.8
- qkv_left: float32 [1024, 1024], P(('dp', 'ffn')), may hold values from -100663296 to 402653184
- qkv_right: float32 [3072, 3072], P(('dp', 'ffn')), may hold values from -33554432 to 134217728
- out_left: float32 [1024, 1024], P(('dp', 'ffn')), may hold values from -5368709 to 21474836
- out_right: float32 [1024, 1024], P(('dp', 'ffn')), may hold values from -5368709 to 21474836
- up_left: float32 [1024, 1024], P(('dp', 'ffn')), may hold values from -12079596 to 48318382
- up_right: float32 [4096, 4096], P(('dp', 'ffn')), may hold values from -3019899 to 12079596
- down_left: float32 [4096, 4096], P(('dp', 'ffn')), may hold values from -14176748 to 5.670699e+07
- down_right: float32 [1024, 1024], P(('dp', 'ffn')), may hold values from -5.670699e+07 to 2.2682796e+08
- qkv_left_root: float32 [1024, 1024], P(('dp', 'ffn')), may hold values from -0.009983486 to 0.039933944
- qkv_right_root: float32 [3072, 3072], P(('dp', 'ffn')), may hold values from -0.0131390065 to 0.052556026
- out_left_root: float32 [1024, 1024], P(('dp', 'ffn')), may hold values from -0.020774593 to 0.083098373
- out_right_root: float32 [1024, 1024], P(('dp', 'ffn')), may hold values from -0.020774593 to 0.083098373
- up_left_root: float32 [1024, 1024], P(('dp', 'ffn')), may hold values from -0.016962384 to 0.06784954
- up_right_root: float32 [4096, 4096], P(('dp', 'ffn')), may hold values from -0.023988434122900557 to 0.09595374
- down_left_root: float32 [4096, 4096], P(('dp', 'ffn')), may hold values from -0.016296932 to 0.06518773
- down_right_root: float32 [1024, 1024], P(('dp', 'ffn')), may hold values from -0.011523671 to 0.046094684
- vector_stat: float32 [8, 1024], P(None, ('dp', 'ffn')), may hold values from 16384 to 65536
- b_up_stat: float32 [4096], P(('dp', 'ffn')), may hold values from 2949.12 to 11796.48
Outputs:
- block_output: bfloat16 [32768, 1024], P(('dp', 'ffn'))
- input_grad: bfloat16 [32768, 1024], P(('dp', 'ffn'))
- qkv_grad: float32 [1024, 3072], P(None, ('dp', 'ffn'))
- out_grad: float32 [1024, 1024], P(None, ('dp', 'ffn'))
- up_grad: float32 [1024, 4096], P(None, ('dp', 'ffn'))
- down_grad: float32 [4096, 1024], P(('dp', 'ffn'))
- vector_grad: float32 [8, 1024], P(None, ('dp', 'ffn'))
- b_up_grad: float32 [4096], P(('dp', 'ffn'))
- new_qkv_left: float32 [1024, 1024], P(('dp', 'ffn'))
- new_qkv_right: float32 [3072, 3072], P(('dp', 'ffn'))
- new_out_left: float32 [1024, 1024], P(('dp', 'ffn'))
- new_out_right: float32 [1024, 1024], P(('dp', 'ffn'))
- new_up_left: float32 [1024, 1024], P(('dp', 'ffn'))
- new_up_right: float32 [4096, 4096], P(('dp', 'ffn'))
- new_down_left: float32 [4096, 4096], P(('dp', 'ffn'))
- new_down_right: float32 [1024, 1024], P(('dp', 'ffn'))
- new_vector_stat: float32 [8, 1024], P(None, ('dp', 'ffn'))
- new_b_up_stat: float32 [4096], P(('dp', 'ffn'))
- new_w_qkv: float32 [1024, 3072], P(None, ('dp', 'ffn'))
- new_w_out: float32 [1024, 1024], P(None, ('dp', 'ffn'))
- new_w_up: float32 [1024, 4096], P(None, ('dp', 'ffn'))
- new_w_down: float32 [4096, 1024], P(('dp', 'ffn'))
- new_vectors: float32 [8, 1024], P(None, ('dp', 'ffn'))
- new_b_up: float32 [4096], P(('dp', 'ffn'))
The draws below stay inside these ranges and needn't reach their ends.
All inputs are finite; a program needn't handle non-finite values.
Results may differ from the reference program's by a relative error of at most 0.025.
Values may be sent and summed in bfloat16 or wider, within the bound.
A program may use at most 448 MiB of HBM per device.

```python
import math
import jax
import jax.numpy as jnp
from jax import lax

D = 1024
HEADS = 8
HEAD_DIM = 128
FF = 4096
TOK_DEV = 1024
TOKENS = 32768


def stat_matrix(key, extent, scale, power):
    first, second = jax.random.split(key)
    level = jax.random.uniform(first, (extent,), jnp.float32) ** power
    diagonal = scale * 4.0 ** level
    noise = jnp.clip(jax.random.normal(second, (extent, extent), jnp.float32), -4.0, 4.0)
    mirrored = 0.5 * (noise + noise.T) * (0.6 * scale / math.sqrt(extent))
    identity = jnp.eye(extent, dtype=jnp.float32)
    return mirrored * (1.0 - identity) + identity * diagonal[None, :]


def positive_rows(key, shape, scale, power):
    level = jax.random.uniform(key, shape, jnp.float32) ** power
    return scale * 4.0 ** level


def draw_vectors(key, part):
    key = jax.random.fold_in(key, 1)
    spread = 0.2 * jnp.clip(jax.random.normal(key, (8, D), jnp.float32), -3.0, 3.0)
    gains = jnp.array([1.0, 0.0, 0.0, 0.0, 0.0, 1.0, 0.0, 0.0], jnp.float32)
    return spread + gains[:, None]


def draw_qkv_left(key, part):
    key = jax.random.fold_in(key, 2)
    power = 1.0
    return stat_matrix(key, D, 3.0 * D * TOKENS, power)


def draw_qkv_right(key, part):
    key = jax.random.fold_in(key, 3)
    power = 1.0
    return stat_matrix(key, 3 * D, 1.0 * D * TOKENS, power)


def draw_out_left(key, part):
    key = jax.random.fold_in(key, 4)
    power = 1.0
    return stat_matrix(key, D, 0.16 * D * TOKENS, power)


def draw_out_right(key, part):
    key = jax.random.fold_in(key, 5)
    power = 1.0
    return stat_matrix(key, D, 0.16 * D * TOKENS, power)


def draw_up_left(key, part):
    key = jax.random.fold_in(key, 6)
    power = 1.0
    return stat_matrix(key, D, 0.09 * FF * TOKENS, power)


def draw_up_right(key, part):
    key = jax.random.fold_in(key, 7)
    power = 1.0
    return stat_matrix(key, FF, 0.09 * D * TOKENS, power)


def draw_down_left(key, part):
    key = jax.random.fold_in(key, 8)
    power = 1.0
    return stat_matrix(key, FF, 0.4225 * D * TOKENS, power)


def draw_down_right(key, part):
    key = jax.random.fold_in(key, 9)
    power = 1.0
    return stat_matrix(key, D, 0.4225 * FF * TOKENS, power)


def draw_qkv_left_root(key, part):
    key = jax.random.fold_in(key, 12)
    power = 1.0
    return stat_matrix(key, D, (3.0 * D * TOKENS) ** (-0.25), power)


def draw_qkv_right_root(key, part):
    key = jax.random.fold_in(key, 13)
    power = 1.0
    return stat_matrix(key, 3 * D, (1.0 * D * TOKENS) ** (-0.25), power)


def draw_out_left_root(key, part):
    key = jax.random.fold_in(key, 14)
    power = 1.0
    return stat_matrix(key, D, (0.16 * D * TOKENS) ** (-0.25), power)


def draw_out_right_root(key, part):
    key = jax.random.fold_in(key, 15)
    power = 1.0
    return stat_matrix(key, D, (0.16 * D * TOKENS) ** (-0.25), power)


def draw_up_left_root(key, part):
    key = jax.random.fold_in(key, 16)
    power = 1.0
    return stat_matrix(key, D, (0.09 * FF * TOKENS) ** (-0.25), power)


def draw_up_right_root(key, part):
    key = jax.random.fold_in(key, 17)
    power = 1.0
    return stat_matrix(key, FF, (0.09 * D * TOKENS) ** (-0.25), power)


def draw_down_left_root(key, part):
    key = jax.random.fold_in(key, 18)
    power = 1.0
    return stat_matrix(key, FF, (0.4225 * D * TOKENS) ** (-0.25), power)


def draw_down_right_root(key, part):
    key = jax.random.fold_in(key, 19)
    power = 1.0
    return stat_matrix(key, D, (0.4225 * FF * TOKENS) ** (-0.25), power)


def draw_vector_stat(key, part):
    key = jax.random.fold_in(key, 20)
    power = 1.0
    return positive_rows(key, (8, D), 0.5 * TOKENS, power)


def draw_b_up_stat(key, part):
    key = jax.random.fold_in(key, 21)
    power = 1.0
    return positive_rows(key, (FF,), 0.09 * TOKENS, power)


def with_spikes(entries, key, source, target, parts, factor):
    def block_of(position):
        return (jnp.arange(entries.shape[position]) // (entries.shape[position] // parts)).reshape((-1,) + (1,) * (entries.ndim - 1 - position))

    first = jax.random.permutation(key, parts)[block_of(target)]
    other_side = (block_of(target) + parts // 2) % parts
    return jnp.where((block_of(source) == first) | (block_of(source) == other_side), factor * entries, entries)


def block_levels(own_key, dims, shards, least, top_value):
    def one(axis_at, parts):
        steps = jax.random.uniform(jax.random.fold_in(jax.random.fold_in(own_key, 6), axis_at), (parts,), jnp.float32, least / len(shards), top_value / len(shards))
        return jnp.repeat(jnp.exp(steps), dims[axis_at] // parts).reshape((-1,) + (1,) * (len(dims) - axis_at - 1))

    level = one(*shards[0])
    for cut in shards[1:]:
        level = level * one(*cut)
    return level


def bell_draw(own_key, shape, deviation, reach, cuts=(), kind=jnp.bfloat16):
    factor_of = block_levels(own_key, shape, cuts, -0.22, 0.18) if cuts else 1.0
    result = jax.random.normal(own_key, shape, jnp.float32) * deviation * factor_of
    return jnp.minimum(jnp.maximum(result, -reach), reach).astype(kind)


def bell_draw_with(key, shape, scale, limit, cuts, heavy, kind=jnp.bfloat16):
    values = scale * jax.random.normal(key, shape, jnp.float32)
    if cuts:
        values = values * block_levels(key, shape, cuts, -0.22, 0.18)
    return jnp.clip(with_spikes(values, jax.random.fold_in(key, 3), *heavy), -limit, limit).astype(kind)


def setup_inputs(seed: int = 0) -> dict:
    seeds = jax.random.split(jax.random.key(seed), 27)
    return {
        "block_input": bell_draw(seeds[0], (TOKENS, D), 1.0, 6.0, ((0, 32),)),
        "cotangent": bell_draw_with(seeds[1], (TOKENS, D), 1.0, 6.0, ((0, 32),), (0, 1, 32, 2.75)),
        "w_qkv": bell_draw(seeds[2], (D, 3 * D), D ** -0.5, 0.1875, ((1, 32),), jnp.float32),
        "w_out": bell_draw(seeds[3], (D, D), (D // 8) ** -0.5, 0.5, ((1, 32),), jnp.float32),
        "w_up": bell_draw(seeds[4], (D, FF), D ** -0.5, 0.1875, ((1, 32),), jnp.float32),
        "w_down": bell_draw(seeds[5], (FF, D), FF ** -0.5, 0.09375, ((0, 32),), jnp.float32),
        "vectors": draw_vectors(jax.random.fold_in(seeds[26], 71), 0),
        "b_up": bell_draw(seeds[7], (FF,), 0.3, 1.8, ((0, 32),), jnp.float32),
        "qkv_left": draw_qkv_left(jax.random.fold_in(seeds[26], 71), 0),
        "qkv_right": draw_qkv_right(jax.random.fold_in(seeds[26], 71), 0),
        "out_left": draw_out_left(jax.random.fold_in(seeds[26], 71), 0),
        "out_right": draw_out_right(jax.random.fold_in(seeds[26], 71), 0),
        "up_left": draw_up_left(jax.random.fold_in(seeds[26], 71), 0),
        "up_right": draw_up_right(jax.random.fold_in(seeds[26], 71), 0),
        "down_left": draw_down_left(jax.random.fold_in(seeds[26], 71), 0),
        "down_right": draw_down_right(jax.random.fold_in(seeds[26], 71), 0),
        "qkv_left_root": draw_qkv_left_root(jax.random.fold_in(seeds[26], 71), 0),
        "qkv_right_root": draw_qkv_right_root(jax.random.fold_in(seeds[26], 71), 0),
        "out_left_root": draw_out_left_root(jax.random.fold_in(seeds[26], 71), 0),
        "out_right_root": draw_out_right_root(jax.random.fold_in(seeds[26], 71), 0),
        "up_left_root": draw_up_left_root(jax.random.fold_in(seeds[26], 71), 0),
        "up_right_root": draw_up_right_root(jax.random.fold_in(seeds[26], 71), 0),
        "down_left_root": draw_down_left_root(jax.random.fold_in(seeds[26], 71), 0),
        "down_right_root": draw_down_right_root(jax.random.fold_in(seeds[26], 71), 0),
        "vector_stat": draw_vector_stat(jax.random.fold_in(seeds[26], 71), 0),
        "b_up_stat": draw_b_up_stat(jax.random.fold_in(seeds[26], 71), 0),
    }


norm_epsilon = 1e-05
decay_rate = 0.5
matrix_rate = 0.5
vector_rate = 0.1
masked_score = -1e+30

@jax.custom_vjp
def low(v):
    return lax.optimization_barrier(v.astype(jnp.bfloat16)).astype(jnp.float32)

@jax.custom_vjp
def low_back(v):
    return v

def low_keep(v):
    return (low(v), None)

def low_pass(kept, grad):
    return (grad,)

def back_keep(v):
    return (v, None)

def back_low(kept, grad):
    return (low(grad),)
low.defvjp(low_keep, low_pass)
low_back.defvjp(back_keep, back_low)

def matmul(left, right):
    return jnp.dot(left, right, precision=lax.Precision.HIGHEST, preferred_element_type=jnp.float32)

def layer_norm(values, gain, shift):
    center = values - lax.optimization_barrier(jnp.mean(values, axis=-1, keepdims=True))
    inverse = lax.rsqrt(lax.optimization_barrier(jnp.mean(center * center, axis=-1, keepdims=True)) + norm_epsilon)
    return center * inverse * gain + shift

def sequence_layer(weights, sequence):
    qkv_low, out_low, up_low, down_low, vector_rows, bias_low = weights
    length = sequence.shape[0]
    normed_one = low(layer_norm(sequence, vector_rows[0], vector_rows[1]))
    qkv_bias = jnp.concatenate([vector_rows[2], jnp.zeros_like(vector_rows[2]), vector_rows[3]])
    projected = low(low_back(matmul(normed_one, qkv_low) + qkv_bias))
    queries = projected[:, :D].reshape(length, HEADS, HEAD_DIM)
    keys = projected[:, D:2 * D].reshape(length, HEADS, HEAD_DIM)
    values = projected[:, 2 * D:].reshape(length, HEADS, HEAD_DIM)
    raw = jnp.einsum('qhd,khd->hqk', queries, keys, precision=lax.Precision.HIGHEST)
    rows = lax.broadcasted_iota(jnp.int32, (length, length), 0)
    cols = lax.broadcasted_iota(jnp.int32, (length, length), 1)
    slopes = 2.0 ** (-8.0 * (jnp.arange(HEADS).astype(jnp.float32) + 1.0) / HEADS)
    distance = (rows - cols).astype(jnp.float32)
    scores = raw * HEAD_DIM ** (-0.5) - slopes[:, None, None] * distance[None]
    scores = low_back(jnp.where((cols <= rows)[None], scores, masked_score))
    probs = low(jax.nn.softmax(scores, axis=-1))
    mixed = jnp.einsum('hqk,khd->qhd', probs, values, precision=lax.Precision.HIGHEST)
    mixed = low(low_back(mixed.reshape(length, D)))
    attended = low_back(matmul(mixed, out_low) + vector_rows[4])
    residual = sequence + attended
    normed_two = low(layer_norm(residual, vector_rows[5], vector_rows[6]))
    pre = low_back(matmul(normed_two, up_low) + bias_low)
    hidden = low(jax.nn.gelu(pre, approximate=False))
    branch = low_back(matmul(hidden, down_low) + vector_rows[7])
    return residual + branch

def forward(w_qkv, w_out, w_up, w_down, vectors, b_up, inputs):
    weights = (low(w_qkv), low(w_out), low(w_up), low(w_down), low(vectors), low(b_up))
    sequences = inputs.reshape(-1, TOK_DEV, D)
    layer = jax.checkpoint(sequence_layer)
    outputs = lax.map(lambda sequence: layer(weights, sequence), sequences)
    return outputs.reshape(-1, D)

def shampoo(weight, grad, left, right, left_root, right_root, right_first):
    grad_low = low(grad)
    new_left = decay_rate * left + (1.0 - decay_rate) * matmul(grad_low, grad_low.T)
    new_right = decay_rate * right + (1.0 - decay_rate) * matmul(grad_low.T, grad_low)
    left_low = low(left_root)
    right_low = low(right_root)
    if right_first:
        step = matmul(left_low, low(matmul(grad_low, right_low.T)))
    else:
        step = matmul(low(matmul(left_low, grad_low)), right_low.T)
    return (new_left, new_right, weight - matrix_rate * step)

def diagonal_update(values, grad, stat):
    new_stat = decay_rate * stat + (1.0 - decay_rate) * grad * grad
    return (new_stat, values - vector_rate * grad * lax.rsqrt(new_stat))

def reference(block_input, cotangent, w_qkv, w_out, w_up, w_down, vectors, b_up, qkv_left, qkv_right, out_left, out_right, up_left, up_right, down_left, down_right, qkv_left_root, qkv_right_root, out_left_root, out_right_root, up_left_root, up_right_root, down_left_root, down_right_root, vector_stat, b_up_stat):
    inputs = block_input.astype(jnp.float32)
    output, pullback = jax.vjp(forward, w_qkv, w_out, w_up, w_down, vectors, b_up, inputs)
    qkv_grad, out_grad, up_grad, down_grad, vector_grad, b_up_grad, input_grad = pullback(cotangent.astype(jnp.float32))
    new_qkv_left, new_qkv_right, new_w_qkv = shampoo(w_qkv, qkv_grad, qkv_left, qkv_right, qkv_left_root, qkv_right_root, True)
    new_out_left, new_out_right, new_w_out = shampoo(w_out, out_grad, out_left, out_right, out_left_root, out_right_root, True)
    new_up_left, new_up_right, new_w_up = shampoo(w_up, up_grad, up_left, up_right, up_left_root, up_right_root, True)
    new_down_left, new_down_right, new_w_down = shampoo(w_down, down_grad, down_left, down_right, down_left_root, down_right_root, False)
    new_vector_stat, new_vectors = diagonal_update(vectors, vector_grad, vector_stat)
    new_b_up_stat, new_b_up = diagonal_update(b_up, b_up_grad, b_up_stat)
    return (output.astype(jnp.bfloat16), input_grad.astype(jnp.bfloat16), qkv_grad, out_grad, up_grad, down_grad, vector_grad, b_up_grad, new_qkv_left, new_qkv_right, new_out_left, new_out_right, new_up_left, new_up_right, new_down_left, new_down_right, new_vector_stat, new_b_up_stat, new_w_qkv, new_w_out, new_w_up, new_w_down, new_vectors, new_b_up)
```

```python
import functools

import jax
import jax.numpy as jnp
from jax import lax
from jax.experimental import pallas as pl
from jax.experimental.pallas import tpu as pltpu
from jax.sharding import PartitionSpec as P

D = 1024
HEADS = 8
HEAD_DIM = 128
MESH = pl.DeviceIdType.MESH
ALL = ("dp", "ffn")
BF = jnp.bfloat16
F32 = jnp.float32
MIB = 2**20

norm_epsilon = 1e-05
decay_rate = 0.5
matrix_rate = 0.5
vector_rate = 0.1
masked_score = -1e30


def layer_norm(values, gain, shift):
    center = values - jnp.mean(values, axis=-1, keepdims=True)
    inverse = lax.rsqrt(jnp.mean(center * center, axis=-1, keepdims=True) + norm_epsilon)
    normed = center * inverse
    return (normed * gain + shift, normed, inverse)


def norm_backward(grad, normed, inverse, gain):
    scaled = grad * gain
    inner = (
        scaled
        - jnp.mean(scaled, axis=-1, keepdims=True)
        - normed * jnp.mean(scaled * normed, axis=-1, keepdims=True)
    )
    return (inner * inverse, jnp.sum(grad * normed, axis=0), jnp.sum(grad, axis=0))


def dot_nt(left, right):
    return lax.dot_general(left, right, (((1,), (1,)), ((), ())), preferred_element_type=F32)


def dot_tn(left, right):
    return lax.dot_general(left, right, (((0,), (0,)), ((), ())), preferred_element_type=F32)


def dot_nn(left, right):
    return jnp.dot(left, right, preferred_element_type=F32)


def coords():
    dp = lax.axis_index("dp")
    return dp // 2, dp % 2, lax.axis_index("ffn")


def flip(value, mask):
    result = value
    bit = 1
    while bit <= mask:
        if mask & bit:
            result = result + bit - 2 * bit * ((result // bit) % 2)
        bit *= 2
    return result


def greet():
    p, c, z = coords()
    barrier = pltpu.get_barrier_semaphore()
    peers = [(flip(p, 1) * 2 + c, z), (flip(p, 2) * 2 + c, z), (p * 2 + 1 - c, z)]
    peers += [(p * 2 + c, flip(z, k)) for k in (1, 2, 3)]
    for peer in peers:
        pl.semaphore_signal(barrier, inc=1, device_id=peer, device_id_type=MESH)
    pl.semaphore_wait(barrier, len(peers))


FIRST = (1, 2)
SECOND = (2, 1)
GATHER_COPIES = 31
REDUCE_COPIES = 31


def gather_steps(shard, out, send, recv, local_sem):
    p, c, z = coords()
    half_rows = shard.shape[0] // 2
    copies = {}
    local = pltpu.make_async_copy(shard, out.at[p, c, z], local_sem)

    def post(name, src, dst, device):
        at = len(copies)
        copies[name] = pltpu.make_async_remote_copy(
            src, dst, send.at[at], recv.at[at], device_id=device, device_id_type=MESH
        )
        copies[name].start()

    def half(ref, h):
        return ref.at[pl.ds(h * half_rows, half_rows)]

    def spread(k):
        for name, turn in (("first", FIRST), ("second", SECOND)):
            for h in (0, 1):
                dst = half(out.at[p, c, flip(z, k)], h)
                src = dst if k else half(shard, h)
                post((name, k, h), src, dst, (flip(p, turn[h]) * 2 + c, z))

    def begin():
        local.start()
        for k in (1, 2, 3):
            post(("z", k), shard, out.at[p, c, z], (p * 2 + c, flip(z, k)))
        spread(0)

    def landed(k):
        copies["z", k].wait_recv()
        spread(k)

    def forward(k):
        for h in (0, 1):
            copies["first", k, h].wait_recv()
            piece = half(out.at[flip(p, FIRST[h]), c, flip(z, k)], h)
            post(("relay", k, h), piece, piece, (flip(p, SECOND[h]) * 2 + c, z))

    def share(k):
        for h in (0, 1):
            copies["second", k, h].wait_recv()
            copies["relay", k, h].wait_recv()
        if k == 0:
            local.wait()
        piece = out.at[:, c, flip(z, k)]
        post(("core", k), piece, piece, (p * 2 + 1 - c, z))

    def finish():
        for k in range(4):
            copies["core", k].wait_recv()
        for copy in copies.values():
            copy.wait_send()

    plan = [begin, (landed, 1), (forward, 0), (landed, 2), (forward, 1), (share, 0), (landed, 3)]
    plan += [(forward, 2), (share, 1), (forward, 3), (share, 2), (share, 3), finish]
    return plan


def reduce_steps(parts, out, held, from_core, from_second, from_first, from_z, send, recv, load):
    p, c, z = coords()
    half_rows = parts.shape[-2] // 2
    copies = {}
    loads = {}
    order = (1, 2, 3, 0)

    def post(name, src, dst, device):
        at = len(copies)
        copies[name] = pltpu.make_async_remote_copy(
            src, dst, send.at[at], recv.at[at], device_id=device, device_id_type=MESH
        )
        copies[name].start()

    def half(h):
        return pl.ds(h * half_rows, half_rows)

    def begin():
        for k in order:
            post(("core", k), parts.at[:, 1 - c, flip(z, k)], from_core.at[k], (p * 2 + 1 - c, z))
            loads[k] = pltpu.make_async_copy(
                parts.at[:, c, flip(z, k)], held.at[k], load.at[k]
            )
            loads[k].start()

    def add(dst, *sources):
        total = dst[...].astype(F32)
        for source in sources:
            total = total + source[...].astype(F32)
        dst[...] = total.astype(BF)

    def cores(k):
        loads[k].wait()
        copies["core", k].wait_recv()
        for j in range(4):
            add(held.at[k, j], from_core.at[k, j])
        for h in (0, 1):
            for j, q in ((1, flip(p, 3)), (0, flip(p, SECOND[h]))):
                post(
                    ("second", k, h, j),
                    held.at[k, q, half(h)],
                    from_second.at[k, h, j],
                    (flip(p, SECOND[h]) * 2 + c, z),
                )

    def second(k):
        for h in (0, 1):
            copies["second", k, h, 1].wait_recv()
            q = flip(p, FIRST[h])
            add(held.at[k, q, half(h)], from_second.at[k, h, 1])
            post(("first", k, h), held.at[k, q, half(h)], from_first.at[k, h], (q * 2 + c, z))

    def first(k):
        for h in (0, 1):
            copies["second", k, h, 0].wait_recv()
            copies["first", k, h].wait_recv()
            add(held.at[k, p, half(h)], from_second.at[k, h, 0], from_first.at[k, h])
        if k:
            post(("z", k), held.at[k, p], from_z.at[k - 1], (p * 2 + c, flip(z, k)))

    def finish():
        for k in (1, 2, 3):
            copies["z", k].wait_recv()
        total = held[0, p].astype(F32)
        for k in range(3):
            total = total + from_z[k].astype(F32)
        out[...] = total
        for copy in copies.values():
            copy.wait_send()

    plan = [begin, (cores, 1), (cores, 2), (second, 1), (cores, 3), (second, 2), (first, 1)]
    plan += [(cores, 0), (second, 3), (first, 2), (second, 0), (first, 3), (first, 0), finish]
    return plan


def run_step(step):
    if isinstance(step, tuple):
        step[0](step[1])
    else:
        step()


def interleave(plans, offset):
    total = max(len(plan) + offset * g for g, plan in enumerate(plans))
    merged = []
    for t in range(total):
        for g, plan in enumerate(plans):
            at = t - offset * g
            if 0 <= at < len(plan):
                merged.append(plan[at])
    return merged


def gather_kernel(count, *refs):
    ins, outs = refs[:count], refs[count : 2 * count]
    send, recv, local = refs[2 * count :]
    greet()
    plans = [
        gather_steps(ins[g], outs[g], send.at[g], recv.at[g], local.at[g]) for g in range(count)
    ]
    for step in interleave(plans, 7):
        run_step(step)


def reduce_kernel(count, *refs):
    ins, outs = refs[:count], refs[count : 2 * count]
    scratch = refs[2 * count :]
    greet()
    plans = [reduce_steps(ins[g], outs[g], *scratch[8 * g : 8 * g + 8]) for g in range(count)]
    for step in interleave(plans, 7):
        run_step(step)


def reduce_scratch(rows, width):
    return [
        pltpu.VMEM((4, 4, rows, width), BF),
        pltpu.VMEM((4, 4, rows, width), BF),
        pltpu.VMEM((4, 2, 2, rows // 2, width), BF),
        pltpu.VMEM((4, 2, rows // 2, width), BF),
        pltpu.VMEM((3, rows, width), BF),
        pltpu.SemaphoreType.DMA((REDUCE_COPIES,)),
        pltpu.SemaphoreType.DMA((REDUCE_COPIES,)),
        pltpu.SemaphoreType.DMA((4,)),
    ]


def fits_grid(rows):
    return (
        lax.axis_size("dp") == 8 and lax.axis_size("ffn") == 4 and all(r % 32 == 0 for r in rows)
    )


def gather_all(shards, collective_id):
    if not fits_grid([item.shape[0] for item in shards]):
        return [lax.all_gather(item, ALL, axis=0, tiled=True) for item in shards]
    count = len(shards)
    anywhere = pl.BlockSpec(memory_space=pl.ANY)
    outs = pl.pallas_call(
        functools.partial(gather_kernel, count),
        out_shape=tuple(jax.ShapeDtypeStruct((4, 2, 4) + item.shape, BF) for item in shards),
        in_specs=[anywhere] * count,
        out_specs=(anywhere,) * count,
        scratch_shapes=[
            pltpu.SemaphoreType.DMA((count, GATHER_COPIES)),
            pltpu.SemaphoreType.DMA((count, GATHER_COPIES)),
            pltpu.SemaphoreType.DMA((count,)),
        ],
        compiler_params=pltpu.CompilerParams(collective_id=collective_id, has_side_effects=True),
    )(*shards)
    return [item.reshape(-1, item.shape[-1]) for item in outs]


def reduce_all(parts, collective_id):
    devices = lax.axis_size("dp") * lax.axis_size("ffn")
    rows = [item.shape[0] // devices for item in parts]
    if not fits_grid(rows):
        return [
            lax.psum_scatter(item.astype(BF), ALL, scatter_dimension=0, tiled=True).astype(F32)
            for item in parts
        ]
    count = len(parts)
    scratch = []
    for item, r in zip(parts, rows):
        scratch += reduce_scratch(r, item.shape[-1])
    outs = pl.pallas_call(
        functools.partial(reduce_kernel, count),
        out_shape=tuple(
            jax.ShapeDtypeStruct((r, item.shape[-1]), F32) for item, r in zip(parts, rows)
        ),
        in_specs=[pl.BlockSpec(memory_space=pl.ANY)] * count,
        out_specs=(pl.BlockSpec(memory_space=pltpu.VMEM),) * count,
        scratch_shapes=scratch,
        compiler_params=pltpu.CompilerParams(
            collective_id=collective_id, has_side_effects=True, vmem_limit_bytes=56 * MIB
        ),
    )(*[item.reshape(4, 2, 4, r, item.shape[-1]) for item, r in zip(parts, rows)])
    return list(outs)


QUERY_BLOCK = 256


def scores_t(query, keys, slope, start, rows):
    raw = dot_nt(keys, query)
    at_key = lax.broadcasted_iota(jnp.int32, (rows, 1), 0).astype(F32)
    return raw * HEAD_DIM ** (-0.5) + at_key * slope


def mask_t(scores, start, rows, width):
    at_key = lax.broadcasted_iota(jnp.int32, (rows, width), 0)
    at_query = lax.broadcasted_iota(jnp.int32, (rows, width), 1) + start
    return jnp.where(at_key <= at_query, scores, masked_score)


def head_slope(head):
    level = head.astype(F32) + 1.0
    return jnp.exp2(jnp.full((1, 1), -8.0 / HEADS, F32) * level)


def attend_kernel(q_ref, k_ref, v_ref, o_ref, lse_ref):
    slope = head_slope(pl.program_id(0))
    length = q_ref.shape[0]
    values_t = v_ref[...].astype(F32).T.astype(BF)
    for start in range(0, length, QUERY_BLOCK):
        rows = start + QUERY_BLOCK
        scores = scores_t(q_ref[start:rows, :], k_ref[:rows, :], slope, start, rows)
        scores = mask_t(scores, start, rows, QUERY_BLOCK)
        highest = jnp.max(scores, axis=0, keepdims=True)
        weights = jnp.exp(scores - highest)
        totals = jnp.sum(weights, axis=0, keepdims=True)
        mixed = dot_nn(values_t[:, :rows], weights.astype(BF)) / totals
        o_ref[start:rows, :] = mixed.T.astype(BF)
        lse_ref[0, :, start:rows] = highest + jnp.log(totals)


def attend(projected):
    tokens = projected.shape[0]
    column = lambda offset: pl.BlockSpec((tokens, HEAD_DIM), lambda h: (0, offset + h))
    return pl.pallas_call(
        attend_kernel,
        grid=(HEADS,),
        out_shape=(
            jax.ShapeDtypeStruct((tokens, D), BF),
            jax.ShapeDtypeStruct((HEADS, 1, tokens), F32),
        ),
        in_specs=[column(0), column(HEADS), column(2 * HEADS)],
        out_specs=(column(0), pl.BlockSpec((1, 1, tokens), lambda h: (h, 0, 0))),
        compiler_params=pltpu.CompilerParams(vmem_limit_bytes=48 * MIB),
    )(projected, projected, projected)


def attend_back_kernel(q_ref, k_ref, v_ref, do_ref, lse_ref, out_ref, dk, dv):
    slope = head_slope(pl.program_id(0))
    length = q_ref.shape[0]
    scale = HEAD_DIM ** (-0.5)
    keys_t = k_ref[...].astype(F32).T.astype(BF)
    for start in reversed(range(0, length, QUERY_BLOCK)):
        rows = start + QUERY_BLOCK
        query = q_ref[start:rows, :]
        upstream = do_ref[start:rows, :]
        scores = scores_t(query, k_ref[:rows, :], slope, start, rows)
        scores = mask_t(scores, start, rows, QUERY_BLOCK)
        probs = jnp.exp(scores - lse_ref[0, :, start:rows])
        prob_grad = dot_nt(v_ref[:rows, :], upstream)
        weighted = probs * prob_grad
        centered = jnp.sum(weighted, axis=0, keepdims=True)
        score_grad = (weighted - probs * centered).astype(BF)
        out_ref[0, start:rows, :] = (dot_nn(keys_t[:, :rows], score_grad) * scale).T.astype(BF)
        key_part = dot_nn(score_grad, query)
        value_part = dot_nn(probs.astype(BF), upstream)
        if rows == length:
            dk[...] = key_part
            dv[...] = value_part
        else:
            dk[:rows, :] += key_part
            dv[:rows, :] += value_part
    out_ref[1] = (dk[...] * scale).astype(BF)
    out_ref[2] = dv[...].astype(BF)


def attend_back(projected, upstream, lse):
    tokens = projected.shape[0]
    column = lambda offset: pl.BlockSpec((tokens, HEAD_DIM), lambda h: (0, offset + h))
    return pl.pallas_call(
        attend_back_kernel,
        grid=(HEADS,),
        out_shape=jax.ShapeDtypeStruct((3, tokens, D), BF),
        in_specs=[
            column(0),
            column(HEADS),
            column(2 * HEADS),
            column(0),
            pl.BlockSpec((1, 1, tokens), lambda h: (h, 0, 0)),
        ],
        out_specs=pl.BlockSpec((3, tokens, HEAD_DIM), lambda h: (0, 0, h)),
        scratch_shapes=[pltpu.VMEM((tokens, HEAD_DIM), F32), pltpu.VMEM((tokens, HEAD_DIM), F32)],
        compiler_params=pltpu.CompilerParams(vmem_limit_bytes=48 * MIB),
    )(projected, projected, projected, upstream, lse)


def gelu_pair(pre):
    half = 0.5 * (1.0 + lax.erf(pre * 0.7071067811865476))
    slope = half + pre * jnp.exp(-0.5 * pre * pre) * 0.3989422804014327
    return pre * half, slope


def hidden_kernel(acts_ref, up_ref, bias_ref, hidden_ref, slope_ref):
    pre = dot_nt(acts_ref[...], up_ref[...]) + bias_ref[...]
    hidden, slope = gelu_pair(pre)
    hidden_ref[...] = hidden.astype(BF)
    slope_ref[...] = slope.astype(BF)


def hidden_units(acts, up_full, bias):
    tokens = acts.shape[0]
    units = up_full.shape[0]
    block = 512
    column = pl.BlockSpec((tokens, block), lambda n: (0, n))
    return pl.pallas_call(
        hidden_kernel,
        grid=(units // block,),
        out_shape=(jax.ShapeDtypeStruct((tokens, units), BF),) * 2,
        in_specs=[
            pl.BlockSpec((tokens, D), lambda n: (0, 0)),
            pl.BlockSpec((block, D), lambda n: (n, 0)),
            pl.BlockSpec((1, block), lambda n: (0, n)),
        ],
        out_specs=(column, column),
        compiler_params=pltpu.CompilerParams(vmem_limit_bytes=48 * MIB),
    )(acts, up_full, bias.reshape(1, -1))


SMALL_ROWS = 32
SMALL_WIDTH = 128


def pack_small(vector_part, bias_part):
    owners = vector_part.shape[0]
    flat = jnp.concatenate([vector_part.reshape(owners, -1), bias_part.reshape(owners, -1)], axis=1)
    room = SMALL_ROWS * SMALL_WIDTH
    flat = jnp.pad(flat, ((0, 0), (0, room - flat.shape[1])))
    return flat.reshape(owners * SMALL_ROWS, SMALL_WIDTH)


def unpack_small(packed, columns, units):
    owners = packed.shape[0] // SMALL_ROWS
    flat = packed.reshape(owners, -1)
    vector_part = flat[:, : 8 * columns].reshape(owners, 8, columns)
    bias_part = flat[:, 8 * columns : 8 * columns + units]
    return vector_part, bias_part


def shards(
    block_input,
    cotangent,
    w_qkv,
    w_out,
    w_up,
    w_down,
    vectors,
    b_up,
    qkv_left,
    qkv_right,
    out_left,
    out_right,
    up_left,
    up_right,
    down_left,
    down_right,
    qkv_left_root,
    qkv_right_root,
    out_left_root,
    out_right_root,
    up_left_root,
    up_right_root,
    down_left_root,
    down_right_root,
    vector_stat,
    b_up_stat,
):
    owners = lax.axis_size("dp") * lax.axis_size("ffn")
    me = lax.axis_index("dp") * lax.axis_size("ffn") + lax.axis_index("ffn")
    columns = vectors.shape[1]
    units = b_up.shape[0]
    small = pack_small(vectors[None], b_up[None]).astype(BF)
    small_full, qkv_full, out_full, up_full, down_full = gather_all(
        [
            small,
            w_qkv.T.astype(BF),
            w_out.T.astype(BF),
            w_up.T.astype(BF),
            w_down.astype(BF),
        ],
        1,
    )
    vector_low, bias_low = unpack_small(small_full, columns, units)
    vector_rows = vector_low.transpose(1, 0, 2).reshape(8, D).astype(F32)
    up_bias = bias_low.reshape(-1).astype(F32)
    inputs = block_input.astype(F32)
    normed_one, unit_one, inverse_one = layer_norm(inputs, vector_rows[0], vector_rows[1])
    acts_one = normed_one.astype(BF)
    qkv_bias = jnp.concatenate([vector_rows[2], jnp.zeros_like(vector_rows[2]), vector_rows[3]])
    projected = (dot_nt(acts_one, qkv_full) + qkv_bias).astype(BF)
    mixed_low, logsum = attend(projected)
    residual = inputs + dot_nt(mixed_low, out_full) + vector_rows[4]
    normed_two, unit_two, inverse_two = layer_norm(residual, vector_rows[5], vector_rows[6])
    acts_two = normed_two.astype(BF)
    cot_float = cotangent.astype(F32)
    hidden, slope = hidden_units(acts_two, up_full, up_bias)
    block_output = (residual + dot_nn(hidden, down_full) + vector_rows[7]).astype(BF)
    down_t = dot_tn(hidden, cotangent).astype(BF)
    slope_low = (dot_nt(cotangent, down_full) * slope.astype(F32)).astype(BF)
    up_t = dot_tn(slope_low, acts_two).astype(BF)
    bias_grad = jnp.sum(slope_low, axis=0, dtype=F32)
    back_two = dot_nn(slope_low, up_full)
    down_g, up_g = reduce_all([down_t, up_t], 2)
    norm_two_back, gain_two_grad, shift_two_grad = norm_backward(
        back_two, unit_two, inverse_two, vector_rows[5]
    )
    residual_grad = cot_float + norm_two_back
    branch_low = residual_grad.astype(BF)
    out_t = dot_tn(branch_low, mixed_low).astype(BF)
    out_bias_grad = jnp.sum(branch_low, axis=0, dtype=F32)
    mixed_grad = dot_nn(branch_low, out_full).astype(BF)
    projected_grad = attend_back(projected, mixed_grad, logsum)
    qkv_t = jnp.concatenate([dot_tn(projected_grad[i], acts_one) for i in range(3)], 0).astype(BF)
    projected_sums = jnp.sum(projected_grad, axis=1, dtype=F32)
    back_one = sum(dot_nn(projected_grad[i], qkv_full[i * D : (i + 1) * D]) for i in range(3))
    norm_one_back, gain_one_grad, shift_one_grad = norm_backward(
        back_one, unit_one, inverse_one, vector_rows[0]
    )
    input_grad = (residual_grad + norm_one_back).astype(BF)
    vector_part = jnp.stack(
        [
            gain_one_grad,
            shift_one_grad,
            projected_sums[0],
            projected_sums[2],
            out_bias_grad,
            gain_two_grad,
            shift_two_grad,
            jnp.sum(cot_float, axis=0),
        ]
    )
    small_part = pack_small(
        vector_part.reshape(8, owners, columns).transpose(1, 0, 2), bias_grad.reshape(owners, units)
    )
    qkv_g, out_g, small_g = reduce_all([qkv_t, out_t, small_part.astype(BF)], 3)
    vector_grad, b_up_grad = unpack_small(small_g, columns, units)
    vector_grad, b_up_grad = vector_grad[0], b_up_grad[0]
    grads = [qkv_g, out_g, up_g, down_g]
    lows = [item.astype(BF) for item in grads]
    m_roots = [qkv_left_root, out_left_root, up_left_root, down_right_root]
    gathered = gather_all(lows + [root.astype(BF) for root in m_roots], 4)
    grads_full, roots_full = gathered[:4], gathered[4:]
    n_roots = [qkv_right_root, out_right_root, up_right_root, down_left_root]
    m_stats = [qkv_left, out_left, up_left, down_right]
    n_stats = [qkv_right, out_right, up_right, down_left]
    rows_owned = m_stats[0].shape[0]
    new_m, new_n, steps = [], [], []
    for low, full, root, n_root, m_stat, n_stat in zip(
        lows, grads_full, roots_full, n_roots, m_stats, n_stats
    ):
        new_n.append(decay_rate * n_stat + (1.0 - decay_rate) * dot_nt(low, full))
        mine = lax.dynamic_slice_in_dim(full, me * rows_owned, rows_owned, 1)
        new_m.append(decay_rate * m_stat + (1.0 - decay_rate) * dot_tn(mine, full))
        product = dot_nn(n_root.astype(BF), full)
        steps.append(dot_nt(product.astype(BF), root))
    new_w_qkv = w_qkv - matrix_rate * steps[0].T
    new_w_out = w_out - matrix_rate * steps[1].T
    new_w_up = w_up - matrix_rate * steps[2].T
    new_w_down = w_down - matrix_rate * steps[3]
    new_vector_stat = decay_rate * vector_stat + (1.0 - decay_rate) * vector_grad * vector_grad
    new_vectors = vectors - vector_rate * vector_grad * lax.rsqrt(new_vector_stat)
    new_b_up_stat = decay_rate * b_up_stat + (1.0 - decay_rate) * b_up_grad * b_up_grad
    new_b_up = b_up - vector_rate * b_up_grad * lax.rsqrt(new_b_up_stat)
    return (
        block_output,
        input_grad,
        grads[0].T,
        grads[1].T,
        grads[2].T,
        grads[3],
        vector_grad,
        b_up_grad,
        new_m[0],
        new_n[0],
        new_m[1],
        new_n[1],
        new_m[2],
        new_n[2],
        new_n[3],
        new_m[3],
        new_vector_stat,
        new_b_up_stat,
        new_w_qkv,
        new_w_out,
        new_w_up,
        new_w_down,
        new_vectors,
        new_b_up,
    )


def solution(mesh):
    return jax.shard_map(
        shards,
        mesh=mesh,
        in_specs=(
            P(("dp", "ffn"), None),
            P(("dp", "ffn"), None),
            P(None, ("dp", "ffn")),
            P(None, ("dp", "ffn")),
            P(None, ("dp", "ffn")),
            P(("dp", "ffn"), None),
            P(None, ("dp", "ffn")),
            P(("dp", "ffn")),
            P(("dp", "ffn"), None),
            P(("dp", "ffn"), None),
            P(("dp", "ffn"), None),
            P(("dp", "ffn"), None),
            P(("dp", "ffn"), None),
            P(("dp", "ffn"), None),
            P(("dp", "ffn"), None),
            P(("dp", "ffn"), None),
            P(("dp", "ffn"), None),
            P(("dp", "ffn"), None),
            P(("dp", "ffn"), None),
            P(("dp", "ffn"), None),
            P(("dp", "ffn"), None),
            P(("dp", "ffn"), None),
            P(("dp", "ffn"), None),
            P(("dp", "ffn"), None),
            P(None, ("dp", "ffn")),
            P(("dp", "ffn")),
        ),
        out_specs=(
            P(("dp", "ffn"), None),
            P(("dp", "ffn"), None),
            P(None, ("dp", "ffn")),
            P(None, ("dp", "ffn")),
            P(None, ("dp", "ffn")),
            P(("dp", "ffn"), None),
            P(None, ("dp", "ffn")),
            P(("dp", "ffn")),
            P(("dp", "ffn"), None),
            P(("dp", "ffn"), None),
            P(("dp", "ffn"), None),
            P(("dp", "ffn"), None),
            P(("dp", "ffn"), None),
            P(("dp", "ffn"), None),
            P(("dp", "ffn"), None),
            P(("dp", "ffn"), None),
            P(None, ("dp", "ffn")),
            P(("dp", "ffn")),
            P(None, ("dp", "ffn")),
            P(None, ("dp", "ffn")),
            P(None, ("dp", "ffn")),
            P(("dp", "ffn"), None),
            P(None, ("dp", "ffn")),
            P(("dp", "ffn")),
        ),
        check_vma=False,
    )
```

```python
import functools

import jax
import jax.numpy as jnp
from jax import lax
from jax.experimental import pallas as pl
from jax.experimental.pallas import tpu as pltpu
from jax.sharding import PartitionSpec as P

D = 1024
HEADS = 8
HEAD_DIM = 128
MESH = pl.DeviceIdType.MESH
ALL = ("dp", "ffn")
BF = jnp.bfloat16
F32 = jnp.float32
MIB = 2**20

norm_epsilon = 1e-05
decay_rate = 0.5
matrix_rate = 0.5
vector_rate = 0.1
masked_score = -1e30


def layer_norm(values, gain, shift):
    center = values - jnp.mean(values, axis=-1, keepdims=True)
    inverse = lax.rsqrt(jnp.mean(center * center, axis=-1, keepdims=True) + norm_epsilon)
    normed = center * inverse
    return (normed * gain + shift, normed, inverse)


def norm_backward(grad, normed, inverse, gain):
    scaled = grad * gain
    inner = (
        scaled
        - jnp.mean(scaled, axis=-1, keepdims=True)
        - normed * jnp.mean(scaled * normed, axis=-1, keepdims=True)
    )
    return (inner * inverse, jnp.sum(grad * normed, axis=0), jnp.sum(grad, axis=0))


def dot_nt(left, right):
    return lax.dot_general(left, right, (((1,), (1,)), ((), ())), preferred_element_type=F32)


def dot_tn(left, right):
    return lax.dot_general(left, right, (((0,), (0,)), ((), ())), preferred_element_type=F32)


def dot_nn(left, right):
    return jnp.dot(left, right, preferred_element_type=F32)


def coords():
    dp = lax.axis_index("dp")
    return dp // 2, dp % 2, lax.axis_index("ffn")


def flip(value, mask):
    result = value
    bit = 1
    while bit <= mask:
        if mask & bit:
            result = result + bit - 2 * bit * ((result // bit) % 2)
        bit *= 2
    return result


def greet():
    p, c, z = coords()
    barrier = pltpu.get_barrier_semaphore()
    peers = [(flip(p, 1) * 2 + c, z), (flip(p, 2) * 2 + c, z), (p * 2 + 1 - c, z)]
    peers += [(p * 2 + c, flip(z, k)) for k in (1, 2, 3)]
    for peer in peers:
        pl.semaphore_signal(barrier, inc=1, device_id=peer, device_id_type=MESH)
    pl.semaphore_wait(barrier, len(peers))


FIRST = (1, 2)
SECOND = (2, 1)


class Copies:
    def __init__(self, send, recv):
        self.send, self.recv, self.made = send, recv, {}

    def copy(self, name):
        at, make = self.made[name]
        src, dst, device = make()
        return pltpu.make_async_remote_copy(
            src, dst, self.send.at[at], self.recv.at[at], device_id=device, device_id_type=MESH
        )

    def post(self, name, make):
        self.made[name] = (len(self.made), make)
        self.copy(name).start()

    def got(self, name):
        self.copy(name).wait_recv()

    def sent(self):
        for name in self.made:
            self.copy(name).wait_send()


def gather_plan(place, shard, out, send, recv, local_sem):
    p, c, z = place
    half_rows = shard.shape[0] // 2
    copies = Copies(send, recv)

    def local():
        return pltpu.make_async_copy(shard, out.at[p, c, z], local_sem)

    def half(ref, h):
        return ref.at[pl.ds(h * half_rows, half_rows)]

    def along_z(k):
        copies.post(("z", k), lambda: (shard, out.at[p, c, z], (p * 2 + c, flip(z, k))))

    def spread(k):
        for name, turn in (("first", FIRST), ("second", SECOND)):
            for h in (0, 1):

                def make(h=h, turn=turn):
                    dst = half(out.at[p, c, flip(z, k)], h)
                    return (dst if k else half(shard, h)), dst, (flip(p, turn[h]) * 2 + c, z)

                copies.post((name, k, h), make)

    def begin():
        along_z(1)
        spread(0)
        local().start()

    def landed(k):
        copies.got(("z", k))
        if k < 3:
            along_z(k + 1)
        spread(k)

    def forward(k):
        for h in (0, 1):
            copies.got(("first", k, h))

            def make(h=h):
                piece = half(out.at[flip(p, FIRST[h]), c, flip(z, k)], h)
                return piece, piece, (flip(p, SECOND[h]) * 2 + c, z)

            copies.post(("relay", k, h), make)

    def share(k):
        for h in (0, 1):
            copies.got(("second", k, h))
            copies.got(("relay", k, h))
        if k == 0:
            local().wait()

        def make():
            piece = out.at[:, c, flip(z, k)]
            return piece, piece, (p * 2 + 1 - c, z)

        copies.post(("core", k), make)

    def finish():
        for k in range(4):
            copies.got(("core", k))
        copies.sent()

    do = functools.partial
    plan = [begin, do(landed, 1), do(forward, 0), do(landed, 2), do(forward, 1), do(share, 0)]
    plan += [do(landed, 3), do(forward, 2), do(share, 1), do(forward, 3), do(share, 2)]
    return plan + [do(share, 3), finish]


def reduce_plan(
    place, parts, out, held, from_core, from_second, from_first, from_z, send, recv, load
):
    p, c, z = place
    half_rows = parts.shape[-2] // 2
    copies = Copies(send, recv)
    order = (3, 2, 1, 0)

    def half(h):
        return pl.ds(h * half_rows, half_rows)

    def local(k):
        return pltpu.make_async_copy(parts.at[:, c, flip(z, k)], held.at[k], load.at[k])

    def to_core(k):
        copies.post(
            ("core", k),
            lambda: (parts.at[:, 1 - c, flip(z, k)], from_core.at[k], (p * 2 + 1 - c, z)),
        )
        local(k).start()

    def add(dst, *sources):
        total = dst[...].astype(F32)
        for source in sources:
            total = total + source[...].astype(F32)
        dst[...] = total.astype(BF)

    def begin():
        to_core(order[0])

    def cores(k):
        local(k).wait()
        copies.got(("core", k))
        if k:
            to_core(order[order.index(k) + 1])
        for h in (0, 1):
            for j, mask in ((1, 3), (0, SECOND[h])):
                q = flip(p, mask)
                add(held.at[k, q, half(h)], from_core.at[k, q, half(h)])
                copies.post(
                    ("second", k, h, j),
                    lambda h=h, j=j, mask=mask: (
                        held.at[k, flip(p, mask), half(h)],
                        from_second.at[k, h, j],
                        (flip(p, SECOND[h]) * 2 + c, z),
                    ),
                )
        for h in (0, 1):
            for mask in (0, FIRST[h]):
                q = flip(p, mask)
                add(held.at[k, q, half(h)], from_core.at[k, q, half(h)])

    def second(k):
        for h in (0, 1):
            copies.got(("second", k, h, 1))
            add(held.at[k, flip(p, FIRST[h]), half(h)], from_second.at[k, h, 1])
            copies.post(
                ("first", k, h),
                lambda h=h: (
                    held.at[k, flip(p, FIRST[h]), half(h)],
                    from_first.at[k, h],
                    (flip(p, FIRST[h]) * 2 + c, z),
                ),
            )

    def first(k):
        for h in (0, 1):
            copies.got(("second", k, h, 0))
            copies.got(("first", k, h))
            add(held.at[k, p, half(h)], from_second.at[k, h, 0], from_first.at[k, h])
        if k:
            copies.post(
                ("z", k), lambda: (held.at[k, p], from_z.at[k - 1], (p * 2 + c, flip(z, k)))
            )

    def finish():
        for k in (3, 2, 1):
            copies.got(("z", k))
        total = held[0, p].astype(F32)
        for k in range(3):
            total = total + from_z[k].astype(F32)
        out[...] = total
        copies.sent()

    do = functools.partial
    plan = [begin, do(cores, 3), do(cores, 2), do(second, 3), do(cores, 1), do(second, 2)]
    plan += [do(first, 3), do(cores, 0), do(second, 1), do(first, 2), do(second, 0)]
    return plan + [do(first, 1), do(first, 0), finish]


def merge_plans(plans, offset):
    total = max(len(plan) + offset * g for g, plan in enumerate(plans))
    merged = []
    for t in range(total):
        for g, plan in enumerate(plans):
            at = t - offset * g
            if 0 <= at < len(plan):
                merged.append(plan[at])
    return merged


ANYWHERE = pl.BlockSpec(memory_space=pl.ANY)
COPIES = 31


class Gather:
    def __init__(self, shard):
        self.array = shard
        self.rows, self.width = shard.shape
        self.shape = jax.ShapeDtypeStruct((4, 2, 4, self.rows, self.width), BF)
        self.spec = ANYWHERE
        sems = pltpu.SemaphoreType.DMA((COPIES,))
        self.scratch = [sems, sems, pltpu.SemaphoreType.DMA]
        self.plan = gather_plan

    def finish(self, out):
        return out.reshape(-1, self.width)

    def plainly(self):
        return lax.all_gather(self.array, ALL, axis=0, tiled=True)


class Reduce:
    def __init__(self, parts):
        devices = lax.axis_size("dp") * lax.axis_size("ffn")
        self.parts = parts
        self.rows, width = parts.shape[0] // devices, parts.shape[1]
        self.shape = jax.ShapeDtypeStruct((self.rows, width), F32)
        self.spec = pl.BlockSpec((self.rows, width), lambda *_: (0, 0))
        sems = pltpu.SemaphoreType.DMA((COPIES,))
        rows = self.rows
        self.scratch = [
            pltpu.VMEM((4, 4, rows, width), BF),
            pltpu.VMEM((4, 4, rows, width), BF),
            pltpu.VMEM((4, 2, 2, rows // 2, width), BF),
            pltpu.VMEM((4, 2, rows // 2, width), BF),
            pltpu.VMEM((3, rows, width), BF),
            sems,
            sems,
            pltpu.SemaphoreType.DMA((4,)),
        ]
        self.plan = reduce_plan

    @property
    def array(self):
        return self.parts.reshape(4, 2, 4, self.rows, self.parts.shape[1])

    def finish(self, out):
        return out

    def plainly(self):
        return lax.psum_scatter(self.parts, ALL, scatter_dimension=0, tiled=True).astype(F32)


def on_fast_grid():
    return lax.axis_size("dp") == 8 and lax.axis_size("ffn") == 4


def fused_call(body, steps, ins, outs, scratch, jobs, collective_id, spread=None):
    plainly = not (on_fast_grid() and all(job.rows % 32 == 0 for job in jobs))
    run = [] if plainly else jobs
    counts = [len(ins), len(run), len(outs), len(run), len(scratch)]

    def kernel(*refs):
        groups = []
        at = 0
        for count in counts:
            groups.append(refs[at : at + count])
            at += count
        own_in, job_in, own_out, job_out, own_scratch = groups
        t = pl.program_id(0)
        if run:
            place = coords()
            plans = []
            for job, src, dst in zip(run, job_in, job_out):
                plans.append(job.plan(place, src, dst, *refs[at : at + len(job.scratch)]))
                at += len(job.scratch)
            merged = merge_plans(plans, 7)
            stops = spread or steps
            for step in range(steps):
                now = [m for i, m in enumerate(merged[:-1]) if i * stops // len(merged) == step]
                if step == 0:
                    now = [greet] + now
                if now:

                    @pl.when(t == step)
                    def _(now=now):
                        for each in now:
                            each()

        if body is not None:
            body(t, *own_in, *own_out, *own_scratch)
        if run:

            @pl.when(t == steps - 1)
            def _():
                merged[-1]()

    all_scratch = list(scratch)
    for job in run:
        all_scratch += job.scratch
    extra = dict(collective_id=collective_id, has_side_effects=True) if run else {}
    results = pl.pallas_call(
        kernel,
        grid=(steps,),
        out_shape=tuple(o[0] for o in outs) + tuple(job.shape for job in run),
        in_specs=[i[1] for i in ins] + [ANYWHERE] * len(run),
        out_specs=tuple(o[1] for o in outs) + tuple(job.spec for job in run),
        scratch_shapes=all_scratch,
        compiler_params=pltpu.CompilerParams(vmem_limit_bytes=60 * MIB, **extra),
    )(*[i[0] for i in ins], *[job.array for job in run])
    own = list(results[: len(outs)])
    if plainly:
        return own, [job.plainly() for job in jobs]
    return own, [job.finish(out) for job, out in zip(jobs, results[len(outs) :])]


def transfer(jobs, collective_id):
    if not (on_fast_grid() and all(job.rows % 32 == 0 for job in jobs)):
        return [job.plainly() for job in jobs]
    return fused_call(None, 1, [], [], [], jobs, collective_id)[1]


def whole(array):
    rank = len(array.shape)
    spec = pl.BlockSpec(array.shape, lambda t: (0,) * rank, pipeline_mode=pl.Buffered(1))
    return array, spec


def block(array, shape, at):
    return array, pl.BlockSpec(shape, at)


def result(shape, dtype, tile=None, at=None):
    rank = len(shape)
    if tile is None:
        return jax.ShapeDtypeStruct(shape, dtype), pl.BlockSpec(shape, lambda t: (0,) * rank)
    return jax.ShapeDtypeStruct(shape, dtype), pl.BlockSpec(tile, at)


def chunks(rows, size, body):
    @pl.loop(0, rows // size)
    def _(i):
        body(pl.ds(pl.multiple_of(i * size, size), size))


QUERY_BLOCK = 256
CHUNK = 128
UNITS = 512


def head_slope(head):
    level = head.astype(F32) + 1.0
    return jnp.exp2(jnp.full((1, 1), -8.0 / HEADS, F32) * level)


def scores_t(query, keys, slope, start, rows):
    at_key = lax.broadcasted_iota(jnp.int32, (rows, 1), 0).astype(F32)
    scores = dot_nt(keys, query) * HEAD_DIM ** (-0.5) + at_key * slope
    at_key = lax.broadcasted_iota(jnp.int32, (rows, QUERY_BLOCK), 0)
    at_query = lax.broadcasted_iota(jnp.int32, (rows, QUERY_BLOCK), 1) + start
    return jnp.where(at_key <= at_query, scores, masked_score)


def attend_body(t, x, vec, wq, wk, wv, head_vec, qkv, mixed, lse, acts):
    length = x.shape[0]

    @pl.when(t == 0)
    def _():
        def norm(rows):
            normed = layer_norm(x[rows, :].astype(F32), vec[0:1, :], vec[1:2, :])[0]
            acts[rows, :] = normed.astype(BF)

        chunks(length, CHUNK, norm)

    weights = jnp.concatenate([wq[...], wk[...], wv[...]], axis=0)
    projected = dot_nt(acts[...], weights)
    qkv[0] = (projected[:, :HEAD_DIM] + head_vec[2:3, :]).astype(BF)
    qkv[1] = projected[:, HEAD_DIM : 2 * HEAD_DIM].astype(BF)
    values = projected[:, 2 * HEAD_DIM :] + head_vec[3:4, :]
    qkv[2] = values.astype(BF)
    values_t = values.T.astype(BF)
    slope = head_slope(t)
    for start in range(0, length, QUERY_BLOCK):
        rows = start + QUERY_BLOCK
        scores = scores_t(qkv[0, start:rows, :], qkv[1, :rows, :], slope, start, rows)
        highest = jnp.max(scores, axis=0, keepdims=True)
        weights = jnp.exp(scores - highest)
        totals = jnp.sum(weights, axis=0, keepdims=True)
        mix = dot_nn(values_t[:, :rows], weights.astype(BF)) / totals
        mixed[start:rows, :] = mix.T.astype(BF)
        lse[0, :, start:rows] = highest + jnp.log(totals)


def attend(x, vec, qkv_full, jobs, collective_id):
    tokens = x.shape[0]
    head_rows = lambda part: block(
        qkv_full, (HEAD_DIM, D), lambda h: (part * HEADS + h, 0)
    )
    return fused_call(
        attend_body,
        HEADS,
        [
            whole(x),
            whole(vec),
            head_rows(0),
            head_rows(1),
            head_rows(2),
            block(vec, (8, HEAD_DIM), lambda h: (0, h)),
        ],
        [
            result((3, tokens, D), BF, (3, tokens, HEAD_DIM), lambda h: (0, 0, h)),
            result((tokens, D), BF, (tokens, HEAD_DIM), lambda h: (0, h)),
            result((HEADS, 1, tokens), F32, (1, 1, tokens), lambda h: (h, 0, 0)),
            result((tokens, D), BF),
        ],
        [],
        jobs,
        collective_id,
    )


def gelu_pair(pre):
    half = 0.5 * (1.0 + lax.erf(pre * 0.7071067811865476))
    slope = half + pre * jnp.exp(-0.5 * pre * pre) * 0.3989422804014327
    return pre * half, slope


def hidden_body(t, x, mixed, out_w, vec, dy, up, bias, residual, acts, hidden, slope, down_t):
    tokens = x.shape[0]

    @pl.when(t == 0)
    def _():
        def enter(rows):
            attended = dot_nt(mixed[rows, :], out_w[...]) + vec[4:5, :]
            here = x[rows, :].astype(F32) + attended
            residual[rows, :] = here
            acts[rows, :] = layer_norm(here, vec[5:6, :], vec[6:7, :])[0].astype(BF)

        chunks(tokens, 2 * CHUNK, enter)

    for start in range(0, tokens, 256):
        rows = slice(start, start + 256)
        pre = dot_nt(acts[rows, :], up[...]) + bias[...]
        value, steep = gelu_pair(pre)
        hidden[rows, :] = value.astype(BF)
        slope[rows, :] = steep.astype(BF)
    down_t[...] = dot_tn(hidden[...], dy[...]).astype(BF)


def hidden_forward(x, mixed, out_full, vec, dy, up_full, bias, jobs, collective_id):
    tokens = x.shape[0]
    units = up_full.shape[0]
    return fused_call(
        hidden_body,
        units // UNITS,
        [
            whole(x),
            whole(mixed),
            whole(out_full),
            whole(vec),
            whole(dy),
            block(up_full, (UNITS, D), lambda n: (n, 0)),
            block(bias, (1, UNITS), lambda n: (0, n)),
        ],
        [
            result((tokens, D), F32),
            result((tokens, D), BF),
            result((tokens, units), BF, (tokens, UNITS), lambda n: (0, n)),
            result((tokens, units), BF, (tokens, UNITS), lambda n: (0, n)),
            result((units, D), BF, (UNITS, D), lambda n: (n, 0)),
        ],
        [],
        jobs,
        collective_id,
    )


def hidden_back_body(
    t, dy, acts, residual, hidden, slope, down, up, vec, out, up_t, bias_sum, dh, dh_low, sums, total, back, du
):
    tokens = dy.shape[0]
    last = pl.num_programs(0) - 1

    def accumulate(into, value):
        @pl.when(t == 0)
        def _():
            into[...] = value

        @pl.when(t > 0)
        def _():
            into[...] += value

    accumulate(total, dot_nn(hidden[...], down[...]))
    du[...] = (dot_nt(dy[...], down[...]) * slope[...].astype(F32)).astype(BF)
    bias_sum[...] = jnp.sum(du[...].astype(F32), axis=0, keepdims=True)
    up_t[...] = dot_tn(du[...], acts[...]).astype(BF)
    accumulate(back, dot_nn(du[...], up[...]))

    @pl.when(t == last)
    def _():
        sums[...] = jnp.zeros_like(sums)

        def leave(rows):
            here = residual[rows, :]
            out[rows, :] = (here + total[rows, :] + vec[7:8, :]).astype(BF)
            grad = back[rows, :]
            normed, inverse = layer_norm(here, 1.0, 0.0)[1:]
            change, gain, shift = norm_backward(grad, normed, inverse, vec[5:6, :])
            upstream = dy[rows, :].astype(F32)
            here = upstream + change
            dh[rows, :] = here
            low = here.astype(BF)
            dh_low[rows, :] = low
            for row, value in enumerate((jnp.sum(low.astype(F32), axis=0), gain, shift, jnp.sum(upstream, axis=0))):
                sums[4 + row : 5 + row, :] += value[None]

        chunks(tokens, CHUNK, leave)


def hidden_backward(
    dy, acts, residual, hidden, slope, down_full, up_full, vec, jobs, collective_id
):
    tokens = dy.shape[0]
    units = up_full.shape[0]
    column = lambda array: block(array, (tokens, UNITS), lambda n: (0, n))
    rows = lambda array: block(array, (UNITS, D), lambda n: (n, 0))
    return fused_call(
        hidden_back_body,
        units // UNITS,
        [
            whole(dy),
            whole(acts),
            whole(residual),
            column(hidden),
            column(slope),
            rows(down_full),
            rows(up_full),
            whole(vec),
        ],
        [
            result((tokens, D), BF),
            result((units, D), BF, (UNITS, D), lambda n: (n, 0)),
            result((1, units), F32, (1, UNITS), lambda n: (0, n)),
            result((tokens, D), F32),
            result((tokens, D), BF),
            result((8, D), F32),
        ],
        [
            pltpu.VMEM((tokens, D), F32),
            pltpu.VMEM((tokens, D), F32),
            pltpu.VMEM((tokens, UNITS), BF),
        ],
        jobs,
        collective_id,
    )


def attend_back_body(
    t, dh_low, out_w, mixed, x, dh, vec, acts, qkv, lse, wq, wk, wv, sums_in,
    out_t, qkv_t, grad_in, sums, upstream, grads, dk, dv, back,
):
    length = x.shape[0]
    last = pl.num_programs(0) - 1
    scale = HEAD_DIM ** (-0.5)

    @pl.when(t == 0)
    def _():
        def enter(rows):
            value = dot_nn(dh_low[rows, :], out_w[...]).astype(BF)
            for head in range(HEADS):
                upstream[head, rows, :] = value[:, head * HEAD_DIM : (head + 1) * HEAD_DIM]

        chunks(length, 2 * CHUNK, enter)
        out_t[...] = dot_tn(dh_low[...], mixed[...]).astype(BF)
        sums[...] = sums_in[...]

    slope = head_slope(t)
    keys_t = qkv[1].astype(F32).T.astype(BF)
    for start in reversed(range(0, length, QUERY_BLOCK)):
        rows = start + QUERY_BLOCK
        query = qkv[0, start:rows, :]
        above = upstream[t, start:rows, :]
        scores = scores_t(query, qkv[1, :rows, :], slope, start, rows)
        probs = jnp.exp(scores - lse[0, :, start:rows])
        prob_grad = dot_nt(qkv[2, :rows, :], above)
        weighted = probs * prob_grad
        centered = jnp.sum(weighted, axis=0, keepdims=True)
        score_grad = (weighted - probs * centered).astype(BF)
        query_grad = dot_nn(keys_t[:, :rows], score_grad) * scale
        grads[start:rows, :HEAD_DIM] = query_grad.T.astype(BF)
        key_part = dot_nn(score_grad, query)
        value_part = dot_nn(probs.astype(BF), above)
        if rows == length:
            dk[...] = key_part
            dv[...] = value_part
        else:
            dk[:rows, :] += key_part
            dv[:rows, :] += value_part
    grads[:, HEAD_DIM : 2 * HEAD_DIM] = (dk[...] * scale).astype(BF)
    grads[:, 2 * HEAD_DIM :] = dv[...].astype(BF)
    totals = jnp.sum(grads[...].astype(F32), axis=0, keepdims=True)
    lanes = pl.ds(pl.multiple_of(t * HEAD_DIM, HEAD_DIM), HEAD_DIM)
    sums[2:3, lanes] = totals[:, :HEAD_DIM]
    sums[3:4, lanes] = totals[:, 2 * HEAD_DIM :]
    weight_grad = dot_tn(grads[...], acts[...]).astype(BF)
    for part in range(3):
        qkv_t[part] = weight_grad[part * HEAD_DIM : (part + 1) * HEAD_DIM, :]
    weights = jnp.concatenate([wq[...], wk[...], wv[...]], axis=0)
    more = dot_nn(grads[...], weights)

    @pl.when(t == 0)
    def _():
        back[...] = more

    @pl.when(t > 0)
    def _():
        back[...] += more

    @pl.when(t == last)
    def _():
        def leave(rows):
            normed, inverse = layer_norm(x[rows, :].astype(F32), 1.0, 0.0)[1:]
            change, gain, shift = norm_backward(back[rows, :], normed, inverse, vec[0:1, :])
            grad_in[rows, :] = (dh[rows, :] + change).astype(BF)
            sums[0:1, :] += gain[None]
            sums[1:2, :] += shift[None]

        chunks(length, CHUNK, leave)


def attend_backward(
    dh_low, out_full, mixed, x, dh, vec, acts, qkv, lse, qkv_full, sums, jobs, collective_id
):
    tokens = x.shape[0]
    head_rows = lambda part: block(
        qkv_full, (HEAD_DIM, D), lambda h: (part * HEADS + h, 0)
    )
    return fused_call(
        attend_back_body,
        HEADS,
        [
            whole(dh_low),
            whole(out_full),
            whole(mixed),
            whole(x),
            whole(dh),
            whole(vec),
            whole(acts),
            block(qkv, (3, tokens, HEAD_DIM), lambda h: (0, 0, h)),
            block(lse, (1, 1, tokens), lambda h: (h, 0, 0)),
            head_rows(0),
            head_rows(1),
            head_rows(2),
            whole(sums),
        ],
        [
            result((D, D), BF),
            result((3, D, D), BF, (3, HEAD_DIM, D), lambda h: (0, h, 0)),
            result((tokens, D), BF),
            result((8, D), F32),
        ],
        [
            pltpu.VMEM((HEADS, tokens, HEAD_DIM), BF),
            pltpu.VMEM((tokens, 3 * HEAD_DIM), BF),
            pltpu.VMEM((tokens, HEAD_DIM), F32),
            pltpu.VMEM((tokens, HEAD_DIM), F32),
            pltpu.VMEM((tokens, D), F32),
        ],
        jobs,
        collective_id,
    )


def renew_body(
    t, own, full, root, n_stat, m_stat, m_root, weight, new_n, new_m, new_w, left, product
):
    last = pl.num_programs(0) - 1
    me = lax.axis_index("dp") * lax.axis_size("ffn") + lax.axis_index("ffn")
    rows_owned = m_stat.shape[0]
    share = 128 // rows_owned
    lanes = pl.ds(pl.multiple_of((me // share) * 128, 128), 128)
    here = full[...]
    new_n[...] = decay_rate * n_stat[...] + (1.0 - decay_rate) * dot_nt(own[...], here)
    left_part = dot_tn(full[:, lanes], here)
    product_part = dot_nn(root[...].astype(BF), here)

    @pl.when(t == 0)
    def _():
        left[...] = left_part
        product[...] = product_part

    @pl.when(t > 0)
    def _():
        left[...] += left_part
        product[...] += product_part

    @pl.when(t == last)
    def _():
        mine = left[pl.ds(pl.multiple_of((me % share) * rows_owned, rows_owned), rows_owned), :]
        new_m[...] = decay_rate * m_stat[...] + (1.0 - decay_rate) * mine
        step = dot_nt(product[...].astype(BF), m_root[...])
        new_w[...] = weight[...] - matrix_rate * step


def renew(own, full, n_root, n_stat, m_stat, m_root, weight, jobs, collective_id):
    rows, total = own.shape[0], full.shape[0]
    rows_owned = m_stat.shape[0]
    if not on_fast_grid():
        me = lax.axis_index("dp") * lax.axis_size("ffn") + lax.axis_index("ffn")
        new_n = decay_rate * n_stat + (1.0 - decay_rate) * dot_nt(own, full)
        mine = lax.dynamic_slice_in_dim(full, me * rows_owned, rows_owned, 1)
        new_m = decay_rate * m_stat + (1.0 - decay_rate) * dot_tn(mine, full)
        product = dot_nn(n_root.astype(BF), full)
        new_w = weight - matrix_rate * dot_nt(product.astype(BF), m_root)
        return [new_n, new_m, new_w], [job.plainly() for job in jobs]
    size = 512
    column = lambda array: block(array, (rows, size), lambda n: (0, n))
    return fused_call(
        renew_body,
        total // size,
        [
            whole(own),
            block(full, (size, D), lambda n: (n, 0)),
            column(n_root),
            column(n_stat),
            whole(m_stat),
            whole(m_root),
            whole(weight),
        ],
        [
            result((rows, total), F32, (rows, size), lambda n: (0, n)),
            result((rows_owned, D), F32),
            result((rows, D), F32),
        ],
        [pltpu.VMEM((128, D), F32), pltpu.VMEM((rows, D), F32)],
        jobs,
        collective_id,
    )


SMALL_ROWS = 32
SMALL_WIDTH = 128


def pack_small(vector_part, bias_part):
    owners = vector_part.shape[0]
    flat = jnp.concatenate([vector_part.reshape(owners, -1), bias_part.reshape(owners, -1)], axis=1)
    room = SMALL_ROWS * SMALL_WIDTH
    flat = jnp.pad(flat, ((0, 0), (0, room - flat.shape[1])))
    return flat.reshape(owners * SMALL_ROWS, SMALL_WIDTH)


def unpack_small(packed, columns, units):
    owners = packed.shape[0] // SMALL_ROWS
    flat = packed.reshape(owners, -1)
    vector_part = flat[:, : 8 * columns].reshape(owners, 8, columns)
    bias_part = flat[:, 8 * columns : 8 * columns + units]
    return vector_part, bias_part


def shards(
    block_input,
    cotangent,
    w_qkv,
    w_out,
    w_up,
    w_down,
    vectors,
    b_up,
    qkv_left,
    qkv_right,
    out_left,
    out_right,
    up_left,
    up_right,
    down_left,
    down_right,
    qkv_left_root,
    qkv_right_root,
    out_left_root,
    out_right_root,
    up_left_root,
    up_right_root,
    down_left_root,
    down_right_root,
    vector_stat,
    b_up_stat,
):
    owners = lax.axis_size("dp") * lax.axis_size("ffn")
    columns = vectors.shape[1]
    units = b_up.shape[0]
    qkv_w, out_w, up_w = w_qkv.T, w_out.T, w_up.T
    small = pack_small(vectors[None], b_up[None]).astype(BF)
    small_full, qkv_full = transfer([Gather(small), Gather(qkv_w.astype(BF))], 1)
    vector_low, bias_low = unpack_small(small_full, columns, units)
    vector_rows = vector_low.transpose(1, 0, 2).reshape(8, D).astype(F32)
    up_bias = bias_low.reshape(1, -1).astype(F32)
    (qkv, mixed, lse, acts_one), (out_full, up_full) = attend(
        block_input, vector_rows, qkv_full, [Gather(out_w.astype(BF)), Gather(up_w.astype(BF))], 2
    )
    (residual, acts_two, hidden, slope, down_t), (down_full,) = hidden_forward(
        block_input,
        mixed,
        out_full,
        vector_rows,
        cotangent,
        up_full,
        up_bias,
        [Gather(w_down.astype(BF))],
        3,
    )
    (block_output, up_t, bias_grad, dh, dh_low, sums), (down_g, qkv_mroot) = hidden_backward(
        cotangent,
        acts_two,
        residual,
        hidden,
        slope,
        down_full,
        up_full,
        vector_rows,
        [Reduce(down_t), Gather(qkv_left_root.astype(BF))],
        4,
    )
    (out_t, qkv_t, input_grad, sums), (up_g, out_mroot, up_mroot) = attend_backward(
        dh_low,
        out_full,
        mixed,
        block_input,
        dh,
        vector_rows,
        acts_one,
        qkv,
        lse,
        qkv_full,
        sums,
        [Reduce(up_t), Gather(out_left_root.astype(BF)), Gather(up_left_root.astype(BF))],
        5,
    )
    small_part = pack_small(
        sums.reshape(8, owners, columns).transpose(1, 0, 2), bias_grad.reshape(owners, units)
    ).astype(BF)
    down_low = down_g.astype(BF)
    up_low = up_g.astype(BF)
    qkv_g, out_g, small_g, down_all, down_mroot = transfer(
        [
            Reduce(qkv_t.reshape(-1, D)),
            Reduce(out_t),
            Reduce(small_part),
            Gather(down_low),
            Gather(down_right_root.astype(BF)),
        ],
        6,
    )
    qkv_low, out_low = qkv_g.astype(BF), out_g.astype(BF)
    (new_down_n, new_down_m, new_w_down), (up_all,) = renew(
        down_low,
        down_all,
        down_left_root,
        down_left,
        down_right,
        down_mroot,
        w_down,
        [Gather(up_low)],
        7,
    )
    (new_up_n, new_up_m, new_w_up), (qkv_all, out_all) = renew(
        up_low,
        up_all,
        up_right_root,
        up_right,
        up_left,
        up_mroot,
        up_w,
        [Gather(qkv_low), Gather(out_low)],
        8,
    )
    new_qkv_n, new_qkv_m, new_w_qkv = renew(
        qkv_low, qkv_all, qkv_right_root, qkv_right, qkv_left, qkv_mroot, qkv_w, [], 9
    )[0]
    new_out_n, new_out_m, new_w_out = renew(
        out_low, out_all, out_right_root, out_right, out_left, out_mroot, out_w, [], 9
    )[0]
    new_m = [new_qkv_m, new_out_m, new_up_m, new_down_m]
    new_n = [new_qkv_n, new_out_n, new_up_n, new_down_n]
    new_w_qkv, new_w_out, new_w_up = new_w_qkv.T, new_w_out.T, new_w_up.T
    grads = [qkv_g, out_g, up_g, down_g]
    vector_grad, b_up_grad = unpack_small(small_g, columns, units)
    vector_grad, b_up_grad = vector_grad[0], b_up_grad[0]
    new_vector_stat = decay_rate * vector_stat + (1.0 - decay_rate) * vector_grad * vector_grad
    new_vectors = vectors - vector_rate * vector_grad * lax.rsqrt(new_vector_stat)
    new_b_up_stat = decay_rate * b_up_stat + (1.0 - decay_rate) * b_up_grad * b_up_grad
    new_b_up = b_up - vector_rate * b_up_grad * lax.rsqrt(new_b_up_stat)
    return (
        block_output,
        input_grad,
        grads[0].T,
        grads[1].T,
        grads[2].T,
        grads[3],
        vector_grad,
        b_up_grad,
        new_m[0],
        new_n[0],
        new_m[1],
        new_n[1],
        new_m[2],
        new_n[2],
        new_n[3],
        new_m[3],
        new_vector_stat,
        new_b_up_stat,
        new_w_qkv,
        new_w_out,
        new_w_up,
        new_w_down,
        new_vectors,
        new_b_up,
    )


def solution(mesh):
    return jax.shard_map(
        shards,
        mesh=mesh,
        in_specs=(
            P(("dp", "ffn"), None),
            P(("dp", "ffn"), None),
            P(None, ("dp", "ffn")),
            P(None, ("dp", "ffn")),
            P(None, ("dp", "ffn")),
            P(("dp", "ffn"), None),
            P(None, ("dp", "ffn")),
            P(("dp", "ffn")),
            P(("dp", "ffn"), None),
            P(("dp", "ffn"), None),
            P(("dp", "ffn"), None),
            P(("dp", "ffn"), None),
            P(("dp", "ffn"), None),
            P(("dp", "ffn"), None),
            P(("dp", "ffn"), None),
            P(("dp", "ffn"), None),
            P(("dp", "ffn"), None),
            P(("dp", "ffn"), None),
            P(("dp", "ffn"), None),
            P(("dp", "ffn"), None),
            P(("dp", "ffn"), None),
            P(("dp", "ffn"), None),
            P(("dp", "ffn"), None),
            P(("dp", "ffn"), None),
            P(None, ("dp", "ffn")),
            P(("dp", "ffn")),
        ),
        out_specs=(
            P(("dp", "ffn"), None),
            P(("dp", "ffn"), None),
            P(None, ("dp", "ffn")),
            P(None, ("dp", "ffn")),
            P(None, ("dp", "ffn")),
            P(("dp", "ffn"), None),
            P(None, ("dp", "ffn")),
            P(("dp", "ffn")),
            P(("dp", "ffn"), None),
            P(("dp", "ffn"), None),
            P(("dp", "ffn"), None),
            P(("dp", "ffn"), None),
            P(("dp", "ffn"), None),
            P(("dp", "ffn"), None),
            P(("dp", "ffn"), None),
            P(("dp", "ffn"), None),
            P(None, ("dp", "ffn")),
            P(("dp", "ffn")),
            P(None, ("dp", "ffn")),
            P(None, ("dp", "ffn")),
            P(None, ("dp", "ffn")),
            P(("dp", "ffn"), None),
            P(None, ("dp", "ffn")),
            P(("dp", "ffn")),
        ),
        check_vma=False,
    )
```

```python
import functools

import jax
import jax.numpy as jnp
from jax import lax
from jax.experimental import pallas as pl
from jax.experimental.pallas import tpu as pltpu
from jax.sharding import PartitionSpec as P

D = 1024
HEADS = 8
HEAD_DIM = 128
MESH = pl.DeviceIdType.MESH
ALL = ("dp", "ffn")
BF = jnp.bfloat16
F32 = jnp.float32
MIB = 2**20

norm_epsilon = 1e-05
decay_rate = 0.5
matrix_rate = 0.5
vector_rate = 0.1
masked_score = -1e30


def layer_norm(values, gain, shift):
    center = values - jnp.mean(values, axis=-1, keepdims=True)
    inverse = lax.rsqrt(jnp.mean(center * center, axis=-1, keepdims=True) + norm_epsilon)
    normed = center * inverse
    return (normed * gain + shift, normed, inverse)


def norm_backward(grad, normed, inverse, gain):
    scaled = grad * gain
    inner = (
        scaled
        - jnp.mean(scaled, axis=-1, keepdims=True)
        - normed * jnp.mean(scaled * normed, axis=-1, keepdims=True)
    )
    return (inner * inverse, jnp.sum(grad * normed, axis=0), jnp.sum(grad, axis=0))


def dot_nt(left, right):
    return lax.dot_general(left, right, (((1,), (1,)), ((), ())), preferred_element_type=F32)


def dot_tn(left, right):
    return lax.dot_general(left, right, (((0,), (0,)), ((), ())), preferred_element_type=F32)


def dot_nn(left, right):
    return jnp.dot(left, right, preferred_element_type=F32)


def flip(value, mask):
    result = value
    bit = 1
    while bit <= mask:
        if mask & bit:
            result = result + bit - 2 * bit * ((result // bit) % 2)
        bit *= 2
    return result


class Copies:
    def __init__(self, send, recv):
        self.send, self.recv, self.made = send, recv, {}

    def copy(self, name):
        at, make = self.made[name]
        src, dst, device = make()
        return pltpu.make_async_remote_copy(
            src, dst, self.send.at[at], self.recv.at[at], device_id=device, device_id_type=MESH
        )

    def plan(self, name, make):
        self.made[name] = (len(self.made), make)

    def post(self, name):
        self.copy(name).start()

    def got(self, name):
        self.copy(name).wait_recv()

    def sent(self):
        for name in self.made:
            self.copy(name).wait_send()


class Place:
    def __init__(self):
        dp = lax.axis_index("dp")
        self.y, self.x, self.c, self.z = dp // 4, (dp // 2) % 2, dp % 2, lax.axis_index("ffn")

    def device(self, y=0, x=0, c=0, z=0):
        dp = (flip(self.y, y) * 2 + flip(self.x, x)) * 2 + flip(self.c, c)
        return dp, flip(self.z, z)

    def span(self, group):
        if len(group) == 1:
            return pl.ds(flip(self.z, group[0]), 1)
        if len(group) == 2:
            return pl.ds(flip(self.z // 2, group[0] // 2) * 2, 2)
        return pl.ds(0, 4)


def greet(place):
    barrier = pltpu.get_barrier_semaphore()
    steps = [dict(y=1), dict(x=1), dict(c=1), dict(z=1), dict(z=2), dict(z=3)]
    for step in steps:
        pl.semaphore_signal(
            barrier, inc=1, device_id=place.device(**step), device_id_type=MESH
        )
    pl.semaphore_wait(barrier, len(steps))


def one(index):
    return pl.ds(index, 1)


TURNS = (("x", "y"), ("y", "x"))


def gather_plan(place, shard, out, send, recv, local_sem):
    y, x, c, z = place.y, place.x, place.c, place.z
    half_rows = shard.shape[0] // 2
    copies = Copies(send, recv)

    def half(ref, h):
        return ref.at[pl.ds(h * half_rows, half_rows)]

    def local():
        return pltpu.make_async_copy(shard, out.at[y, x, c, z], local_sem)

    def along_z(k):
        return shard, out.at[y, x, c, z], place.device(z=k)

    def own(turn, k, h):
        dst = half(out.at[y, x, c, flip(z, k)], h)
        return (dst if k else half(shard, h)), dst, place.device(**{TURNS[h][turn]: 1})

    def relay(k, h):
        block = out.at[y, 1 - x, c, flip(z, k)] if h == 0 else out.at[1 - y, x, c, flip(z, k)]
        return half(block, h), half(block, h), place.device(**{TURNS[h][1]: 1})

    def across(k):
        piece = out.at[:, :, c, flip(z, k)]
        return piece, piece, place.device(c=1)

    do = functools.partial
    for k in range(4):
        if k:
            copies.plan(("z", k), do(along_z, k))
        for h in (0, 1):
            copies.plan(("first", k, h), do(own, 0, k, h))
            copies.plan(("second", k, h), do(own, 1, k, h))
            copies.plan(("relay", k, h), do(relay, k, h))
        copies.plan(("core", k), do(across, k))

    def spread(k):
        for name in ("first", "second"):
            for h in (0, 1):
                copies.post((name, k, h))

    def begin():
        copies.post(("z", 1))
        spread(0)
        local().start()

    def landed(k):
        copies.got(("z", k))
        if k < 3:
            copies.post(("z", k + 1))
        spread(k)

    def forward(k):
        for h in (0, 1):
            copies.got(("first", k, h))
            copies.post(("relay", k, h))

    def share(k):
        for h in (0, 1):
            copies.got(("second", k, h))
            copies.got(("relay", k, h))
        if k == 0:
            local().wait()
        copies.post(("core", k))

    def finish():
        for k in range(4):
            copies.got(("core", k))
        copies.sent()

    return [
        (0, 0, begin),
        (4, 1, do(forward, 0)),
        (6, 1, do(landed, 1)),
        (13, 2, do(share, 0)),
        (14, 2, do(forward, 1)),
        (18, 2, do(landed, 2)),
        (20, 3, do(share, 1)),
        (24, 3, do(forward, 2)),
        (30, 2, do(landed, 3)),
        (31, 3, do(share, 2)),
        (35, 3, do(forward, 3)),
        (39, 3, do(share, 3)),
        (40, 4, finish),
    ]


def gather_small_plan(place, shard, out, send, recv, local_sem):
    y, x, c, z = place.y, place.x, place.c, place.z
    rows = shard.shape[0]
    copies = Copies(send, recv)

    def half(h):
        return pl.ds(h * (rows // 2), rows // 2)

    def local():
        return pltpu.make_async_copy(shard, out.at[y, x, c, z], local_sem)

    def along_z(k):
        return shard, out.at[y, x, c, z], place.device(z=k)

    def first(h):
        piece = out.at[y, x, c, :, half(h)]
        return piece, piece, place.device(**{TURNS[h][0]: 1})

    def second(h):
        piece = out.at[y, :, c, :, half(h)] if h == 0 else out.at[:, x, c, :, half(h)]
        return piece, piece, place.device(**{TURNS[h][1]: 1})

    def across():
        piece = out.at[:, :, c]
        return piece, piece, place.device(c=1)

    do = functools.partial
    for k in (1, 2, 3):
        copies.plan(("z", k), do(along_z, k))
    for h in (0, 1):
        copies.plan(("first", h), do(first, h))
        copies.plan(("second", h), do(second, h))
    copies.plan("core", across)

    def begin():
        local().start()
        for k in (1, 2, 3):
            copies.post(("z", k))

    def start_first():
        for k in (1, 2, 3):
            copies.got(("z", k))
        local().wait()
        for h in (0, 1):
            copies.post(("first", h))

    def start_second():
        for h in (0, 1):
            copies.got(("first", h))
            copies.post(("second", h))

    def share():
        for h in (0, 1):
            copies.got(("second", h))
        copies.post("core")

    def finish():
        copies.got("core")
        copies.sent()

    return [
        (0, 0, begin),
        (24, 1, start_first),
        (36, 2, start_second),
        (60, 3, share),
        (62, 4, finish),
    ]


def gather_z_last_plan(place, shard, out, send, recv, local_sem):
    y, x, c, z = place.y, place.x, place.c, place.z
    rows = shard.shape[0]
    copies = Copies(send, recv)

    def half(h):
        return pl.ds(h * (rows // 2), rows // 2)

    def local():
        return pltpu.make_async_copy(shard, out.at[y, x, c, z], local_sem)

    def first(h):
        return shard.at[half(h)], out.at[y, x, c, z, half(h)], place.device(**{TURNS[h][0]: 1})

    def second(h):
        piece = out.at[y, :, c, z, half(h)] if h == 0 else out.at[:, x, c, z, half(h)]
        return piece, piece, place.device(**{TURNS[h][1]: 1})

    def along_z(k):
        piece = out.at[:, :, c, z]
        return piece, piece, place.device(z=k)

    def across():
        piece = out.at[:, :, c]
        return piece, piece, place.device(c=1)

    do = functools.partial
    for h in (0, 1):
        copies.plan(("first", h), do(first, h))
        copies.plan(("second", h), do(second, h))
    for k in (1, 2, 3):
        copies.plan(("z", k), do(along_z, k))
    copies.plan("core", across)

    def begin():
        local().start()
        for h in (0, 1):
            copies.post(("first", h))

    def start_second():
        local().wait()
        for h in (0, 1):
            copies.got(("first", h))
            copies.post(("second", h))

    def column():
        for h in (0, 1):
            copies.got(("second", h))
        for k in (1, 2, 3):
            copies.post(("z", k))

    def share():
        for k in (1, 2, 3):
            copies.got(("z", k))
        copies.post("core")

    def finish():
        copies.got("core")
        copies.sent()

    return [(0, 0, begin), (3, 1, start_second), (9, 2, column), (93, 3, share), (100, 4, finish)]


def reduce_plan(
    place, parts, out, held, from_core, from_second, from_first, from_z, send, recv, load
):
    y, x, c, z = place.y, place.x, place.c, place.z
    rows = parts.shape[-2]
    whole_first = rows < 64
    groups = [(0, 1, 2, 3)] if whole_first else [(3,), (2,), (1,), (0,)]
    copies = Copies(send, recv)

    def half(h):
        return pl.ds(h * (rows // 2), rows // 2)

    def local(group):
        span = place.span(group)
        return pltpu.make_async_copy(
            parts.at[:, :, c, span], held.at[:, :, span], load.at[groups.index(group)]
        )

    def core_route(group):
        span = place.span(group)
        return parts.at[:, :, 1 - c, span], from_core.at[:, :, span], place.device(c=1)

    def second_part(group, h, other):
        at = (1 - y if other else y) if h == 0 else (1 - x if other else x)
        if h == 0:
            return (at, slice(None), place.span(group), half(h))
        return (slice(None), at, place.span(group), half(h))

    def second_route(group, h):
        return (
            held.at[second_part(group, h, True)],
            from_second.at[h, :, place.span(group)],
            place.device(**{TURNS[h][1]: 1}),
        )

    def first_part(group, h):
        return (y, 1 - x, place.span(group), half(h)) if h == 0 else (1 - y, x, place.span(group), half(h))

    def first_route(group, h):
        return (
            held.at[first_part(group, h)],
            from_first.at[h, place.span(group)],
            place.device(**{TURNS[h][0]: 1}),
        )

    def z_route(k):
        return held.at[y, x, flip(z, k)], from_z.at[k - 1], place.device(z=k)

    do = functools.partial
    for group in groups:
        copies.plan(("core", group), do(core_route, group))
        for h in (0, 1):
            copies.plan(("second", group, h), do(second_route, group, h))
            copies.plan(("first", group, h), do(first_route, group, h))
        for k in group:
            if k:
                copies.plan(("z", k), do(z_route, k))

    def add(dst, *sources):
        total = dst[...].astype(F32)
        for source in sources:
            total = total + source[...].astype(F32)
        dst[...] = total.astype(BF)

    def to_core(group):
        copies.post(("core", group))
        local(group).start()

    def begin():
        to_core(groups[0])

    def cores(group):
        local(group).wait()
        copies.got(("core", group))
        at = groups.index(group)
        if at + 1 < len(groups):
            to_core(groups[at + 1])
        for other in (True, False):
            for h in (0, 1):
                part = second_part(group, h, other)
                add(held.at[part], from_core.at[part])
                if other:
                    copies.post(("second", group, h))

    def second(group):
        span = place.span(group)
        for h in (0, 1):
            copies.got(("second", group, h))
            away = 1 - x if h == 0 else 1 - y
            add(held.at[first_part(group, h)], from_second.at[h, away, span])
            copies.post(("first", group, h))

    def first(group):
        span = place.span(group)
        for h in (0, 1):
            copies.got(("first", group, h))
            mine = x if h == 0 else y
            add(held.at[y, x, span, half(h)], from_second.at[h, mine, span], from_first.at[h, span])
        for k in group:
            if k:
                copies.post(("z", k))

    def finish():
        for k in (1, 2, 3):
            copies.got(("z", k))
        total = held[y, x, z].astype(F32)
        for k in range(3):
            total = total + from_z[k].astype(F32)
        out[...] = total
        copies.sent()

    if whole_first:
        (group,) = groups
        return [
            (0, 0, begin),
            (7, 1, do(cores, group)),
            (31, 2, do(second, group)),
            (43, 3, do(first, group)),
            (67, 4, finish),
        ]
    a, b, d, e = groups
    return [
        (0, 0, begin),
        (2, 1, do(cores, a)),
        (4, 1.2, do(cores, b)),
        (6, 2, do(second, a)),
        (8, 2, do(cores, d)),
        (12, 3, do(first, a)),
        (15, 2, do(second, b)),
        (17, 2, do(cores, e)),
        (20, 3, do(first, b)),
        (24, 2, do(second, d)),
        (29, 3, do(first, d)),
        (33, 2, do(second, e)),
        (38, 3, do(first, e)),
        (42, 4, finish),
    ]


HOP_US = 2.0
FULL_BLOCK = 128 * 1024


def merge_plans(jobs, plans):
    timed = []
    start = 0.0
    for g, (job, plan) in enumerate(zip(jobs, plans)):
        size = job.rows * job.width / FULL_BLOCK
        own = 0.0 if job.beside else start
        at = 0.0
        for i, (volume, hops, step) in enumerate(plan):
            ahead = 0.0 if i else min(own, 8.0 * size)
            at = max(at, own - ahead + volume * size + hops * HOP_US)
            timed.append((at, g, i, step))
        if not job.beside:
            start += 36.0 * size
        else:
            start += 9.0 * size
    timed.sort(key=lambda item: item[:3])
    return [(item[0], item[3]) for item in timed]


ANYWHERE = pl.BlockSpec(memory_space=pl.ANY)
COPIES = 31


class Gather:
    def __init__(self, shard, z_last=False):
        self.array = shard
        self.rows, self.width = shard.shape
        self.shape = jax.ShapeDtypeStruct((2, 2, 2, 4, self.rows, self.width), BF)
        self.spec = ANYWHERE
        sems = pltpu.SemaphoreType.DMA((COPIES,))
        self.scratch = [sems, sems, pltpu.SemaphoreType.DMA]
        self.beside = z_last
        self.plan = gather_plan if self.rows >= 64 else gather_small_plan
        if z_last:
            self.plan = gather_z_last_plan

    def finish(self, out):
        return out.reshape(-1, self.width)

    def plainly(self):
        return lax.all_gather(self.array, ALL, axis=0, tiled=True)


class Reduce:
    def __init__(self, parts):
        devices = lax.axis_size("dp") * lax.axis_size("ffn")
        self.parts = parts
        self.rows, width = parts.shape[0] // devices, parts.shape[1]
        self.width, self.beside = width, False
        self.shape = jax.ShapeDtypeStruct((self.rows, width), F32)
        self.spec = pl.BlockSpec((self.rows, width), lambda *_: (0, 0))
        sems = pltpu.SemaphoreType.DMA((COPIES,))
        rows = self.rows
        self.scratch = [
            pltpu.VMEM((2, 2, 4, rows, width), BF),
            pltpu.VMEM((2, 2, 4, rows, width), BF),
            pltpu.VMEM((2, 2, 4, rows // 2, width), BF),
            pltpu.VMEM((2, 4, rows // 2, width), BF),
            pltpu.VMEM((3, rows, width), BF),
            sems,
            sems,
            pltpu.SemaphoreType.DMA((4,)),
        ]
        self.plan = reduce_plan

    @property
    def array(self):
        return self.parts.reshape(2, 2, 2, 4, self.rows, self.parts.shape[1])

    def finish(self, out):
        return out

    def plainly(self):
        return lax.psum_scatter(self.parts, ALL, scatter_dimension=0, tiled=True).astype(F32)


def on_fast_grid():
    return lax.axis_size("dp") == 8 and lax.axis_size("ffn") == 4


def fused_call(body, steps, ins, outs, scratch, jobs, collective_id, ticks=1, cost=(0, 1, 0)):
    plainly = not (on_fast_grid() and all(job.rows % 32 == 0 for job in jobs))
    run = [] if plainly else jobs
    held = [i for i, item in enumerate(ins) if item[1] is None]
    counts = [len(ins), len(run), len(outs), len(run), len(scratch), len(held), len(held)]

    def kernel(*refs):
        groups = []
        at = 0
        for count in counts:
            groups.append(refs[at : at + count])
            at += count
        own_in, job_in, own_out, job_out, own_scratch, buffers, arrived = groups
        own_in = list(own_in)
        loads = []
        for i, buffer, sem in zip(held, buffers, arrived):
            loads.append((own_in[i], buffer, sem))
            own_in[i] = buffer
        t = pl.program_id(0)
        if loads:

            @pl.when(t == 0)
            def _():
                for load in loads:
                    pltpu.make_async_copy(*load).start()

        here = {}
        rest = []
        if run:
            place = Place()
            plans = []
            for job, src, dst in zip(run, job_in, job_out):
                plans.append(job.plan(place, src, dst, *refs[at : at + len(job.scratch)]))
                at += len(job.scratch)
            merged = merge_plans(run, plans)
            before, each_step, after = cost
            pace = min(1.0, (before + each_step * steps + after) / merged[-1][0])
            position = 0
            for when, step in merged:
                while position < steps * ticks:
                    clock = position * each_step / ticks + (before if position else 0)
                    if clock >= when * pace:
                        break
                    position += 1
                if position < steps * ticks:
                    here.setdefault(position, []).append(step)
                else:
                    rest.append(step)
            here.setdefault(0, []).insert(0, functools.partial(greet, place))

        def tick(j):
            for position in sorted(here):
                if position % ticks == j:

                    @pl.when(t == position // ticks)
                    def _(now=here[position]):
                        for each in now:
                            each()

        tick(0)
        if loads:

            @pl.when(t == 0)
            def _():
                for load in loads:
                    pltpu.make_async_copy(*load).wait()

        if body is not None:
            body(t, tick, *own_in, *own_out, *own_scratch)
        if rest:

            @pl.when(t == steps - 1)
            def _():
                for each in rest:
                    each()

    all_scratch = list(scratch)
    all_scratch += [pltpu.VMEM(ins[i][0].shape, ins[i][0].dtype) for i in held]
    all_scratch += [pltpu.SemaphoreType.DMA] * len(held)
    for job in run:
        all_scratch += job.scratch
    extra = dict(collective_id=collective_id, has_side_effects=True) if run else {}
    results = pl.pallas_call(
        kernel,
        grid=(steps,),
        out_shape=tuple(o[0] for o in outs) + tuple(job.shape for job in run),
        in_specs=[i[1] or ANYWHERE for i in ins] + [ANYWHERE] * len(run),
        out_specs=tuple(o[1] for o in outs) + tuple(job.spec for job in run),
        scratch_shapes=all_scratch,
        compiler_params=pltpu.CompilerParams(vmem_limit_bytes=60 * MIB, **extra),
    )(*[i[0] for i in ins], *[job.array for job in run])
    own = list(results[: len(outs)])
    if plainly:
        return own, [job.plainly() for job in jobs]
    return own, [job.finish(out) for job, out in zip(jobs, results[len(outs) :])]


def transfer(jobs, collective_id):
    if not (on_fast_grid() and all(job.rows % 32 == 0 for job in jobs)):
        return [job.plainly() for job in jobs]
    return fused_call(None, 1, [], [], [], jobs, collective_id)[1]


def whole(array):
    return array, None


def rows_of(array, first, count):
    if on_fast_grid() and count % 16 == 0 and first % count == 0:
        shape = (array.shape[0], count, D)
        at = first // count
        return array, pl.BlockSpec(shape, lambda t: (0, at, 0), pipeline_mode=pl.Buffered(1))
    return whole(array[:, first : first + count].reshape(-1, D))


def unit_rows(array, count, total):
    return array, pl.BlockSpec((total // count, count, D), lambda n: (n, 0, 0))


def flat(ref):
    return ref[...].reshape(-1, D)


def block(array, shape, at):
    return array, pl.BlockSpec(shape, at)


def result(shape, dtype, tile=None, at=None):
    rank = len(shape)
    if tile is None:
        return jax.ShapeDtypeStruct(shape, dtype), pl.BlockSpec(shape, lambda t: (0,) * rank)
    return jax.ShapeDtypeStruct(shape, dtype), pl.BlockSpec(tile, at)


def chunks(rows, size, body):
    @pl.loop(0, rows // size)
    def _(i):
        body(pl.ds(pl.multiple_of(i * size, size), size))


QUERY_BLOCK = 256
CHUNK = 128
UNITS = 512


def head_slope(head):
    level = head.astype(F32) + 1.0
    return jnp.exp2(jnp.full((1, 1), -8.0 / HEADS, F32) * level)


def scores_t(query, keys, slope, start, rows):
    at_key = lax.broadcasted_iota(jnp.int32, (rows, 1), 0).astype(F32)
    scores = dot_nt(keys, query) * HEAD_DIM ** (-0.5) + at_key * slope
    at_key = lax.broadcasted_iota(jnp.int32, (rows, QUERY_BLOCK), 0)
    at_query = lax.broadcasted_iota(jnp.int32, (rows, QUERY_BLOCK), 1) + start
    return jnp.where(at_key <= at_query, scores, masked_score)


def attend_body(t, tick, x, vec, wq, wk, wv, head_vec, qkv, mixed, lse, acts):
    length = x.shape[0]

    @pl.when(t == 0)
    def _():
        def norm(rows):
            normed = layer_norm(x[rows, :].astype(F32), vec[0:1, :], vec[1:2, :])[0]
            acts[rows, :] = normed.astype(BF)

        chunks(length, CHUNK, norm)

    weights = jnp.concatenate([wq[...], wk[...], wv[...]], axis=0)
    projected = dot_nt(acts[...], weights)
    qkv[0] = (projected[:, :HEAD_DIM] + head_vec[2:3, :]).astype(BF)
    qkv[1] = projected[:, HEAD_DIM : 2 * HEAD_DIM].astype(BF)
    values = projected[:, 2 * HEAD_DIM :] + head_vec[3:4, :]
    qkv[2] = values.astype(BF)
    values_t = values.T.astype(BF)
    tick(1)
    slope = head_slope(t)
    for start in range(0, length, QUERY_BLOCK):
        rows = start + QUERY_BLOCK
        scores = scores_t(qkv[0, start:rows, :], qkv[1, :rows, :], slope, start, rows)
        highest = jnp.max(scores, axis=0, keepdims=True)
        weights = jnp.exp(scores - highest)
        totals = jnp.sum(weights, axis=0, keepdims=True)
        mix = dot_nn(values_t[:, :rows], weights.astype(BF)) / totals
        mixed[start:rows, :] = mix.T.astype(BF)
        lse[0, :, start:rows] = highest + jnp.log(totals)
        if rows < length:
            tick(2 + start // QUERY_BLOCK)


def attend(x, vec, qkv_full, jobs, collective_id):
    tokens = x.shape[0]
    head_rows = lambda part: block(
        qkv_full, (HEAD_DIM, D), lambda h: (part * HEADS + h, 0)
    )
    return fused_call(
        attend_body,
        HEADS,
        [
            whole(x),
            whole(vec),
            head_rows(0),
            head_rows(1),
            head_rows(2),
            block(vec, (8, HEAD_DIM), lambda h: (0, h)),
        ],
        [
            result((3, tokens, D), BF, (3, tokens, HEAD_DIM), lambda h: (0, 0, h)),
            result((tokens, D), BF, (tokens, HEAD_DIM), lambda h: (0, h)),
            result((HEADS, 1, tokens), F32, (1, 1, tokens), lambda h: (h, 0, 0)),
            result((tokens, D), BF),
        ],
        [],
        jobs,
        collective_id,
        ticks=5,
        cost=(3, 3.4, 0),
    )


def gelu_pair(pre):
    half = 0.5 * (1.0 + lax.erf(pre * 0.7071067811865476))
    slope = half + pre * jnp.exp(-0.5 * pre * pre) * 0.3989422804014327
    return pre * half, slope


def hidden_body(t, tick, x, mixed, out_w, vec, dy, up, bias, residual, acts, hidden, slope, down_t):
    tokens = x.shape[0]

    @pl.when(t == 0)
    def _():
        def enter(rows):
            attended = dot_nt(mixed[rows, :], flat(out_w)) + vec[4:5, :]
            here = x[rows, :].astype(F32) + attended
            residual[rows, :] = here
            acts[rows, :] = layer_norm(here, vec[5:6, :], vec[6:7, :])[0].astype(BF)

        chunks(tokens, 2 * CHUNK, enter)

    for start in range(0, tokens, 256):
        rows = slice(start, start + 256)
        pre = dot_nt(acts[rows, :], flat(up)) + bias[...]
        value, steep = gelu_pair(pre)
        hidden[rows, :] = value.astype(BF)
        slope[rows, :] = steep.astype(BF)
        tick(1 + start // 256)
    down_t[...] = dot_tn(hidden[...], dy[...]).astype(BF)


def hidden_forward(x, mixed, weights, widths, vec, dy, bias, jobs, collective_id):
    tokens = x.shape[0]
    units = bias.shape[1]
    up_rows, out_rows = widths
    return fused_call(
        hidden_body,
        units // UNITS,
        [
            whole(x),
            whole(mixed),
            rows_of(weights, up_rows, out_rows),
            whole(vec),
            whole(dy),
            unit_rows(weights, up_rows, UNITS),
            block(bias, (1, UNITS), lambda n: (0, n)),
        ],
        [
            result((tokens, D), F32),
            result((tokens, D), BF),
            result((tokens, units), BF, (tokens, UNITS), lambda n: (0, n)),
            result((tokens, units), BF, (tokens, UNITS), lambda n: (0, n)),
            result((units, D), BF, (UNITS, D), lambda n: (n, 0)),
        ],
        [],
        jobs,
        collective_id,
        ticks=5,
        cost=(5, 4, 0),
    )


def hidden_back_body(
    t, tick, dy, acts, residual, hidden, slope, down, up, vec,
    out, up_t, bias_sum, dh, dh_low, sums, total, back, du,
):
    tokens = dy.shape[0]
    last = pl.num_programs(0) - 1

    def accumulate(into, value):
        @pl.when(t == 0)
        def _():
            into[...] = value

        @pl.when(t > 0)
        def _():
            into[...] += value

    accumulate(total, dot_nn(hidden[...], flat(down)))
    tick(1)
    du[...] = (dot_nt(dy[...], flat(down)) * slope[...].astype(F32)).astype(BF)
    bias_sum[...] = jnp.sum(du[...].astype(F32), axis=0, keepdims=True)
    tick(2)
    up_t[...] = dot_tn(du[...], acts[...]).astype(BF)
    tick(3)
    accumulate(back, dot_nn(du[...], flat(up)))

    @pl.when(t == last)
    def _():
        sums[...] = jnp.zeros_like(sums)

        def leave(rows):
            here = residual[rows, :]
            out[rows, :] = (here + total[rows, :] + vec[7:8, :]).astype(BF)
            grad = back[rows, :]
            normed, inverse = layer_norm(here, 1.0, 0.0)[1:]
            change, gain, shift = norm_backward(grad, normed, inverse, vec[5:6, :])
            upstream = dy[rows, :].astype(F32)
            here = upstream + change
            dh[rows, :] = here
            low = here.astype(BF)
            dh_low[rows, :] = low
            bias = jnp.sum(low.astype(F32), axis=0)
            for row, value in enumerate((bias, gain, shift, jnp.sum(upstream, axis=0))):
                sums[4 + row : 5 + row, :] += value[None]

        chunks(tokens, CHUNK, leave)


def hidden_backward(
    dy, acts, residual, hidden, slope, down_weights, weights, unit_count, vec, jobs, collective_id
):
    tokens = dy.shape[0]
    units = hidden.shape[1]
    column = lambda array: block(array, (tokens, UNITS), lambda n: (0, n))
    return fused_call(
        hidden_back_body,
        units // UNITS,
        [
            whole(dy),
            whole(acts),
            whole(residual),
            column(hidden),
            column(slope),
            unit_rows(down_weights, unit_count, UNITS),
            unit_rows(weights, unit_count, UNITS),
            whole(vec),
        ],
        [
            result((tokens, D), BF),
            result((units, D), BF, (UNITS, D), lambda n: (n, 0)),
            result((1, units), F32, (1, UNITS), lambda n: (0, n)),
            result((tokens, D), F32),
            result((tokens, D), BF),
            result((8, D), F32),
        ],
        [
            pltpu.VMEM((tokens, D), F32),
            pltpu.VMEM((tokens, D), F32),
            pltpu.VMEM((tokens, UNITS), BF),
        ],
        jobs,
        collective_id,
        ticks=4,
        cost=(0, 6.5, 6),
    )


def attend_back_body(
    t, tick, dh_low, out_w, mixed, x, dh, vec, acts, qkv, lse, wq, wk, wv, sums_in,
    out_t, qkv_t, grad_in, sums, upstream, grads, dk, dv, back,
):
    length = x.shape[0]
    last = pl.num_programs(0) - 1
    scale = HEAD_DIM ** (-0.5)

    @pl.when(t == 0)
    def _():
        def enter(rows):
            value = dot_nn(dh_low[rows, :], flat(out_w)).astype(BF)
            for head in range(HEADS):
                upstream[head, rows, :] = value[:, head * HEAD_DIM : (head + 1) * HEAD_DIM]

        chunks(length, 2 * CHUNK, enter)
        out_t[...] = dot_tn(dh_low[...], mixed[...]).astype(BF)
        sums[...] = sums_in[...]

    slope = head_slope(t)
    keys_t = qkv[1].astype(F32).T.astype(BF)
    for start in reversed(range(0, length, QUERY_BLOCK)):
        rows = start + QUERY_BLOCK
        query = qkv[0, start:rows, :]
        above = upstream[t, start:rows, :]
        scores = scores_t(query, qkv[1, :rows, :], slope, start, rows)
        probs = jnp.exp(scores - lse[0, :, start:rows])
        prob_grad = dot_nt(qkv[2, :rows, :], above)
        weighted = probs * prob_grad
        centered = jnp.sum(weighted, axis=0, keepdims=True)
        score_grad = (weighted - probs * centered).astype(BF)
        query_grad = dot_nn(keys_t[:, :rows], score_grad) * scale
        grads[start:rows, :HEAD_DIM] = query_grad.T.astype(BF)
        key_part = dot_nn(score_grad, query)
        value_part = dot_nn(probs.astype(BF), above)
        if rows == length:
            dk[...] = key_part
            dv[...] = value_part
        else:
            dk[:rows, :] += key_part
            dv[:rows, :] += value_part
        tick((length - start) // QUERY_BLOCK)
    grads[:, HEAD_DIM : 2 * HEAD_DIM] = (dk[...] * scale).astype(BF)
    grads[:, 2 * HEAD_DIM :] = dv[...].astype(BF)
    totals = jnp.sum(grads[...].astype(F32), axis=0, keepdims=True)
    lanes = pl.ds(pl.multiple_of(t * HEAD_DIM, HEAD_DIM), HEAD_DIM)
    sums[2:3, lanes] = totals[:, :HEAD_DIM]
    sums[3:4, lanes] = totals[:, 2 * HEAD_DIM :]
    weight_grad = dot_tn(grads[...], acts[...]).astype(BF)
    for part in range(3):
        qkv_t[part] = weight_grad[part * HEAD_DIM : (part + 1) * HEAD_DIM, :]
    tick(length // QUERY_BLOCK + 1)
    weights = jnp.concatenate([wq[...], wk[...], wv[...]], axis=0)
    more = dot_nn(grads[...], weights)

    @pl.when(t == 0)
    def _():
        back[...] = more

    @pl.when(t > 0)
    def _():
        back[...] += more

    @pl.when(t == last)
    def _():
        def leave(rows):
            normed, inverse = layer_norm(x[rows, :].astype(F32), 1.0, 0.0)[1:]
            change, gain, shift = norm_backward(back[rows, :], normed, inverse, vec[0:1, :])
            grad_in[rows, :] = (dh[rows, :] + change).astype(BF)
            sums[0:1, :] += gain[None]
            sums[1:2, :] += shift[None]

        chunks(length, CHUNK, leave)


def attend_backward(
    dh_low, weights, widths, mixed, x, dh, vec, acts, qkv, lse, qkv_full, sums, jobs, collective_id
):
    tokens = x.shape[0]
    head_rows = lambda part: block(
        qkv_full, (HEAD_DIM, D), lambda h: (part * HEADS + h, 0)
    )
    return fused_call(
        attend_back_body,
        HEADS,
        [
            whole(dh_low),
            rows_of(weights, *widths),
            whole(mixed),
            whole(x),
            whole(dh),
            whole(vec),
            whole(acts),
            block(qkv, (3, tokens, HEAD_DIM), lambda h: (0, 0, h)),
            block(lse, (1, 1, tokens), lambda h: (h, 0, 0)),
            head_rows(0),
            head_rows(1),
            head_rows(2),
            whole(sums),
        ],
        [
            result((D, D), BF),
            result((3, D, D), BF, (3, HEAD_DIM, D), lambda h: (0, h, 0)),
            result((tokens, D), BF),
            result((8, D), F32),
        ],
        [
            pltpu.VMEM((HEADS, tokens, HEAD_DIM), BF),
            pltpu.VMEM((tokens, 3 * HEAD_DIM), BF),
            pltpu.VMEM((tokens, HEAD_DIM), F32),
            pltpu.VMEM((tokens, HEAD_DIM), F32),
            pltpu.VMEM((tokens, D), F32),
        ],
        jobs,
        collective_id,
        ticks=6,
        cost=(9, 6.7, 6),
    )


def renew_body(
    t, tick, own, full, root, n_stat, m_stat, m_root, weight, new_n, new_m, new_w, left, product
):
    last = pl.num_programs(0) - 1
    me = lax.axis_index("dp") * lax.axis_size("ffn") + lax.axis_index("ffn")
    rows_owned = m_stat.shape[0]
    share = 128 // rows_owned
    lanes = pl.ds(pl.multiple_of((me // share) * 128, 128), 128)
    here = flat(full)
    new_n[...] = decay_rate * n_stat[...] + (1.0 - decay_rate) * dot_nt(own[...], here)
    left_part = dot_tn(full[:, :, lanes].reshape(-1, 128), here)
    product_part = dot_nn(root[...].astype(BF), here)

    @pl.when(t == 0)
    def _():
        left[...] = left_part
        product[...] = product_part

    @pl.when(t > 0)
    def _():
        left[...] += left_part
        product[...] += product_part

    @pl.when(t == last)
    def _():
        mine = left[pl.ds(pl.multiple_of((me % share) * rows_owned, rows_owned), rows_owned), :]
        new_m[...] = decay_rate * m_stat[...] + (1.0 - decay_rate) * mine
        step = dot_nt(product[...].astype(BF), flat(m_root))
        new_w[...] = weight[...] - matrix_rate * step


def renew(own, gathered, at, n_root, n_stat, m_stat, roots, root_at, weight, jobs, collective_id):
    rows, total = own.shape[0], n_stat.shape[1]
    rows_owned = m_stat.shape[0]
    if not on_fast_grid():
        full = gathered[:, at : at + rows].reshape(-1, D)
        m_root = roots[:, root_at : root_at + rows_owned].reshape(-1, D)
        me = lax.axis_index("dp") * lax.axis_size("ffn") + lax.axis_index("ffn")
        new_n = decay_rate * n_stat + (1.0 - decay_rate) * dot_nt(own, full)
        mine = lax.dynamic_slice_in_dim(full, me * rows_owned, rows_owned, 1)
        new_m = decay_rate * m_stat + (1.0 - decay_rate) * dot_tn(mine, full)
        product = dot_nn(n_root.astype(BF), full)
        new_w = weight - matrix_rate * dot_nt(product.astype(BF), m_root)
        return [new_n, new_m, new_w], [job.plainly() for job in jobs]
    owners = 16 if rows == 32 else 4
    size = owners * rows
    column = lambda array: block(array, (rows, size), lambda n: (0, n))
    return fused_call(
        renew_body,
        total // size,
        [
            whole(own),
            block(gathered, (owners, rows, D), lambda n: (n, at // rows, 0)),
            column(n_root),
            column(n_stat),
            whole(m_stat),
            rows_of(roots, root_at, rows_owned),
            whole(weight),
        ],
        [
            result((rows, total), F32, (rows, size), lambda n: (0, n)),
            result((rows_owned, D), F32),
            result((rows, D), F32),
        ],
        [pltpu.VMEM((128, D), F32), pltpu.VMEM((rows, D), F32)],
        jobs,
        collective_id,
        cost=(0, 1.6, 1),
    )


SMALL_ROWS = 32
SMALL_WIDTH = 128


def pack_small(vector_part, bias_part):
    owners = vector_part.shape[0]
    flat = jnp.concatenate([vector_part.reshape(owners, -1), bias_part.reshape(owners, -1)], axis=1)
    room = SMALL_ROWS * SMALL_WIDTH
    flat = jnp.pad(flat, ((0, 0), (0, room - flat.shape[1])))
    return flat.reshape(owners * SMALL_ROWS, SMALL_WIDTH)


def unpack_small(packed, columns, units):
    owners = packed.shape[0] // SMALL_ROWS
    flat = packed.reshape(owners, -1)
    vector_part = flat[:, : 8 * columns].reshape(owners, 8, columns)
    bias_part = flat[:, 8 * columns : 8 * columns + units]
    return vector_part, bias_part


def shards(
    block_input,
    cotangent,
    w_qkv,
    w_out,
    w_up,
    w_down,
    vectors,
    b_up,
    qkv_left,
    qkv_right,
    out_left,
    out_right,
    up_left,
    up_right,
    down_left,
    down_right,
    qkv_left_root,
    qkv_right_root,
    out_left_root,
    out_right_root,
    up_left_root,
    up_right_root,
    down_left_root,
    down_right_root,
    vector_stat,
    b_up_stat,
):
    owners = lax.axis_size("dp") * lax.axis_size("ffn")
    columns = vectors.shape[1]
    units = b_up.shape[0]
    qkv_w, out_w, up_w = w_qkv.T, w_out.T, w_up.T
    small = pack_small(vectors[None], b_up[None]).astype(BF)
    units_rows, qkv_rows, out_rows = units, qkv_w.shape[0], out_w.shape[0]
    root_rows = qkv_left_root.shape[0]

    def stack(*items):
        return Gather(jnp.concatenate([item.astype(BF) for item in items], axis=0))

    def by_owner(array):
        return array.reshape(owners, -1, D)

    small_full, qkv_full = transfer([Gather(small), Gather(qkv_w.astype(BF))], 1)
    vector_low, bias_low = unpack_small(small_full, columns, units)
    vector_rows = vector_low.transpose(1, 0, 2).reshape(8, D).astype(F32)
    up_bias = bias_low.reshape(1, -1).astype(F32)
    (qkv, mixed, lse, acts_one), (up_set,) = attend(
        block_input, vector_rows, qkv_full, [stack(up_w, out_w, qkv_left_root)], 2
    )
    up_set = by_owner(up_set)
    (residual, acts_two, hidden, slope, down_t), (down_set,) = hidden_forward(
        block_input,
        mixed,
        up_set,
        (units_rows, out_rows),
        vector_rows,
        cotangent,
        up_bias,
        [stack(w_down, out_left_root)],
        3,
    )
    down_set = by_owner(down_set)
    (block_output, up_t, bias_grad, dh, dh_low, sums), (down_g, down_mroot) = hidden_backward(
        cotangent,
        acts_two,
        residual,
        hidden,
        slope,
        down_set,
        up_set,
        units_rows,
        vector_rows,
        [Reduce(down_t), stack(down_right_root)],
        4,
    )
    down_low = down_g.astype(BF)
    (out_t, qkv_t, input_grad, sums), (up_g, down_all) = attend_backward(
        dh_low,
        up_set,
        (units_rows, out_rows),
        mixed,
        block_input,
        dh,
        vector_rows,
        acts_one,
        qkv,
        lse,
        qkv_full,
        sums,
        [Reduce(up_t), Gather(down_low)],
        5,
    )
    small_part = pack_small(
        sums.reshape(8, owners, columns).transpose(1, 0, 2), bias_grad.reshape(owners, units)
    ).astype(BF)
    up_low = up_g.astype(BF)
    (new_down_n, new_down_m, new_w_down), (up_all, qkv_g, out_g, small_g) = renew(
        down_low,
        by_owner(down_all),
        0,
        down_left_root,
        down_left,
        down_right,
        by_owner(down_mroot),
        0,
        w_down,
        [
            stack(up_low, up_left_root),
            Reduce(qkv_t.reshape(-1, D)),
            Reduce(out_t),
            Reduce(small_part),
        ],
        6,
    )
    qkv_low, out_low = qkv_g.astype(BF), out_g.astype(BF)
    up_all = by_owner(up_all)
    (new_up_n, new_up_m, new_w_up), (last_all,) = renew(
        up_low,
        up_all,
        0,
        up_right_root,
        up_right,
        up_left,
        up_all,
        units_rows,
        up_w,
        [stack(qkv_low, out_low)],
        7,
    )
    last_all = by_owner(last_all)
    new_qkv_n, new_qkv_m, new_w_qkv = renew(
        qkv_low,
        last_all,
        0,
        qkv_right_root,
        qkv_right,
        qkv_left,
        up_set,
        units_rows + out_rows,
        qkv_w,
        [],
        8,
    )[0]
    new_out_n, new_out_m, new_w_out = renew(
        out_low,
        last_all,
        qkv_rows,
        out_right_root,
        out_right,
        out_left,
        down_set,
        units_rows,
        out_w,
        [],
        8,
    )[0]
    new_m = [new_qkv_m, new_out_m, new_up_m, new_down_m]
    new_n = [new_qkv_n, new_out_n, new_up_n, new_down_n]
    new_w_qkv, new_w_out, new_w_up = new_w_qkv.T, new_w_out.T, new_w_up.T
    grads = [qkv_g, out_g, up_g, down_g]
    vector_grad, b_up_grad = unpack_small(small_g, columns, units)
    vector_grad, b_up_grad = vector_grad[0], b_up_grad[0]
    new_vector_stat = decay_rate * vector_stat + (1.0 - decay_rate) * vector_grad * vector_grad
    new_vectors = vectors - vector_rate * vector_grad * lax.rsqrt(new_vector_stat)
    new_b_up_stat = decay_rate * b_up_stat + (1.0 - decay_rate) * b_up_grad * b_up_grad
    new_b_up = b_up - vector_rate * b_up_grad * lax.rsqrt(new_b_up_stat)
    return (
        block_output,
        input_grad,
        grads[0].T,
        grads[1].T,
        grads[2].T,
        grads[3],
        vector_grad,
        b_up_grad,
        new_m[0],
        new_n[0],
        new_m[1],
        new_n[1],
        new_m[2],
        new_n[2],
        new_n[3],
        new_m[3],
        new_vector_stat,
        new_b_up_stat,
        new_w_qkv,
        new_w_out,
        new_w_up,
        new_w_down,
        new_vectors,
        new_b_up,
    )


def solution(mesh):
    return jax.shard_map(
        shards,
        mesh=mesh,
        in_specs=(
            P(("dp", "ffn"), None),
            P(("dp", "ffn"), None),
            P(None, ("dp", "ffn")),
            P(None, ("dp", "ffn")),
            P(None, ("dp", "ffn")),
            P(("dp", "ffn"), None),
            P(None, ("dp", "ffn")),
            P(("dp", "ffn")),
            P(("dp", "ffn"), None),
            P(("dp", "ffn"), None),
            P(("dp", "ffn"), None),
            P(("dp", "ffn"), None),
            P(("dp", "ffn"), None),
            P(("dp", "ffn"), None),
            P(("dp", "ffn"), None),
            P(("dp", "ffn"), None),
            P(("dp", "ffn"), None),
            P(("dp", "ffn"), None),
            P(("dp", "ffn"), None),
            P(("dp", "ffn"), None),
            P(("dp", "ffn"), None),
            P(("dp", "ffn"), None),
            P(("dp", "ffn"), None),
            P(("dp", "ffn"), None),
            P(None, ("dp", "ffn")),
            P(("dp", "ffn")),
        ),
        out_specs=(
            P(("dp", "ffn"), None),
            P(("dp", "ffn"), None),
            P(None, ("dp", "ffn")),
            P(None, ("dp", "ffn")),
            P(None, ("dp", "ffn")),
            P(("dp", "ffn"), None),
            P(None, ("dp", "ffn")),
            P(("dp", "ffn")),
            P(("dp", "ffn"), None),
            P(("dp", "ffn"), None),
            P(("dp", "ffn"), None),
            P(("dp", "ffn"), None),
            P(("dp", "ffn"), None),
            P(("dp", "ffn"), None),
            P(("dp", "ffn"), None),
            P(("dp", "ffn"), None),
            P(None, ("dp", "ffn")),
            P(("dp", "ffn")),
            P(None, ("dp", "ffn")),
            P(None, ("dp", "ffn")),
            P(None, ("dp", "ffn")),
            P(("dp", "ffn"), None),
            P(None, ("dp", "ffn")),
            P(("dp", "ffn")),
        ),
        check_vma=False,
    )
```

```python
import functools
import math

import jax
import jax.numpy as jnp
from jax import lax
from jax.experimental import pallas as pl
from jax.experimental.pallas import tpu as pltpu
from jax.sharding import PartitionSpec as P

D = 1024
HEADS = 8
HEAD_DIM = 128
MESH = pl.DeviceIdType.MESH
ALL = ("dp", "ffn")
BF = jnp.bfloat16
F32 = jnp.float32
MIB = 2**20

norm_epsilon = 1e-05
decay_rate = 0.5
matrix_rate = 0.5
vector_rate = 0.1
masked_score = -1e30


def layer_norm(values, gain, shift):
    center = values - jnp.mean(values, axis=-1, keepdims=True)
    inverse = lax.rsqrt(jnp.mean(center * center, axis=-1, keepdims=True) + norm_epsilon)
    normed = center * inverse
    return (normed * gain + shift, normed, inverse)


def norm_backward(grad, normed, inverse, gain):
    scaled = grad * gain
    inner = (
        scaled
        - jnp.mean(scaled, axis=-1, keepdims=True)
        - normed * jnp.mean(scaled * normed, axis=-1, keepdims=True)
    )
    return (inner * inverse, jnp.sum(grad * normed, axis=0), jnp.sum(grad, axis=0))


def dot_nt(left, right):
    return lax.dot_general(left, right, (((1,), (1,)), ((), ())), preferred_element_type=F32)


def dot_tn(left, right):
    return lax.dot_general(left, right, (((0,), (0,)), ((), ())), preferred_element_type=F32)


def dot_nn(left, right):
    return jnp.dot(left, right, preferred_element_type=F32)


def flip(value, mask):
    result = value
    bit = 1
    while bit <= mask:
        if mask & bit:
            result = result + bit - 2 * bit * ((result // bit) % 2)
        bit *= 2
    return result


class Copies:
    def __init__(self, send, recv):
        self.send, self.recv, self.made = send, recv, {}

    def copy(self, name):
        at, make = self.made[name]
        src, dst, device = make()
        return pltpu.make_async_remote_copy(
            src, dst, self.send.at[at], self.recv.at[at], device_id=device, device_id_type=MESH
        )

    def plan(self, name, make):
        self.made[name] = (len(self.made), make)

    def post(self, name):
        self.copy(name).start()

    def got(self, name):
        self.copy(name).wait_recv()

    def sent(self):
        for name in self.made:
            self.copy(name).wait_send()


class Place:
    def __init__(self):
        dp = lax.axis_index("dp")
        self.y, self.x, self.c, self.z = dp // 4, (dp // 2) % 2, dp % 2, lax.axis_index("ffn")

    def device(self, y=0, x=0, c=0, z=0):
        dp = (flip(self.y, y) * 2 + flip(self.x, x)) * 2 + flip(self.c, c)
        return dp, flip(self.z, z)

    def span(self, group):
        if len(group) == 1:
            return pl.ds(flip(self.z, group[0]), 1)
        if len(group) == 2:
            return pl.ds(flip(self.z // 2, group[0] // 2) * 2, 2)
        return pl.ds(0, 4)


def greet(place):
    barrier = pltpu.get_barrier_semaphore()
    steps = [dict(y=1), dict(x=1), dict(c=1), dict(z=1), dict(z=2), dict(z=3)]
    for step in steps:
        pl.semaphore_signal(
            barrier, inc=1, device_id=place.device(**step), device_id_type=MESH
        )
    pl.semaphore_wait(barrier, len(steps))


def one(index):
    return pl.ds(index, 1)


TURNS = (("x", "y"), ("y", "x"))


def gather_plan(place, shard, out, send, recv, local_sem):
    y, x, c, z = place.y, place.x, place.c, place.z
    half_rows = shard.shape[0] // 2
    copies = Copies(send, recv)

    def half(ref, h):
        return ref.at[pl.ds(h * half_rows, half_rows)]

    def local():
        return pltpu.make_async_copy(shard, out.at[y, x, c, z], local_sem)

    def along_z(k):
        return shard, out.at[y, x, c, z], place.device(z=k)

    def own(turn, k, h):
        dst = half(out.at[y, x, c, flip(z, k)], h)
        return (dst if k else half(shard, h)), dst, place.device(**{TURNS[h][turn]: 1})

    def relay(k, h):
        block = out.at[y, 1 - x, c, flip(z, k)] if h == 0 else out.at[1 - y, x, c, flip(z, k)]
        return half(block, h), half(block, h), place.device(**{TURNS[h][1]: 1})

    def across(k):
        piece = out.at[:, :, c, flip(z, k)]
        return piece, piece, place.device(c=1)

    do = functools.partial
    for k in range(4):
        if k:
            copies.plan(("z", k), do(along_z, k))
        for h in (0, 1):
            copies.plan(("first", k, h), do(own, 0, k, h))
            copies.plan(("second", k, h), do(own, 1, k, h))
            copies.plan(("relay", k, h), do(relay, k, h))
        copies.plan(("core", k), do(across, k))

    def spread(k):
        for name in ("first", "second"):
            for h in (0, 1):
                copies.post((name, k, h))

    def begin():
        copies.post(("z", 1))
        spread(0)
        local().start()

    def landed(k):
        copies.got(("z", k))
        if k < 3:
            copies.post(("z", k + 1))
        spread(k)

    def forward(k):
        for h in (0, 1):
            copies.got(("first", k, h))
            copies.post(("relay", k, h))

    def share(k):
        for h in (0, 1):
            copies.got(("second", k, h))
            copies.got(("relay", k, h))
        if k == 0:
            local().wait()
        copies.post(("core", k))

    def finish():
        for k in range(4):
            copies.got(("core", k))
        copies.sent()

    return [
        (0, 0, begin),
        (4, 1, do(forward, 0)),
        (6, 1, do(landed, 1)),
        (13, 2, do(share, 0)),
        (14, 2, do(forward, 1)),
        (18, 2, do(landed, 2)),
        (20, 3, do(share, 1)),
        (24, 3, do(forward, 2)),
        (30, 2, do(landed, 3)),
        (31, 3, do(share, 2)),
        (35, 3, do(forward, 3)),
        (39, 3, do(share, 3)),
        (40, 4, finish),
    ]


def gather_small_plan(place, shard, out, send, recv, local_sem):
    y, x, c, z = place.y, place.x, place.c, place.z
    rows = shard.shape[0]
    copies = Copies(send, recv)

    def half(h):
        return pl.ds(h * (rows // 2), rows // 2)

    def local():
        return pltpu.make_async_copy(shard, out.at[y, x, c, z], local_sem)

    def along_z(k):
        return shard, out.at[y, x, c, z], place.device(z=k)

    def first(h):
        piece = out.at[y, x, c, :, half(h)]
        return piece, piece, place.device(**{TURNS[h][0]: 1})

    def second(h):
        piece = out.at[y, :, c, :, half(h)] if h == 0 else out.at[:, x, c, :, half(h)]
        return piece, piece, place.device(**{TURNS[h][1]: 1})

    def across():
        piece = out.at[:, :, c]
        return piece, piece, place.device(c=1)

    do = functools.partial
    for k in (1, 2, 3):
        copies.plan(("z", k), do(along_z, k))
    for h in (0, 1):
        copies.plan(("first", h), do(first, h))
        copies.plan(("second", h), do(second, h))
    copies.plan("core", across)

    def begin():
        local().start()
        for k in (1, 2, 3):
            copies.post(("z", k))

    def start_first():
        for k in (1, 2, 3):
            copies.got(("z", k))
        local().wait()
        for h in (0, 1):
            copies.post(("first", h))

    def start_second():
        for h in (0, 1):
            copies.got(("first", h))
            copies.post(("second", h))

    def share():
        for h in (0, 1):
            copies.got(("second", h))
        copies.post("core")

    def finish():
        copies.got("core")
        copies.sent()

    return [
        (0, 0, begin),
        (24, 1, start_first),
        (36, 2, start_second),
        (60, 3, share),
        (62, 4, finish),
    ]


def gather_z_last_plan(place, shard, out, send, recv, local_sem):
    y, x, c, z = place.y, place.x, place.c, place.z
    rows = shard.shape[0]
    copies = Copies(send, recv)

    def half(h):
        return pl.ds(h * (rows // 2), rows // 2)

    def local():
        return pltpu.make_async_copy(shard, out.at[y, x, c, z], local_sem)

    def first(h):
        return shard.at[half(h)], out.at[y, x, c, z, half(h)], place.device(**{TURNS[h][0]: 1})

    def second(h):
        piece = out.at[y, :, c, z, half(h)] if h == 0 else out.at[:, x, c, z, half(h)]
        return piece, piece, place.device(**{TURNS[h][1]: 1})

    def along_z(k):
        piece = out.at[:, :, c, z]
        return piece, piece, place.device(z=k)

    def across():
        piece = out.at[:, :, c]
        return piece, piece, place.device(c=1)

    do = functools.partial
    for h in (0, 1):
        copies.plan(("first", h), do(first, h))
        copies.plan(("second", h), do(second, h))
    for k in (1, 2, 3):
        copies.plan(("z", k), do(along_z, k))
    copies.plan("core", across)

    def begin():
        local().start()
        for h in (0, 1):
            copies.post(("first", h))

    def start_second():
        local().wait()
        for h in (0, 1):
            copies.got(("first", h))
            copies.post(("second", h))

    def column():
        for h in (0, 1):
            copies.got(("second", h))
        for k in (1, 2, 3):
            copies.post(("z", k))

    def share():
        for k in (1, 2, 3):
            copies.got(("z", k))
        copies.post("core")

    def finish():
        copies.got("core")
        copies.sent()

    return [(0, 0, begin), (3, 1, start_second), (9, 2, column), (93, 3, share), (100, 4, finish)]


def reduce_plan(
    place, parts, out, held, from_core, from_second, from_first, from_z, send, recv, load
):
    y, x, c, z = place.y, place.x, place.c, place.z
    rows = parts.shape[-2]
    whole_first = rows < 64
    groups = [(0, 1, 2, 3)] if whole_first else [(3,), (2,), (1,), (0,)]
    copies = Copies(send, recv)

    def half(h):
        return pl.ds(h * (rows // 2), rows // 2)

    def local(group):
        span = place.span(group)
        return pltpu.make_async_copy(
            parts.at[:, :, c, span], held.at[:, :, span], load.at[groups.index(group)]
        )

    def core_route(group):
        span = place.span(group)
        return parts.at[:, :, 1 - c, span], from_core.at[:, :, span], place.device(c=1)

    def second_part(group, h, other):
        at = (1 - y if other else y) if h == 0 else (1 - x if other else x)
        if h == 0:
            return (at, slice(None), place.span(group), half(h))
        return (slice(None), at, place.span(group), half(h))

    def second_route(group, h):
        return (
            held.at[second_part(group, h, True)],
            from_second.at[h, :, place.span(group)],
            place.device(**{TURNS[h][1]: 1}),
        )

    def first_part(group, h):
        return (y, 1 - x, place.span(group), half(h)) if h == 0 else (1 - y, x, place.span(group), half(h))

    def first_route(group, h):
        return (
            held.at[first_part(group, h)],
            from_first.at[h, place.span(group)],
            place.device(**{TURNS[h][0]: 1}),
        )

    def z_route(k):
        return held.at[y, x, flip(z, k)], from_z.at[k - 1], place.device(z=k)

    do = functools.partial
    for group in groups:
        copies.plan(("core", group), do(core_route, group))
        for h in (0, 1):
            copies.plan(("second", group, h), do(second_route, group, h))
            copies.plan(("first", group, h), do(first_route, group, h))
        for k in group:
            if k:
                copies.plan(("z", k), do(z_route, k))

    def add(dst, *sources):
        if len(sources) == 1:
            dst[...] += sources[0][...]
            return
        total = dst[...].astype(F32)
        for source in sources:
            total = total + source[...].astype(F32)
        dst[...] = total.astype(BF)

    def to_core(group):
        copies.post(("core", group))
        local(group).start()

    def begin():
        to_core(groups[0])

    def cores(group):
        local(group).wait()
        copies.got(("core", group))
        at = groups.index(group)
        if at + 1 < len(groups):
            to_core(groups[at + 1])
        for other in (True, False):
            for h in (0, 1):
                part = second_part(group, h, other)
                add(held.at[part], from_core.at[part])
                if other:
                    copies.post(("second", group, h))

    def second(group):
        span = place.span(group)
        for h in (0, 1):
            copies.got(("second", group, h))
            away = 1 - x if h == 0 else 1 - y
            add(held.at[first_part(group, h)], from_second.at[h, away, span])
            copies.post(("first", group, h))

    def first(group):
        span = place.span(group)
        for h in (0, 1):
            copies.got(("first", group, h))
            mine = x if h == 0 else y
            add(held.at[y, x, span, half(h)], from_second.at[h, mine, span], from_first.at[h, span])
        for k in group:
            if k:
                copies.post(("z", k))

    def finish():
        for k in (1, 2, 3):
            copies.got(("z", k))
        total = held[y, x, z].astype(F32)
        for k in range(3):
            total = total + from_z[k].astype(F32)
        out[...] = total
        copies.sent()

    if whole_first:
        (group,) = groups
        return [
            (0, 0, begin),
            (7, 1, do(cores, group)),
            (31, 2, do(second, group)),
            (43, 3, do(first, group)),
            (67, 4, finish),
        ]
    a, b, d, e = groups
    return [
        (0, 0, begin),
        (2, 1, do(cores, a)),
        (4, 1.2, do(cores, b)),
        (6, 2, do(second, a)),
        (8, 2, do(cores, d)),
        (12, 3, do(first, a)),
        (15, 2, do(second, b)),
        (17, 2, do(cores, e)),
        (20, 3, do(first, b)),
        (24, 2, do(second, d)),
        (29, 3, do(first, d)),
        (33, 2, do(second, e)),
        (38, 3, do(first, e)),
        (42, 4, finish),
    ]


HOP_US = 2.0
FULL_BLOCK = 128 * 1024


def merge_plans(jobs, plans, stagger):
    timed = []
    start = 0.0
    for g, (job, plan) in enumerate(zip(jobs, plans)):
        size = job.rows * job.width / FULL_BLOCK
        own = 0.0 if job.beside else start
        at = 0.0
        for i, (volume, hops, step) in enumerate(plan):
            ahead = 0.0 if i else min(own, 20.0 * size)
            at = max(at, own - ahead + volume * size + hops * HOP_US)
            timed.append((at, g, i, step))
        if not job.beside:
            start += stagger * size
        else:
            start += 9.0 * size
    timed.sort(key=lambda item: item[:3])
    return [(at, step, g, i == len(plans[g]) - 1) for at, g, i, step in timed]


ANYWHERE = pl.BlockSpec(memory_space=pl.ANY)
COPIES = 31


class Gather:
    def __init__(self, shard, z_last=False):
        self.array = shard
        self.rows, self.width = shard.shape
        self.shape = jax.ShapeDtypeStruct((2, 2, 2, 4, self.rows, self.width), BF)
        self.spec = ANYWHERE
        sems = pltpu.SemaphoreType.DMA((COPIES,))
        self.scratch = [sems, sems, pltpu.SemaphoreType.DMA]
        self.beside = z_last
        self.plan = gather_plan if self.rows >= 64 else gather_small_plan
        if z_last:
            self.plan = gather_z_last_plan

    def finish(self, out):
        return out.reshape(-1, self.width)

    def plainly(self):
        return lax.all_gather(self.array, ALL, axis=0, tiled=True)


class Reduce:
    def __init__(self, parts):
        devices = lax.axis_size("dp") * lax.axis_size("ffn")
        self.parts = parts
        self.rows, width = parts.shape[0] // devices, parts.shape[1]
        self.width, self.beside = width, False
        self.shape = jax.ShapeDtypeStruct((self.rows, width), F32)
        self.spec = pl.BlockSpec((self.rows, width), lambda *_: (0, 0))
        sems = pltpu.SemaphoreType.DMA((COPIES,))
        rows = self.rows
        self.scratch = [
            pltpu.VMEM((2, 2, 4, rows, width), BF),
            pltpu.VMEM((2, 2, 4, rows, width), BF),
            pltpu.VMEM((2, 2, 4, rows // 2, width), BF),
            pltpu.VMEM((2, 4, rows // 2, width), BF),
            pltpu.VMEM((3, rows, width), BF),
            sems,
            sems,
            pltpu.SemaphoreType.DMA((4,)),
        ]
        self.plan = reduce_plan

    @property
    def array(self):
        return self.parts.reshape(2, 2, 2, 4, self.rows, self.parts.shape[1])

    def finish(self, out):
        return out

    def plainly(self):
        return lax.psum_scatter(self.parts, ALL, scatter_dimension=0, tiled=True).astype(F32)


def on_fast_grid():
    return lax.axis_size("dp") == 8 and lax.axis_size("ffn") == 4


def fused_call(
    body,
    steps,
    ins,
    outs,
    scratch,
    jobs,
    collective_id,
    ticks=1,
    cost=(0, 1, 0),
    stagger=28.0,
    needs=None,
    timeline=None,
):
    plainly = not (on_fast_grid() and all(job.rows % 32 == 0 for job in jobs))
    run = [] if plainly else jobs
    held = [i for i, item in enumerate(ins) if item[1] is None]
    counts = [len(ins), len(run), len(outs), len(run), len(scratch), len(held), len(held)]

    def kernel(*refs):
        groups = []
        at = 0
        for count in counts:
            groups.append(refs[at : at + count])
            at += count
        own_in, job_in, own_out, job_out, own_scratch, buffers, arrived = groups
        own_in = list(own_in)
        loads = []
        for i, buffer, sem in zip(held, buffers, arrived):
            loads.append((own_in[i], buffer, sem))
            own_in[i] = buffer
        t = pl.program_id(0)
        if loads:

            @pl.when(t == 0)
            def _():
                for load in loads:
                    pltpu.make_async_copy(*load).start()

        here = {}
        rest = []
        if run:
            place = Place()
            plans = []
            for job, src, dst in zip(run, job_in, job_out):
                plans.append(job.plan(place, src, dst, *refs[at : at + len(job.scratch)]))
                at += len(job.scratch)
            merged = merge_plans(run, plans, stagger)
            before, each_step, after = cost
            pace = min(1.0, (before + each_step * steps + after) / merged[-1][0])
            spans = [(before * (i > 0) + each_step * i, each_step) for i in range(steps)]
            if timeline:
                pace = 1.0
                spans = timeline({g: when for when, _, g, is_last in merged if is_last})
            clocks = [0.0]
            for start, length in spans:
                clocks += [start + length * j / ticks for j in range(ticks)]
            clocks = [0.0] + clocks[2:]
            limits = [(needs or {}).get(g, steps) * ticks if is_last else steps * ticks for _, _, g, is_last in merged]
            position = 0
            for i, (when, step, _, _) in enumerate(merged):
                while position < steps * ticks and clocks[position] < when * pace:
                    position += 1
                position = min([position] + limits[i:])
                if position < steps * ticks:
                    here.setdefault(position, []).append(step)
                else:
                    rest.append(step)
            here.setdefault(0, []).insert(0, functools.partial(greet, place))

        def tick(j, least=0, most=steps):
            for position in sorted(here):
                if position % ticks == j and least <= position // ticks < most:

                    @pl.when(t == position // ticks)
                    def _(now=here[position]):
                        for each in now:
                            each()

        tick(0)
        if loads:

            @pl.when(t == 0)
            def _():
                for load in loads:
                    pltpu.make_async_copy(*load).wait()

        if body is not None:
            shared = [job_out] if needs else []
            body(t, tick, *shared, *own_in, *own_out, *own_scratch)
        if rest:

            @pl.when(t == steps - 1)
            def _():
                for each in rest:
                    each()

    all_scratch = list(scratch)
    all_scratch += [pltpu.VMEM(ins[i][0].shape, ins[i][0].dtype) for i in held]
    all_scratch += [pltpu.SemaphoreType.DMA] * len(held)
    for job in run:
        all_scratch += job.scratch
    extra = dict(collective_id=collective_id, has_side_effects=True) if run else {}
    results = pl.pallas_call(
        kernel,
        grid=(steps,),
        out_shape=tuple(o[0] for o in outs) + tuple(job.shape for job in run),
        in_specs=[i[1] or ANYWHERE for i in ins] + [ANYWHERE] * len(run),
        out_specs=tuple(o[1] for o in outs) + tuple(job.spec for job in run),
        scratch_shapes=all_scratch,
        compiler_params=pltpu.CompilerParams(vmem_limit_bytes=60 * MIB, **extra),
    )(*[i[0] for i in ins], *[job.array for job in run])
    own = list(results[: len(outs)])
    if plainly:
        return own, [job.plainly() for job in jobs]
    return own, [job.finish(out) for job, out in zip(jobs, results[len(outs) :])]


def transfer(jobs, collective_id):
    if not (on_fast_grid() and all(job.rows % 32 == 0 for job in jobs)):
        return [job.plainly() for job in jobs]
    return fused_call(None, 1, [], [], [], jobs, collective_id)[1]


def whole(array):
    return array, None


def rows_of(array, first, count):
    if on_fast_grid() and count % 16 == 0 and first % count == 0:
        shape = (array.shape[0], count, D)
        at = first // count
        return array, pl.BlockSpec(shape, lambda t: (0, at, 0), pipeline_mode=pl.Buffered(1))
    return whole(array[:, first : first + count].reshape(-1, D))


def unit_rows(array, count, total):
    return array, pl.BlockSpec((total // count, count, D), lambda n: (n, 0, 0))


def flat(ref):
    return ref[...].reshape(-1, D)


def block(array, shape, at):
    return array, pl.BlockSpec(shape, at)


def result(shape, dtype, tile=None, at=None):
    rank = len(shape)
    if tile is None:
        return jax.ShapeDtypeStruct(shape, dtype), pl.BlockSpec(shape, lambda t: (0,) * rank)
    return jax.ShapeDtypeStruct(shape, dtype), pl.BlockSpec(tile, at)


def chunks(rows, size, body):
    @pl.loop(0, rows // size)
    def _(i):
        body(pl.ds(pl.multiple_of(i * size, size), size))


QUERY_BLOCK = 256
CHUNK = 128
UNITS = 512


def head_slope(head):
    level = head.astype(F32) + 1.0
    return jnp.exp2(jnp.full((1, 1), -8.0 / HEADS, F32) * level)


def scores_t(query, keys, slope, start, rows):
    at_key = lax.broadcasted_iota(jnp.int32, (rows, 1), 0).astype(F32)
    scores = dot_nt(keys, query) * HEAD_DIM ** (-0.5) + at_key * slope
    at_key = lax.broadcasted_iota(jnp.int32, (rows, QUERY_BLOCK), 0)
    at_query = lax.broadcasted_iota(jnp.int32, (rows, QUERY_BLOCK), 1) + start
    return jnp.where(at_key <= at_query, scores, masked_score)


def attend_body(t, tick, x, vec, wq, wk, wv, head_vec, qkv, mixed, lse, acts):
    length = x.shape[0]

    @pl.when(t == 0)
    def _():
        def norm(rows):
            normed = layer_norm(x[rows, :].astype(F32), vec[0:1, :], vec[1:2, :])[0]
            acts[rows, :] = normed.astype(BF)

        chunks(length, CHUNK, norm)

    weights = jnp.concatenate([wq[...], wk[...], wv[...]], axis=0)
    projected = dot_nt(acts[...], weights)
    qkv[0] = (projected[:, :HEAD_DIM] + head_vec[2:3, :]).astype(BF)
    qkv[1] = projected[:, HEAD_DIM : 2 * HEAD_DIM].astype(BF)
    values = projected[:, 2 * HEAD_DIM :] + head_vec[3:4, :]
    qkv[2] = values.astype(BF)
    values_t = values.T.astype(BF)
    tick(1)
    slope = head_slope(t)
    for start in range(0, length, QUERY_BLOCK):
        rows = start + QUERY_BLOCK
        scores = scores_t(qkv[0, start:rows, :], qkv[1, :rows, :], slope, start, rows)
        highest = jnp.max(scores, axis=0, keepdims=True)
        weights = jnp.exp(scores - highest)
        totals = jnp.sum(weights, axis=0, keepdims=True)
        mix = dot_nn(values_t[:, :rows], weights.astype(BF)) / totals
        mixed[start:rows, :] = mix.T.astype(BF)
        lse[0, :, start:rows] = highest + jnp.log(totals)
        if rows < length:
            tick(2 + start // QUERY_BLOCK)


def attend(x, vec, qkv_full, jobs, collective_id):
    tokens = x.shape[0]
    head_rows = lambda part: block(
        qkv_full, (HEAD_DIM, D), lambda h: (part * HEADS + h, 0)
    )
    return fused_call(
        attend_body,
        HEADS,
        [
            whole(x),
            whole(vec),
            head_rows(0),
            head_rows(1),
            head_rows(2),
            block(vec, (8, HEAD_DIM), lambda h: (0, h)),
        ],
        [
            result((3, tokens, D), BF, (3, tokens, HEAD_DIM), lambda h: (0, 0, h)),
            result((tokens, D), BF, (tokens, HEAD_DIM), lambda h: (0, h)),
            result((HEADS, 1, tokens), F32, (1, 1, tokens), lambda h: (h, 0, 0)),
            result((tokens, D), BF),
        ],
        [],
        jobs,
        collective_id,
        ticks=5,
        cost=(3, 3.4, 0),
    )


def gelu_pair(pre):
    half = 0.5 * (1.0 + lax.erf(pre * 0.7071067811865476))
    slope = half + pre * jnp.exp(-0.5 * pre * pre) * 0.3989422804014327
    return pre * half, slope


def hidden_body(t, tick, x, mixed, out_w, vec, dy, up, bias, residual, acts, hidden, slope, down_t):
    tokens = x.shape[0]

    @pl.when(t == 0)
    def _():
        def enter(rows):
            attended = dot_nt(mixed[rows, :], flat(out_w)) + vec[4:5, :]
            here = x[rows, :].astype(F32) + attended
            residual[rows, :] = here
            acts[rows, :] = layer_norm(here, vec[5:6, :], vec[6:7, :])[0].astype(BF)

        chunks(tokens, 2 * CHUNK, enter)

    for start in range(0, tokens, 256):
        rows = slice(start, start + 256)
        pre = dot_nt(acts[rows, :], flat(up)) + bias[...]
        value, steep = gelu_pair(pre)
        hidden[rows, :] = value.astype(BF)
        slope[rows, :] = steep.astype(BF)
        tick(1 + start // 256)
    down_t[...] = dot_tn(hidden[...], dy[...]).astype(BF)


def hidden_forward(x, mixed, weights, widths, vec, dy, bias, jobs, collective_id):
    tokens = x.shape[0]
    units = bias.shape[1]
    up_rows, out_rows = widths
    return fused_call(
        hidden_body,
        units // UNITS,
        [
            whole(x),
            whole(mixed),
            rows_of(weights, up_rows, out_rows),
            whole(vec),
            whole(dy),
            unit_rows(weights, up_rows, UNITS),
            block(bias, (1, UNITS), lambda n: (0, n)),
        ],
        [
            result((tokens, D), F32),
            result((tokens, D), BF),
            result((tokens, units), BF, (tokens, UNITS), lambda n: (0, n)),
            result((tokens, units), BF, (tokens, UNITS), lambda n: (0, n)),
            result((units, D), BF, (UNITS, D), lambda n: (n, 0)),
        ],
        [],
        jobs,
        collective_id,
        ticks=5,
        cost=(5, 4, 0),
    )


def accumulate(t, into, value):
    @pl.when(t == 0)
    def _():
        into[...] = value

    @pl.when(t > 0)
    def _():
        into[...] += value


def hidden_back_body(
    t, tick, dy, acts, residual, slope, down, up, vec, up_t, bias_sum, dh, dh_low, sums, back, du
):
    tokens = dy.shape[0]
    last = pl.num_programs(0) - 1
    du[...] = (dot_nt(dy[...], flat(down)) * slope[...].astype(F32)).astype(BF)
    bias_sum[...] = jnp.sum(du[...].astype(F32), axis=0, keepdims=True)
    tick(1)
    up_t[...] = dot_tn(du[...], acts[...]).astype(BF)
    tick(2)
    accumulate(t, back, dot_nn(du[...], flat(up)))

    @pl.when(t == last)
    def _():
        sums[...] = jnp.zeros_like(sums)

        def leave(rows):
            grad = back[rows, :]
            normed, inverse = layer_norm(residual[rows, :], 1.0, 0.0)[1:]
            change, gain, shift = norm_backward(grad, normed, inverse, vec[5:6, :])
            upstream = dy[rows, :].astype(F32)
            here = upstream + change
            dh[rows, :] = here
            low = here.astype(BF)
            dh_low[rows, :] = low
            bias = jnp.sum(low.astype(F32), axis=0)
            for row, value in enumerate((bias, gain, shift, jnp.sum(upstream, axis=0))):
                sums[4 + row : 5 + row, :] += value[None]

        chunks(tokens, CHUNK, leave)


def hidden_backward(
    dy, acts, residual, slope, down_weights, weights, unit_count, vec, jobs, collective_id
):
    tokens = dy.shape[0]
    units = slope.shape[1]
    return fused_call(
        hidden_back_body,
        units // UNITS,
        [
            whole(dy),
            whole(acts),
            whole(residual),
            block(slope, (tokens, UNITS), lambda n: (0, n)),
            unit_rows(down_weights, unit_count, UNITS),
            unit_rows(weights, unit_count, UNITS),
            whole(vec),
        ],
        [
            result((units, D), BF, (UNITS, D), lambda n: (n, 0)),
            result((1, units), F32, (1, UNITS), lambda n: (0, n)),
            result((tokens, D), F32),
            result((tokens, D), BF),
            result((8, D), F32),
        ],
        [pltpu.VMEM((tokens, D), F32), pltpu.VMEM((tokens, UNITS), BF)],
        jobs,
        collective_id,
        ticks=3,
        cost=(0, 5, 5),
        stagger=10.0,
    )


def output_body(t, tick, hidden, down, residual, vec, out, total):
    accumulate(t, total, dot_nn(hidden[...], flat(down)))

    @pl.when(t == pl.num_programs(0) - 1)
    def _():
        def leave(rows):
            out[rows, :] = (residual[rows, :] + total[rows, :] + vec[7:8, :]).astype(BF)

        chunks(hidden.shape[0], CHUNK, leave)


def output_part(hidden, down_weights, unit_count, residual, vec):
    tokens = hidden.shape[0]
    return (
        output_body,
        [
            block(hidden, (tokens, UNITS), lambda n: (0, n)),
            unit_rows(down_weights, unit_count, UNITS),
            whole(residual),
            whole(vec),
        ],
        [result((tokens, D), BF)],
        [pltpu.VMEM((tokens, D), F32)],
        (0, 1.7, 2),
    )


def attend_back_body(
    t, tick, dh_low, out_w, mixed, acts, qkv, lse, sums_in,
    out_t, qkv_t, grads_out, sums, upstream, dk, dv,
):
    length = acts.shape[0]
    scale = HEAD_DIM ** (-0.5)
    grads = grads_out.at[0]

    @pl.when(t == 0)
    def _():
        def enter(rows):
            value = dot_nn(dh_low[rows, :], flat(out_w)).astype(BF)
            for head in range(HEADS):
                upstream[head, rows, :] = value[:, head * HEAD_DIM : (head + 1) * HEAD_DIM]

        chunks(length, 2 * CHUNK, enter)
        out_t[...] = dot_tn(dh_low[...], mixed[...]).astype(BF)
        sums[...] = sums_in[...]

    slope = head_slope(t)
    keys_t = qkv[1].astype(F32).T.astype(BF)
    for start in reversed(range(0, length, QUERY_BLOCK)):
        rows = start + QUERY_BLOCK
        query = qkv[0, start:rows, :]
        above = upstream[t, start:rows, :]
        scores = scores_t(query, qkv[1, :rows, :], slope, start, rows)
        probs = jnp.exp(scores - lse[0, :, start:rows])
        prob_grad = dot_nt(qkv[2, :rows, :], above)
        weighted = probs * prob_grad
        centered = jnp.sum(weighted, axis=0, keepdims=True)
        score_grad = (weighted - probs * centered).astype(BF)
        query_grad = dot_nn(keys_t[:, :rows], score_grad) * scale
        grads[start:rows, :HEAD_DIM] = query_grad.T.astype(BF)
        key_part = dot_nn(score_grad, query)
        value_part = dot_nn(probs.astype(BF), above)
        if rows == length:
            dk[...] = key_part
            dv[...] = value_part
        else:
            dk[:rows, :] += key_part
            dv[:rows, :] += value_part
        tick((length - start) // QUERY_BLOCK)
    grads[:, HEAD_DIM : 2 * HEAD_DIM] = (dk[...] * scale).astype(BF)
    grads[:, 2 * HEAD_DIM :] = dv[...].astype(BF)
    totals = jnp.sum(grads[...].astype(F32), axis=0, keepdims=True)
    lanes = pl.ds(pl.multiple_of(t * HEAD_DIM, HEAD_DIM), HEAD_DIM)
    sums[2:3, lanes] = totals[:, :HEAD_DIM]
    sums[3:4, lanes] = totals[:, 2 * HEAD_DIM :]
    weight_grad = dot_tn(grads[...], acts[...]).astype(BF)
    for part in range(3):
        qkv_t[part] = weight_grad[part * HEAD_DIM : (part + 1) * HEAD_DIM, :]


def attend_backward(dh_low, weights, widths, mixed, acts, qkv, lse, sums, jobs, collective_id):
    tokens = acts.shape[0]
    return fused_call(
        attend_back_body,
        HEADS,
        [
            whole(dh_low),
            rows_of(weights, *widths),
            whole(mixed),
            whole(acts),
            block(qkv, (3, tokens, HEAD_DIM), lambda h: (0, 0, h)),
            block(lse, (1, 1, tokens), lambda h: (h, 0, 0)),
            whole(sums),
        ],
        [
            result((D, D), BF),
            result((3, D, D), BF, (3, HEAD_DIM, D), lambda h: (0, h, 0)),
            result(
                (HEADS, tokens, 3 * HEAD_DIM), BF, (1, tokens, 3 * HEAD_DIM), lambda h: (h, 0, 0)
            ),
            result((8, D), F32),
        ],
        [
            pltpu.VMEM((HEADS, tokens, HEAD_DIM), BF),
            pltpu.VMEM((tokens, HEAD_DIM), F32),
            pltpu.VMEM((tokens, HEAD_DIM), F32),
        ],
        jobs,
        collective_id,
        ticks=5,
        cost=(7, 5.4, 0),
        stagger=0.1,
    )


def input_body(t, tick, grads, wq, wk, wv, x, dh, vec, grad_in, sums, back):
    weights = jnp.concatenate([wq[...], wk[...], wv[...]], axis=0)
    accumulate(t, back, dot_nn(grads[0], weights))

    @pl.when(t == pl.num_programs(0) - 1)
    def _():
        sums[...] = jnp.zeros_like(sums)

        def leave(rows):
            normed, inverse = layer_norm(x[rows, :].astype(F32), 1.0, 0.0)[1:]
            change, gain, shift = norm_backward(back[rows, :], normed, inverse, vec[0:1, :])
            grad_in[rows, :] = (dh[rows, :] + change).astype(BF)
            sums[0:1, :] += gain[None]
            sums[1:2, :] += shift[None]

        chunks(x.shape[0], CHUNK, leave)


def input_part(grads, qkv_full, x, dh, vec):
    tokens = x.shape[0]
    head_rows = lambda part: block(qkv_full, (HEAD_DIM, D), lambda h: (part * HEADS + h, 0))
    return (
        input_body,
        [
            block(grads, (1, tokens, 3 * HEAD_DIM), lambda h: (h, 0, 0)),
            head_rows(0),
            head_rows(1),
            head_rows(2),
            whole(x),
            whole(dh),
            whole(vec),
        ],
        [result((tokens, D), BF), result((8, D), F32)],
        [pltpu.VMEM((tokens, D), F32)],
        (0, 2, 6),
    )


def owner_place(owner):
    return owner // 16, (owner // 8) % 2, (owner // 4) % 2, owner % 4


def forward_body(
    t, tick, gathered, x, dy, qkv, mixed, lse, acts_one, residual, acts, hidden, slope, down_t, vec,
    small, qkv_w, up_w, out_w, bias, small_sem, qkv_sem, up_sem, out_sem,
):
    small_all, qkv_all, up_all, _ = gathered
    length = x.shape[0]
    owned = qkv_w.shape[4]
    up_rows = up_w.shape[2]
    out_rows = out_w.shape[4]

    def load_up(n):
        dst = up_w.at[n % 2]
        src = up_all.at[n // 4, (n // 2) % 2, n % 2, :, pl.ds(0, up_rows)]
        return pltpu.make_async_copy(src, dst, up_sem.at[n % 2])

    def load_out():
        return pltpu.make_async_copy(
            up_all.at[:, :, :, :, pl.ds(up_rows, out_rows)], out_w, out_sem
        )

    @pl.when(t == 0)
    def _():
        weights = pltpu.make_async_copy(qkv_all, qkv_w, qkv_sem)
        vectors = pltpu.make_async_copy(small_all, small, small_sem)
        weights.start()
        vectors.start()
        vectors.wait()
        for group in range(8):
            total = jnp.zeros((8, 128), F32)
            for z in range(4):
                part = small[group // 4, (group // 2) % 2, group % 2, z].astype(F32)
                total = total + part[:8, :]
                at = (group * 4 + z) * 128
                bias[:, at : at + 128] = part[8:9, :]
            vec[:, group * 128 : (group + 1) * 128] = total

        def norm(rows):
            normed = layer_norm(x[rows, :].astype(F32), vec[0:1, :], vec[1:2, :])[0]
            acts_one[rows, :] = normed.astype(BF)

        chunks(length, CHUNK, norm)
        weights.wait()

    @pl.when(t < HEADS)
    def _():
        unit = math.gcd(owned, HEAD_DIM)
        pieces = []
        for part in range(3):
            for i in range(HEAD_DIM // unit):
                index = (part * HEADS + t) * (HEAD_DIM // unit) + i
                per_owner = owned // unit
                row = pl.multiple_of((index % per_owner) * unit, unit)
                pieces.append(qkv_w[(*owner_place(index // per_owner), pl.ds(row, unit))])
        lanes = pl.ds(pl.multiple_of(t * HEAD_DIM, HEAD_DIM), HEAD_DIM)
        projected = dot_nt(acts_one[...], jnp.concatenate(pieces, axis=0))
        qkv[0] = (projected[:, :HEAD_DIM] + vec[2:3, lanes]).astype(BF)
        qkv[1] = projected[:, HEAD_DIM : 2 * HEAD_DIM].astype(BF)
        values = projected[:, 2 * HEAD_DIM :] + vec[3:4, lanes]
        qkv[2] = values.astype(BF)
        values_t = values.T.astype(BF)
        tick(1, 0, HEADS)
        level = head_slope(t)
        for start in range(0, length, QUERY_BLOCK):
            rows = start + QUERY_BLOCK
            scores = scores_t(qkv[0, start:rows, :], qkv[1, :rows, :], level, start, rows)
            highest = jnp.max(scores, axis=0, keepdims=True)
            weights = jnp.exp(scores - highest)
            totals = jnp.sum(weights, axis=0, keepdims=True)
            mix = dot_nn(values_t[:, :rows], weights.astype(BF)) / totals
            mixed[start:rows, lanes] = mix.T.astype(BF)
            lse[0, :, start:rows] = highest + jnp.log(totals)
            if rows < length:
                tick(2 + start // QUERY_BLOCK, 0, HEADS)

    @pl.when(t == HEADS)
    def _():
        load_out().start()
        load_up(0).start()
        load_out().wait()

        def enter(rows):
            attended = dot_nt(mixed[rows, :], flat(out_w)) + vec[4:5, :]
            here = x[rows, :].astype(F32) + attended
            residual[rows, :] = here
            acts[rows, :] = layer_norm(here, vec[5:6, :], vec[6:7, :])[0].astype(BF)

        chunks(length, 2 * CHUNK, enter)

    @pl.when(t >= HEADS)
    def _():
        n = t - HEADS
        load_up(n).wait()

        @pl.when(t < pl.num_programs(0) - 1)
        def _():
            load_up(n + 1).start()

        weights = up_w.at[n % 2]
        lanes = pl.ds(pl.multiple_of(n * UNITS, UNITS), UNITS)
        for start in range(0, length, 256):
            rows = slice(start, start + 256)
            pre = dot_nt(acts[rows, :], flat(weights)) + bias[:, lanes]
            value, steep = gelu_pair(pre)
            hidden[rows, :] = value.astype(BF)
            slope[rows, :] = steep.astype(BF)
            tick(1 + start // 256, HEADS)
        down_t[...] = dot_tn(hidden[...], dy[...]).astype(BF)


def forward(x, dy, small, qkv_w, up_set, down_set, units_rows, out_rows, collective_id):
    tokens = x.shape[0]
    units = 32 * units_rows
    steps = HEADS + units // UNITS
    head = lambda t: jnp.minimum(t, HEADS - 1)
    unit = lambda t: jnp.maximum(t - HEADS, 0)
    jobs = [Gather(small), Gather(qkv_w), Gather(up_set), Gather(down_set)]

    def timeline(ends):
        spans = [(ends[1] + 4 + 3.5 * i, 3.5) for i in range(HEADS)]
        start = max(ends[1] + 4 + 3.5 * HEADS, ends[2])
        return spans + [(start + 5 * (i > 0) + 4 * i, 4) for i in range(steps - HEADS)]

    column = result((tokens, units), BF, (tokens, UNITS), lambda t: (0, unit(t)))
    return fused_call(
        forward_body,
        steps,
        [whole(x), whole(dy)],
        [
            result((3, tokens, D), BF, (3, tokens, HEAD_DIM), lambda t: (0, 0, head(t))),
            result((tokens, D), BF),
            result((HEADS, 1, tokens), F32, (1, 1, tokens), lambda t: (head(t), 0, 0)),
            result((tokens, D), BF),
            result((tokens, D), F32),
            result((tokens, D), BF),
            column,
            column,
            result((units, D), BF, (UNITS, D), lambda t: (unit(t), 0)),
            result((8, D), F32),
        ],
        [
            pltpu.VMEM(jobs[0].shape.shape, BF),
            pltpu.VMEM(jobs[1].shape.shape, BF),
            pltpu.VMEM((2, 4, units_rows, D), BF),
            pltpu.VMEM((2, 2, 2, 4, out_rows, D), BF),
            pltpu.VMEM((1, units), F32),
            pltpu.SemaphoreType.DMA,
            pltpu.SemaphoreType.DMA,
            pltpu.SemaphoreType.DMA((2,)),
            pltpu.SemaphoreType.DMA,
        ],
        jobs,
        collective_id,
        ticks=5,
        stagger=36.0,
        needs={0: 0, 1: 0, 2: HEADS, 3: steps},
        timeline=timeline,
    )


def renew_body(
    t, tick, own, full, root, n_stat, m_stat, m_root, weight, new_n, new_m, new_w, left, product
):
    last = pl.num_programs(0) - 1
    me = lax.axis_index("dp") * lax.axis_size("ffn") + lax.axis_index("ffn")
    rows_owned = m_stat.shape[0]
    share = 128 // rows_owned
    lanes = pl.ds(pl.multiple_of((me // share) * 128, 128), 128)
    here = flat(full)
    new_n[...] = decay_rate * n_stat[...] + (1.0 - decay_rate) * dot_nt(own[...], here)
    left_part = dot_tn(full[:, :, lanes].reshape(-1, 128), here)
    product_part = dot_nn(root[...].astype(BF), here)

    @pl.when(t == 0)
    def _():
        left[...] = left_part
        product[...] = product_part

    @pl.when(t > 0)
    def _():
        left[...] += left_part
        product[...] += product_part

    @pl.when(t == last)
    def _():
        mine = left[pl.ds(pl.multiple_of((me % share) * rows_owned, rows_owned), rows_owned), :]
        new_m[...] = decay_rate * m_stat[...] + (1.0 - decay_rate) * mine
        step = dot_nt(product[...].astype(BF), flat(m_root))
        new_w[...] = weight[...] - matrix_rate * step


def renew(
    own, gathered, at, n_root, n_stat, m_stat, roots, root_at, weight, jobs, collective_id, part=None
):
    rows, total = own.shape[0], n_stat.shape[1]
    rows_owned = m_stat.shape[0]
    body, ins, outs, scratch, more = part or (None, [], [], [], (0, 0, 0))
    if not on_fast_grid():
        extra = fused_call(body, 8, ins, outs, scratch, [], collective_id)[0] if part else []
        full = gathered[:, at : at + rows].reshape(-1, D)
        m_root = roots[:, root_at : root_at + rows_owned].reshape(-1, D)
        me = lax.axis_index("dp") * lax.axis_size("ffn") + lax.axis_index("ffn")
        new_n = decay_rate * n_stat + (1.0 - decay_rate) * dot_nt(own, full)
        mine = lax.dynamic_slice_in_dim(full, me * rows_owned, rows_owned, 1)
        new_m = decay_rate * m_stat + (1.0 - decay_rate) * dot_tn(mine, full)
        product = dot_nn(n_root.astype(BF), full)
        new_w = weight - matrix_rate * dot_nt(product.astype(BF), m_root)
        return [new_n, new_m, new_w] + extra, [job.plainly() for job in jobs]
    owners = 16 if rows == 32 else 4
    size = owners * rows
    column = lambda array: block(array, (rows, size), lambda n: (0, n))
    own_ins = [
        whole(own),
        block(gathered, (owners, rows, D), lambda n: (n, at // rows, 0)),
        column(n_root),
        column(n_stat),
        whole(m_stat),
        rows_of(roots, root_at, rows_owned),
        whole(weight),
    ]
    own_outs = [
        result((rows, total), F32, (rows, size), lambda n: (0, n)),
        result((rows_owned, D), F32),
        result((rows, D), F32),
    ]
    own_scratch = [pltpu.VMEM((128, D), F32), pltpu.VMEM((rows, D), F32)]
    sizes = [len(own_ins), len(ins), len(own_outs), len(outs), len(own_scratch), len(scratch)]

    def both(t, tick, *refs):
        cuts = [sum(sizes[:i]) for i in range(len(sizes) + 1)]
        groups = [refs[i:j] for i, j in zip(cuts, cuts[1:])]
        renew_body(t, tick, *groups[0], *groups[2], *groups[4])
        if part:
            tick(1)
            body(t, tick, *groups[1], *groups[3], *groups[5])

    return fused_call(
        both,
        total // size,
        own_ins + ins,
        own_outs + outs,
        own_scratch + scratch,
        jobs,
        collective_id,
        ticks=2 if part else 1,
        cost=(0, 1.6 + more[1], 1 + more[2]),
        stagger=0.1 if len(jobs) > 2 else 36.0,
    )


SMALL_ROWS = 32
SMALL_WIDTH = 128


def pack_small(vector_part, bias_part):
    owners = vector_part.shape[0]
    flat = jnp.concatenate([vector_part.reshape(owners, -1), bias_part.reshape(owners, -1)], axis=1)
    room = SMALL_ROWS * SMALL_WIDTH
    flat = jnp.pad(flat, ((0, 0), (0, room - flat.shape[1])))
    return flat.reshape(owners * SMALL_ROWS, SMALL_WIDTH)


def unpack_small(packed, columns, units):
    owners = packed.shape[0] // SMALL_ROWS
    flat = packed.reshape(owners, -1)
    vector_part = flat[:, : 8 * columns].reshape(owners, 8, columns)
    bias_part = flat[:, 8 * columns : 8 * columns + units]
    return vector_part, bias_part


def shards(
    block_input,
    cotangent,
    w_qkv,
    w_out,
    w_up,
    w_down,
    vectors,
    b_up,
    qkv_left,
    qkv_right,
    out_left,
    out_right,
    up_left,
    up_right,
    down_left,
    down_right,
    qkv_left_root,
    qkv_right_root,
    out_left_root,
    out_right_root,
    up_left_root,
    up_right_root,
    down_left_root,
    down_right_root,
    vector_stat,
    b_up_stat,
):
    owners = lax.axis_size("dp") * lax.axis_size("ffn")
    columns = vectors.shape[1]
    units = b_up.shape[0]
    qkv_w, out_w, up_w = w_qkv.T, w_out.T, w_up.T
    units_rows, qkv_rows, out_rows = units, qkv_w.shape[0], out_w.shape[0]
    root_rows = qkv_left_root.shape[0]

    def stack(*items):
        return Gather(jnp.concatenate([item.astype(BF) for item in items], axis=0))

    def by_owner(array):
        return array.reshape(owners, -1, D)

    up_block = [up_w, out_w]
    down_block = [w_down, out_left_root, qkv_left_root]
    if on_fast_grid():
        lane = (lax.axis_index("ffn") * columns).astype(jnp.int32)
        small = jnp.zeros((SMALL_ROWS, SMALL_WIDTH), BF)
        small = lax.dynamic_update_slice(small, vectors.astype(BF), (0, lane))
        small = lax.dynamic_update_slice(small, b_up.astype(BF)[None], (8, 0))
        results, gathered = forward(
            block_input,
            cotangent,
            small,
            qkv_w.astype(BF),
            stack(*up_block).array,
            stack(*down_block).array,
            units_rows,
            out_rows,
            1,
        )
        qkv, mixed, logsum, acts_one, residual, acts_two, hidden, slope, down_t, vector_rows = results
        _, qkv_full, up_set, down_set = gathered
        up_set, down_set = by_owner(up_set), by_owner(down_set)
    else:
        small = pack_small(vectors[None], b_up[None]).astype(BF)
        small_full, qkv_full = transfer([Gather(small), Gather(qkv_w.astype(BF))], 1)
        vector_low, bias_low = unpack_small(small_full, columns, units)
        vector_rows = vector_low.transpose(1, 0, 2).reshape(8, D).astype(F32)
        up_bias = bias_low.reshape(1, -1).astype(F32)
        (qkv, mixed, logsum, acts_one), (up_set,) = attend(
            block_input, vector_rows, qkv_full, [stack(*up_block)], 2
        )
        up_set = by_owner(up_set)
        (residual, acts_two, hidden, slope, down_t), (down_set,) = hidden_forward(
            block_input,
            mixed,
            up_set,
            (units_rows, out_rows),
            vector_rows,
            cotangent,
            up_bias,
            [stack(*down_block)],
            3,
        )
        down_set = by_owner(down_set)
    (up_t, bias_grad, dh, dh_low, sums), (down_g, down_mroot) = hidden_backward(
        cotangent,
        acts_two,
        residual,
        slope,
        down_set,
        up_set,
        units_rows,
        vector_rows,
        [Reduce(down_t), stack(down_right_root)],
        4,
    )
    down_low = down_g.astype(BF)
    (out_t, qkv_t, qkv_grads, sums), (up_g, down_all) = attend_backward(
        dh_low,
        up_set,
        (units_rows, out_rows),
        mixed,
        acts_one,
        qkv,
        logsum,
        sums,
        [Reduce(up_t), Gather(down_low)],
        5,
    )
    up_low = up_g.astype(BF)
    (new_down_n, new_down_m, new_w_down, input_grad, first_sums), (up_all, qkv_g, out_g) = renew(
        down_low,
        by_owner(down_all),
        0,
        down_left_root,
        down_left,
        down_right,
        by_owner(down_mroot),
        0,
        w_down,
        [stack(up_low, up_left_root), Reduce(qkv_t.reshape(-1, D)), Reduce(out_t)],
        6,
        input_part(qkv_grads, qkv_full, block_input, dh, vector_rows),
    )
    small_part = pack_small(
        (sums + first_sums).reshape(8, owners, columns).transpose(1, 0, 2),
        bias_grad.reshape(owners, units),
    ).astype(BF)
    qkv_low, out_low = qkv_g.astype(BF), out_g.astype(BF)
    up_all = by_owner(up_all)
    (new_up_n, new_up_m, new_w_up, block_output), (last_all, small_g) = renew(
        up_low,
        up_all,
        0,
        up_right_root,
        up_right,
        up_left,
        up_all,
        units_rows,
        up_w,
        [stack(qkv_low, out_low), Reduce(small_part)],
        7,
        output_part(hidden, down_set, units_rows, residual, vector_rows),
    )
    last_all = by_owner(last_all)
    new_qkv_n, new_qkv_m, new_w_qkv = renew(
        qkv_low,
        last_all,
        0,
        qkv_right_root,
        qkv_right,
        qkv_left,
        down_set,
        units_rows + root_rows,
        qkv_w,
        [],
        8,
    )[0]
    new_out_n, new_out_m, new_w_out = renew(
        out_low,
        last_all,
        qkv_rows,
        out_right_root,
        out_right,
        out_left,
        down_set,
        units_rows,
        out_w,
        [],
        8,
    )[0]
    new_m = [new_qkv_m, new_out_m, new_up_m, new_down_m]
    new_n = [new_qkv_n, new_out_n, new_up_n, new_down_n]
    new_w_qkv, new_w_out, new_w_up = new_w_qkv.T, new_w_out.T, new_w_up.T
    grads = [qkv_g, out_g, up_g, down_g]
    vector_grad, b_up_grad = unpack_small(small_g, columns, units)
    vector_grad, b_up_grad = vector_grad[0], b_up_grad[0]
    new_vector_stat = decay_rate * vector_stat + (1.0 - decay_rate) * vector_grad * vector_grad
    new_vectors = vectors - vector_rate * vector_grad * lax.rsqrt(new_vector_stat)
    new_b_up_stat = decay_rate * b_up_stat + (1.0 - decay_rate) * b_up_grad * b_up_grad
    new_b_up = b_up - vector_rate * b_up_grad * lax.rsqrt(new_b_up_stat)
    return (
        block_output,
        input_grad,
        grads[0].T,
        grads[1].T,
        grads[2].T,
        grads[3],
        vector_grad,
        b_up_grad,
        new_m[0],
        new_n[0],
        new_m[1],
        new_n[1],
        new_m[2],
        new_n[2],
        new_n[3],
        new_m[3],
        new_vector_stat,
        new_b_up_stat,
        new_w_qkv,
        new_w_out,
        new_w_up,
        new_w_down,
        new_vectors,
        new_b_up,
    )


def solution(mesh):
    return jax.shard_map(
        shards,
        mesh=mesh,
        in_specs=(
            P(("dp", "ffn"), None),
            P(("dp", "ffn"), None),
            P(None, ("dp", "ffn")),
            P(None, ("dp", "ffn")),
            P(None, ("dp", "ffn")),
            P(("dp", "ffn"), None),
            P(None, ("dp", "ffn")),
            P(("dp", "ffn")),
            P(("dp", "ffn"), None),
            P(("dp", "ffn"), None),
            P(("dp", "ffn"), None),
            P(("dp", "ffn"), None),
            P(("dp", "ffn"), None),
            P(("dp", "ffn"), None),
            P(("dp", "ffn"), None),
            P(("dp", "ffn"), None),
            P(("dp", "ffn"), None),
            P(("dp", "ffn"), None),
            P(("dp", "ffn"), None),
            P(("dp", "ffn"), None),
            P(("dp", "ffn"), None),
            P(("dp", "ffn"), None),
            P(("dp", "ffn"), None),
            P(("dp", "ffn"), None),
            P(None, ("dp", "ffn")),
            P(("dp", "ffn")),
        ),
        out_specs=(
            P(("dp", "ffn"), None),
            P(("dp", "ffn"), None),
            P(None, ("dp", "ffn")),
            P(None, ("dp", "ffn")),
            P(None, ("dp", "ffn")),
            P(("dp", "ffn"), None),
            P(None, ("dp", "ffn")),
            P(("dp", "ffn")),
            P(("dp", "ffn"), None),
            P(("dp", "ffn"), None),
            P(("dp", "ffn"), None),
            P(("dp", "ffn"), None),
            P(("dp", "ffn"), None),
            P(("dp", "ffn"), None),
            P(("dp", "ffn"), None),
            P(("dp", "ffn"), None),
            P(None, ("dp", "ffn")),
            P(("dp", "ffn")),
            P(None, ("dp", "ffn")),
            P(None, ("dp", "ffn")),
            P(None, ("dp", "ffn")),
            P(("dp", "ffn"), None),
            P(None, ("dp", "ffn")),
            P(("dp", "ffn")),
        ),
        check_vma=False,
    )
```

```python
import functools
import math

import jax
import jax.numpy as jnp
from jax import lax
from jax.experimental import pallas as pl
from jax.experimental.pallas import tpu as pltpu
from jax.sharding import PartitionSpec as P

D = 1024
HEADS = 8
HEAD_DIM = 128
MESH = pl.DeviceIdType.MESH
ALL = ("dp", "ffn")
BF = jnp.bfloat16
F32 = jnp.float32
MIB = 2**20

norm_epsilon = 1e-05
decay_rate = 0.5
matrix_rate = 0.5
vector_rate = 0.1
masked_score = -1e30


def layer_norm(values, gain, shift):
    center = values - jnp.mean(values, axis=-1, keepdims=True)
    inverse = lax.rsqrt(jnp.mean(center * center, axis=-1, keepdims=True) + norm_epsilon)
    normed = center * inverse
    return (normed * gain + shift, normed, inverse)


def norm_backward(grad, normed, inverse, gain):
    scaled = grad * gain
    inner = (
        scaled
        - jnp.mean(scaled, axis=-1, keepdims=True)
        - normed * jnp.mean(scaled * normed, axis=-1, keepdims=True)
    )
    return (inner * inverse, jnp.sum(grad * normed, axis=0), jnp.sum(grad, axis=0))


def dot_nt(left, right):
    return lax.dot_general(left, right, (((1,), (1,)), ((), ())), preferred_element_type=F32)


def dot_tn(left, right):
    return lax.dot_general(left, right, (((0,), (0,)), ((), ())), preferred_element_type=F32)


def dot_nn(left, right):
    return jnp.dot(left, right, preferred_element_type=F32)


def flip(value, mask):
    result = value
    bit = 1
    while bit <= mask:
        if mask & bit:
            result = result + bit - 2 * bit * ((result // bit) % 2)
        bit *= 2
    return result


class Copies:
    def __init__(self, send, recv):
        self.send, self.recv, self.made = send, recv, {}

    def copy(self, name):
        at, make = self.made[name]
        src, dst, device = make()
        return pltpu.make_async_remote_copy(
            src, dst, self.send.at[at], self.recv.at[at], device_id=device, device_id_type=MESH
        )

    def plan(self, name, make):
        self.made[name] = (len(self.made), make)

    def post(self, name):
        self.copy(name).start()

    def got(self, name):
        self.copy(name).wait_recv()

    def sent(self):
        for name in self.made:
            self.copy(name).wait_send()


class Place:
    def __init__(self):
        dp = lax.axis_index("dp")
        self.y, self.x, self.c, self.z = dp // 4, (dp // 2) % 2, dp % 2, lax.axis_index("ffn")

    def device(self, y=0, x=0, c=0, z=0):
        dp = (flip(self.y, y) * 2 + flip(self.x, x)) * 2 + flip(self.c, c)
        return dp, flip(self.z, z)

    def span(self, group):
        if len(group) == 1:
            return pl.ds(flip(self.z, group[0]), 1)
        if len(group) == 2:
            return pl.ds(flip(self.z // 2, group[0] // 2) * 2, 2)
        return pl.ds(0, 4)


def greet(place):
    barrier = pltpu.get_barrier_semaphore()
    steps = [dict(y=1), dict(x=1), dict(c=1), dict(z=1), dict(z=2), dict(z=3)]
    for step in steps:
        pl.semaphore_signal(
            barrier, inc=1, device_id=place.device(**step), device_id_type=MESH
        )
    pl.semaphore_wait(barrier, len(steps))


def one(index):
    return pl.ds(index, 1)


TURNS = (("x", "y"), ("y", "x"))


def gather_plan(place, shard, out, send, recv, local_sem):
    y, x, c, z = place.y, place.x, place.c, place.z
    half_rows = shard.shape[0] // 2
    copies = Copies(send, recv)

    def half(ref, h):
        return ref.at[pl.ds(h * half_rows, half_rows)]

    def local():
        return pltpu.make_async_copy(shard, out.at[y, x, c, z], local_sem)

    def along_z(k):
        return shard, out.at[y, x, c, z], place.device(z=k)

    def own(turn, k, h):
        dst = half(out.at[y, x, c, flip(z, k)], h)
        return (dst if k else half(shard, h)), dst, place.device(**{TURNS[h][turn]: 1})

    def relay(k, h):
        block = out.at[y, 1 - x, c, flip(z, k)] if h == 0 else out.at[1 - y, x, c, flip(z, k)]
        return half(block, h), half(block, h), place.device(**{TURNS[h][1]: 1})

    def across(k):
        piece = out.at[:, :, c, flip(z, k)]
        return piece, piece, place.device(c=1)

    do = functools.partial
    for k in range(4):
        if k:
            copies.plan(("z", k), do(along_z, k))
        for h in (0, 1):
            copies.plan(("first", k, h), do(own, 0, k, h))
            copies.plan(("second", k, h), do(own, 1, k, h))
            copies.plan(("relay", k, h), do(relay, k, h))
        copies.plan(("core", k), do(across, k))

    def spread(k):
        for name in ("first", "second"):
            for h in (0, 1):
                copies.post((name, k, h))

    def begin():
        copies.post(("z", 1))
        spread(0)
        local().start()

    def landed(k):
        copies.got(("z", k))
        if k < 3:
            copies.post(("z", k + 1))
        spread(k)

    def forward(k):
        for h in (0, 1):
            copies.got(("first", k, h))
            copies.post(("relay", k, h))

    def share(k):
        for h in (0, 1):
            copies.got(("second", k, h))
            copies.got(("relay", k, h))
        if k == 0:
            local().wait()
        copies.post(("core", k))

    def finish():
        for k in range(4):
            copies.got(("core", k))
        copies.sent()

    return [
        (0, 0, begin),
        (4, 1, do(forward, 0)),
        (6, 1, do(landed, 1)),
        (13, 2, do(share, 0)),
        (14, 2, do(forward, 1)),
        (18, 2, do(landed, 2)),
        (20, 3, do(share, 1)),
        (24, 3, do(forward, 2)),
        (30, 2, do(landed, 3)),
        (31, 3, do(share, 2)),
        (35, 3, do(forward, 3)),
        (39, 3, do(share, 3)),
        (40, 4, finish),
    ]


def gather_small_plan(place, shard, out, send, recv, local_sem):
    y, x, c, z = place.y, place.x, place.c, place.z
    rows = shard.shape[0]
    copies = Copies(send, recv)

    def half(h):
        return pl.ds(h * (rows // 2), rows // 2)

    def local():
        return pltpu.make_async_copy(shard, out.at[y, x, c, z], local_sem)

    def along_z(k):
        return shard, out.at[y, x, c, z], place.device(z=k)

    def first(h):
        piece = out.at[y, x, c, :, half(h)]
        return piece, piece, place.device(**{TURNS[h][0]: 1})

    def second(h):
        piece = out.at[y, :, c, :, half(h)] if h == 0 else out.at[:, x, c, :, half(h)]
        return piece, piece, place.device(**{TURNS[h][1]: 1})

    def across():
        piece = out.at[:, :, c]
        return piece, piece, place.device(c=1)

    do = functools.partial
    for k in (1, 2, 3):
        copies.plan(("z", k), do(along_z, k))
    for h in (0, 1):
        copies.plan(("first", h), do(first, h))
        copies.plan(("second", h), do(second, h))
    copies.plan("core", across)

    def begin():
        local().start()
        for k in (1, 2, 3):
            copies.post(("z", k))

    def start_first():
        for k in (1, 2, 3):
            copies.got(("z", k))
        local().wait()
        for h in (0, 1):
            copies.post(("first", h))

    def start_second():
        for h in (0, 1):
            copies.got(("first", h))
            copies.post(("second", h))

    def share():
        for h in (0, 1):
            copies.got(("second", h))
        copies.post("core")

    def finish():
        copies.got("core")
        copies.sent()

    return [
        (0, 0, begin),
        (24, 1, start_first),
        (36, 2, start_second),
        (60, 3, share),
        (62, 4, finish),
    ]


def gather_z_last_plan(place, shard, out, send, recv, local_sem):
    y, x, c, z = place.y, place.x, place.c, place.z
    rows = shard.shape[0]
    copies = Copies(send, recv)

    def half(h):
        return pl.ds(h * (rows // 2), rows // 2)

    def local():
        return pltpu.make_async_copy(shard, out.at[y, x, c, z], local_sem)

    def first(h):
        return shard.at[half(h)], out.at[y, x, c, z, half(h)], place.device(**{TURNS[h][0]: 1})

    def second(h):
        piece = out.at[y, :, c, z, half(h)] if h == 0 else out.at[:, x, c, z, half(h)]
        return piece, piece, place.device(**{TURNS[h][1]: 1})

    def along_z(k):
        piece = out.at[:, :, c, z]
        return piece, piece, place.device(z=k)

    def across():
        piece = out.at[:, :, c]
        return piece, piece, place.device(c=1)

    do = functools.partial
    for h in (0, 1):
        copies.plan(("first", h), do(first, h))
        copies.plan(("second", h), do(second, h))
    for k in (1, 2, 3):
        copies.plan(("z", k), do(along_z, k))
    copies.plan("core", across)

    def begin():
        local().start()
        for h in (0, 1):
            copies.post(("first", h))

    def start_second():
        local().wait()
        for h in (0, 1):
            copies.got(("first", h))
            copies.post(("second", h))

    def column():
        for h in (0, 1):
            copies.got(("second", h))
        for k in (1, 2, 3):
            copies.post(("z", k))

    def share():
        for k in (1, 2, 3):
            copies.got(("z", k))
        copies.post("core")

    def finish():
        copies.got("core")
        copies.sent()

    return [(0, 0, begin), (3, 1, start_second), (9, 2, column), (93, 3, share), (100, 4, finish)]


def reduce_plan(
    place, parts, out, held, from_core, from_second, from_first, from_z, send, recv, load
):
    y, x, c, z = place.y, place.x, place.c, place.z
    rows = parts.shape[-2]
    whole_first = rows < 64
    groups = [(0, 1, 2, 3)] if whole_first else [(3,), (2,), (1,), (0,)]
    copies = Copies(send, recv)

    def half(h):
        return pl.ds(h * (rows // 2), rows // 2)

    def local(group):
        span = place.span(group)
        return pltpu.make_async_copy(
            parts.at[:, :, c, span], held.at[:, :, span], load.at[groups.index(group)]
        )

    def core_route(group):
        span = place.span(group)
        return parts.at[:, :, 1 - c, span], from_core.at[:, :, span], place.device(c=1)

    def second_part(group, h, other):
        at = (1 - y if other else y) if h == 0 else (1 - x if other else x)
        if h == 0:
            return (at, slice(None), place.span(group), half(h))
        return (slice(None), at, place.span(group), half(h))

    def second_route(group, h):
        return (
            held.at[second_part(group, h, True)],
            from_second.at[h, :, place.span(group)],
            place.device(**{TURNS[h][1]: 1}),
        )

    def first_part(group, h):
        return (y, 1 - x, place.span(group), half(h)) if h == 0 else (1 - y, x, place.span(group), half(h))

    def first_route(group, h):
        return (
            held.at[first_part(group, h)],
            from_first.at[h, place.span(group)],
            place.device(**{TURNS[h][0]: 1}),
        )

    def z_route(k):
        return held.at[y, x, flip(z, k)], from_z.at[k - 1], place.device(z=k)

    do = functools.partial
    for group in groups:
        copies.plan(("core", group), do(core_route, group))
        for h in (0, 1):
            copies.plan(("second", group, h), do(second_route, group, h))
            copies.plan(("first", group, h), do(first_route, group, h))
        for k in group:
            if k:
                copies.plan(("z", k), do(z_route, k))

    def add(dst, *sources):
        if len(sources) == 1:
            dst[...] += sources[0][...]
            return
        total = dst[...].astype(F32)
        for source in sources:
            total = total + source[...].astype(F32)
        dst[...] = total.astype(BF)

    def to_core(group):
        copies.post(("core", group))
        local(group).start()

    def begin():
        to_core(groups[0])

    def cores(group):
        local(group).wait()
        copies.got(("core", group))
        at = groups.index(group)
        if at + 1 < len(groups):
            to_core(groups[at + 1])
        for other in (True, False):
            for h in (0, 1):
                part = second_part(group, h, other)
                add(held.at[part], from_core.at[part])
                if other:
                    copies.post(("second", group, h))

    def second(group):
        span = place.span(group)
        for h in (0, 1):
            copies.got(("second", group, h))
            away = 1 - x if h == 0 else 1 - y
            add(held.at[first_part(group, h)], from_second.at[h, away, span])
            copies.post(("first", group, h))

    def first(group):
        span = place.span(group)
        for h in (0, 1):
            copies.got(("first", group, h))
            mine = x if h == 0 else y
            add(held.at[y, x, span, half(h)], from_second.at[h, mine, span], from_first.at[h, span])
        for k in group:
            if k:
                copies.post(("z", k))

    def finish():
        for k in (1, 2, 3):
            copies.got(("z", k))
        total = held[y, x, z].astype(F32)
        for k in range(3):
            total = total + from_z[k].astype(F32)
        out[...] = total
        copies.sent()

    if whole_first:
        (group,) = groups
        return [
            (0, 0, begin),
            (7, 1, do(cores, group)),
            (31, 2, do(second, group)),
            (43, 3, do(first, group)),
            (67, 4, finish),
        ]
    a, b, d, e = groups
    return [
        (0, 0, begin),
        (2, 1, do(cores, a)),
        (4, 1.2, do(cores, b)),
        (6, 2, do(second, a)),
        (8, 2, do(cores, d)),
        (12, 3, do(first, a)),
        (15, 2, do(second, b)),
        (17, 2, do(cores, e)),
        (20, 3, do(first, b)),
        (24, 2, do(second, d)),
        (29, 3, do(first, d)),
        (33, 2, do(second, e)),
        (38, 3, do(first, e)),
        (42, 4, finish),
    ]


HOP_US = 2.0
FULL_BLOCK = 128 * 1024


def merge_plans(jobs, plans, stagger):
    timed = []
    start = 0.0
    for g, (job, plan) in enumerate(zip(jobs, plans)):
        size = job.rows * job.width / FULL_BLOCK
        own = 0.0 if job.beside else start
        at = 0.0
        for i, (volume, hops, step) in enumerate(plan):
            ahead = 0.0 if i else min(own, 20.0 * size)
            at = max(at, own - ahead + volume * size + hops * HOP_US)
            timed.append((at, g, i, step))
        if not job.beside:
            start += stagger * size
        else:
            start += 9.0 * size
    timed.sort(key=lambda item: item[:3])
    return [(at, step, g, i == len(plans[g]) - 1) for at, g, i, step in timed]


ANYWHERE = pl.BlockSpec(memory_space=pl.ANY)
COPIES = 31


class Gather:
    def __init__(self, shard, z_last=False):
        self.array = shard
        self.rows, self.width = shard.shape
        self.shape = jax.ShapeDtypeStruct((2, 2, 2, 4, self.rows, self.width), BF)
        self.spec = ANYWHERE
        sems = pltpu.SemaphoreType.DMA((COPIES,))
        self.scratch = [sems, sems, pltpu.SemaphoreType.DMA]
        self.beside = z_last
        self.plan = gather_plan if self.rows >= 64 else gather_small_plan
        if z_last:
            self.plan = gather_z_last_plan

    def finish(self, out):
        return out.reshape(-1, self.width)

    def plainly(self):
        return lax.all_gather(self.array, ALL, axis=0, tiled=True)


class Reduce:
    def __init__(self, parts):
        devices = lax.axis_size("dp") * lax.axis_size("ffn")
        self.parts = parts
        self.rows, width = parts.shape[0] // devices, parts.shape[1]
        self.width, self.beside = width, False
        self.shape = jax.ShapeDtypeStruct((self.rows, width), F32)
        self.spec = pl.BlockSpec((self.rows, width), lambda *_: (0, 0))
        sems = pltpu.SemaphoreType.DMA((COPIES,))
        rows = self.rows
        self.scratch = [
            pltpu.VMEM((2, 2, 4, rows, width), BF),
            pltpu.VMEM((2, 2, 4, rows, width), BF),
            pltpu.VMEM((2, 2, 4, rows // 2, width), BF),
            pltpu.VMEM((2, 4, rows // 2, width), BF),
            pltpu.VMEM((3, rows, width), BF),
            sems,
            sems,
            pltpu.SemaphoreType.DMA((4,)),
        ]
        self.plan = reduce_plan

    @property
    def array(self):
        return self.parts.reshape(2, 2, 2, 4, self.rows, self.parts.shape[1])

    def finish(self, out):
        return out

    def plainly(self):
        return lax.psum_scatter(self.parts, ALL, scatter_dimension=0, tiled=True).astype(F32)


def on_fast_grid():
    return lax.axis_size("dp") == 8 and lax.axis_size("ffn") == 4


def fused_call(
    body,
    steps,
    ins,
    outs,
    scratch,
    jobs,
    collective_id,
    ticks=1,
    cost=(0, 1, 0),
    stagger=28.0,
    needs=None,
    timeline=None,
):
    plainly = not (on_fast_grid() and all(job.rows % 32 == 0 for job in jobs))
    run = [] if plainly else jobs
    held = [i for i, item in enumerate(ins) if item[1] is None]
    counts = [len(ins), len(run), len(outs), len(run), len(scratch), len(held), len(held)]

    def kernel(*refs):
        groups = []
        at = 0
        for count in counts:
            groups.append(refs[at : at + count])
            at += count
        own_in, job_in, own_out, job_out, own_scratch, buffers, arrived = groups
        own_in = list(own_in)
        loads = []
        for i, buffer, sem in zip(held, buffers, arrived):
            loads.append((own_in[i], buffer, sem))
            own_in[i] = buffer
        t = pl.program_id(0)
        if loads:

            @pl.when(t == 0)
            def _():
                for load in loads:
                    pltpu.make_async_copy(*load).start()

        here = {}
        rest = []
        if run:
            place = Place()
            plans = []
            for job, src, dst in zip(run, job_in, job_out):
                plans.append(job.plan(place, src, dst, *refs[at : at + len(job.scratch)]))
                at += len(job.scratch)
            merged = merge_plans(run, plans, stagger)
            before, each_step, after = cost
            pace = min(1.0, (before + each_step * steps + after) / merged[-1][0])
            spans = [(before * (i > 0) + each_step * i, each_step) for i in range(steps)]
            if timeline:
                pace = 1.0
                spans = timeline({g: when for when, _, g, is_last in merged if is_last})
            clocks = [0.0]
            for start, length in spans:
                clocks += [start + length * j / ticks for j in range(ticks)]
            clocks = [0.0] + clocks[2:]
            limits = [(needs or {}).get(g, steps) * ticks if is_last else steps * ticks for _, _, g, is_last in merged]
            position = 0
            for i, (when, step, _, _) in enumerate(merged):
                while position < steps * ticks and clocks[position] < when * pace:
                    position += 1
                position = min([position] + limits[i:])
                if position < steps * ticks:
                    here.setdefault(position, []).append(step)
                else:
                    rest.append(step)
            here.setdefault(0, []).insert(0, functools.partial(greet, place))

        def tick(j, least=0, most=steps):
            for position in sorted(here):
                if position % ticks == j and least <= position // ticks < most:

                    @pl.when(t == position // ticks)
                    def _(now=here[position]):
                        for each in now:
                            each()

        tick(0)
        if loads:

            @pl.when(t == 0)
            def _():
                for load in loads:
                    pltpu.make_async_copy(*load).wait()

        if body is not None:
            shared = [job_out] if needs else []
            body(t, tick, *shared, *own_in, *own_out, *own_scratch)
        if rest:

            @pl.when(t == steps - 1)
            def _():
                for each in rest:
                    each()

    all_scratch = list(scratch)
    all_scratch += [pltpu.VMEM(ins[i][0].shape, ins[i][0].dtype) for i in held]
    all_scratch += [pltpu.SemaphoreType.DMA] * len(held)
    for job in run:
        all_scratch += job.scratch
    extra = dict(collective_id=collective_id, has_side_effects=True) if run else {}
    results = pl.pallas_call(
        kernel,
        grid=(steps,),
        out_shape=tuple(o[0] for o in outs) + tuple(job.shape for job in run),
        in_specs=[i[1] or ANYWHERE for i in ins] + [ANYWHERE] * len(run),
        out_specs=tuple(o[1] for o in outs) + tuple(job.spec for job in run),
        scratch_shapes=all_scratch,
        compiler_params=pltpu.CompilerParams(vmem_limit_bytes=60 * MIB, **extra),
    )(*[i[0] for i in ins], *[job.array for job in run])
    own = list(results[: len(outs)])
    if plainly:
        return own, [job.plainly() for job in jobs]
    return own, [job.finish(out) for job, out in zip(jobs, results[len(outs) :])]


def transfer(jobs, collective_id):
    if not (on_fast_grid() and all(job.rows % 32 == 0 for job in jobs)):
        return [job.plainly() for job in jobs]
    return fused_call(None, 1, [], [], [], jobs, collective_id)[1]


def whole(array):
    return array, None


def rows_of(array, first, count):
    if on_fast_grid() and count % 16 == 0 and first % count == 0:
        shape = (array.shape[0], count, D)
        at = first // count
        return array, pl.BlockSpec(shape, lambda t: (0, at, 0), pipeline_mode=pl.Buffered(1))
    return whole(array[:, first : first + count].reshape(-1, D))


def unit_rows(array, count, total):
    return array, pl.BlockSpec((total // count, count, D), lambda n: (n, 0, 0))


def flat(ref):
    return ref[...].reshape(-1, D)


def block(array, shape, at):
    return array, pl.BlockSpec(shape, at)


def result(shape, dtype, tile=None, at=None):
    rank = len(shape)
    if tile is None:
        return jax.ShapeDtypeStruct(shape, dtype), pl.BlockSpec(shape, lambda t: (0,) * rank)
    return jax.ShapeDtypeStruct(shape, dtype), pl.BlockSpec(tile, at)


def chunks(rows, size, body):
    @pl.loop(0, rows // size)
    def _(i):
        body(pl.ds(pl.multiple_of(i * size, size), size))


QUERY_BLOCK = 256
CHUNK = 128
UNITS = 512


def head_slope(head):
    level = head.astype(F32) + 1.0
    return jnp.exp2(jnp.full((1, 1), -8.0 / HEADS, F32) * level)


def scores_t(query, keys, slope, start, rows):
    at_key = lax.broadcasted_iota(jnp.int32, (rows, 1), 0).astype(F32)
    scores = dot_nt(keys, query) * HEAD_DIM ** (-0.5) + at_key * slope
    at_key = lax.broadcasted_iota(jnp.int32, (rows, QUERY_BLOCK), 0)
    at_query = lax.broadcasted_iota(jnp.int32, (rows, QUERY_BLOCK), 1) + start
    return jnp.where(at_key <= at_query, scores, masked_score)


def attend_body(t, tick, x, vec, wq, wk, wv, head_vec, qkv, mixed, lse, acts):
    length = x.shape[0]

    @pl.when(t == 0)
    def _():
        def norm(rows):
            normed = layer_norm(x[rows, :].astype(F32), vec[0:1, :], vec[1:2, :])[0]
            acts[rows, :] = normed.astype(BF)

        chunks(length, CHUNK, norm)

    weights = jnp.concatenate([wq[...], wk[...], wv[...]], axis=0)
    projected = dot_nt(acts[...], weights)
    qkv[0] = (projected[:, :HEAD_DIM] + head_vec[2:3, :]).astype(BF)
    qkv[1] = projected[:, HEAD_DIM : 2 * HEAD_DIM].astype(BF)
    values = projected[:, 2 * HEAD_DIM :] + head_vec[3:4, :]
    qkv[2] = values.astype(BF)
    values_t = values.T.astype(BF)
    tick(1)
    slope = head_slope(t)
    for start in range(0, length, QUERY_BLOCK):
        rows = start + QUERY_BLOCK
        scores = scores_t(qkv[0, start:rows, :], qkv[1, :rows, :], slope, start, rows)
        highest = jnp.max(scores, axis=0, keepdims=True)
        weights = jnp.exp(scores - highest)
        totals = jnp.sum(weights, axis=0, keepdims=True)
        mix = dot_nn(values_t[:, :rows], weights.astype(BF)) / totals
        mixed[start:rows, :] = mix.T.astype(BF)
        lse[0, :, start:rows] = highest + jnp.log(totals)
        if rows < length:
            tick(2 + start // QUERY_BLOCK)


def attend(x, vec, qkv_full, jobs, collective_id):
    tokens = x.shape[0]
    head_rows = lambda part: block(
        qkv_full, (HEAD_DIM, D), lambda h: (part * HEADS + h, 0)
    )
    return fused_call(
        attend_body,
        HEADS,
        [
            whole(x),
            whole(vec),
            head_rows(0),
            head_rows(1),
            head_rows(2),
            block(vec, (8, HEAD_DIM), lambda h: (0, h)),
        ],
        [
            result((3, tokens, D), BF, (3, tokens, HEAD_DIM), lambda h: (0, 0, h)),
            result((tokens, D), BF, (tokens, HEAD_DIM), lambda h: (0, h)),
            result((HEADS, 1, tokens), F32, (1, 1, tokens), lambda h: (h, 0, 0)),
            result((tokens, D), BF),
        ],
        [],
        jobs,
        collective_id,
        ticks=5,
        cost=(3, 3.4, 0),
    )


def gelu_pair(pre):
    half = 0.5 * (1.0 + lax.erf(pre * 0.7071067811865476))
    slope = half + pre * jnp.exp(-0.5 * pre * pre) * 0.3989422804014327
    return pre * half, slope


def hidden_body(t, tick, x, mixed, out_w, vec, dy, up, bias, residual, acts, hidden, slope, down_t):
    tokens = x.shape[0]

    @pl.when(t == 0)
    def _():
        def enter(rows):
            attended = dot_nt(mixed[rows, :], flat(out_w)) + vec[4:5, :]
            here = x[rows, :].astype(F32) + attended
            residual[rows, :] = here
            acts[rows, :] = layer_norm(here, vec[5:6, :], vec[6:7, :])[0].astype(BF)

        chunks(tokens, 2 * CHUNK, enter)

    for start in range(0, tokens, 256):
        rows = slice(start, start + 256)
        pre = dot_nt(acts[rows, :], flat(up)) + bias[...]
        value, steep = gelu_pair(pre)
        hidden[rows, :] = value.astype(BF)
        slope[rows, :] = steep.astype(BF)
        tick(1 + start // 256)
    down_t[...] = dot_tn(hidden[...], dy[...]).astype(BF)


def hidden_forward(x, mixed, weights, widths, vec, dy, bias, jobs, collective_id):
    tokens = x.shape[0]
    units = bias.shape[1]
    up_rows, out_rows = widths
    return fused_call(
        hidden_body,
        units // UNITS,
        [
            whole(x),
            whole(mixed),
            rows_of(weights, up_rows, out_rows),
            whole(vec),
            whole(dy),
            unit_rows(weights, up_rows, UNITS),
            block(bias, (1, UNITS), lambda n: (0, n)),
        ],
        [
            result((tokens, D), F32),
            result((tokens, D), BF),
            result((tokens, units), BF, (tokens, UNITS), lambda n: (0, n)),
            result((tokens, units), BF, (tokens, UNITS), lambda n: (0, n)),
            result((units, D), BF, (UNITS, D), lambda n: (n, 0)),
        ],
        [],
        jobs,
        collective_id,
        ticks=5,
        cost=(5, 4, 0),
    )


def accumulate(t, into, value):
    @pl.when(t == 0)
    def _():
        into[...] = value

    @pl.when(t > 0)
    def _():
        into[...] += value


def hidden_back_body(
    t, tick, dy, acts, residual, slope, down, up, vec, up_t, bias_sum, dh, dh_low, sums, back, du
):
    tokens = dy.shape[0]
    last = pl.num_programs(0) - 1
    du[...] = (dot_nt(dy[...], flat(down)) * slope[...].astype(F32)).astype(BF)
    bias_sum[...] = jnp.sum(du[...].astype(F32), axis=0, keepdims=True)
    tick(1)
    up_t[...] = dot_tn(du[...], acts[...]).astype(BF)
    tick(2)
    accumulate(t, back, dot_nn(du[...], flat(up)))

    @pl.when(t == last)
    def _():
        sums[...] = jnp.zeros_like(sums)

        def leave(rows):
            grad = back[rows, :]
            normed, inverse = layer_norm(residual[rows, :], 1.0, 0.0)[1:]
            change, gain, shift = norm_backward(grad, normed, inverse, vec[5:6, :])
            upstream = dy[rows, :].astype(F32)
            here = upstream + change
            dh[rows, :] = here
            low = here.astype(BF)
            dh_low[rows, :] = low
            bias = jnp.sum(low.astype(F32), axis=0)
            for row, value in enumerate((bias, gain, shift, jnp.sum(upstream, axis=0))):
                sums[4 + row : 5 + row, :] += value[None]

        chunks(tokens, CHUNK, leave)


def hidden_backward(
    dy, acts, residual, slope, down_weights, weights, unit_count, vec, jobs, collective_id
):
    tokens = dy.shape[0]
    units = slope.shape[1]
    return fused_call(
        hidden_back_body,
        units // UNITS,
        [
            whole(dy),
            whole(acts),
            whole(residual),
            block(slope, (tokens, UNITS), lambda n: (0, n)),
            unit_rows(down_weights, unit_count, UNITS),
            unit_rows(weights, unit_count, UNITS),
            whole(vec),
        ],
        [
            result((units, D), BF, (UNITS, D), lambda n: (n, 0)),
            result((1, units), F32, (1, UNITS), lambda n: (0, n)),
            result((tokens, D), F32),
            result((tokens, D), BF),
            result((8, D), F32),
        ],
        [pltpu.VMEM((tokens, D), F32), pltpu.VMEM((tokens, UNITS), BF)],
        jobs,
        collective_id,
        ticks=3,
        cost=(0, 5, 5),
        stagger=10.0,
    )


def output_body(t, tick, hidden, down, residual, vec, out, total):
    accumulate(t, total, dot_nn(hidden[...], flat(down)))

    @pl.when(t == pl.num_programs(0) - 1)
    def _():
        def leave(rows):
            out[rows, :] = (residual[rows, :] + total[rows, :] + vec[7:8, :]).astype(BF)

        chunks(hidden.shape[0], CHUNK, leave)


def output_part(hidden, down_weights, unit_count, residual, vec):
    tokens = hidden.shape[0]
    return (
        output_body,
        [
            block(hidden, (tokens, UNITS), lambda n: (0, n)),
            unit_rows(down_weights, unit_count, UNITS),
            whole(residual),
            whole(vec),
        ],
        [result((tokens, D), BF)],
        [pltpu.VMEM((tokens, D), F32)],
        (0, 1.7, 2),
    )


def attend_back_body(
    t, tick, dh_low, out_w, mixed, acts, qkv, lse, sums_in,
    out_t, qkv_t, grads_out, sums, upstream, dk, dv,
):
    length = acts.shape[0]
    scale = HEAD_DIM ** (-0.5)
    grads = grads_out.at[0]

    @pl.when(t == 0)
    def _():
        def enter(rows):
            value = dot_nn(dh_low[rows, :], flat(out_w)).astype(BF)
            for head in range(HEADS):
                upstream[head, rows, :] = value[:, head * HEAD_DIM : (head + 1) * HEAD_DIM]

        chunks(length, 2 * CHUNK, enter)
        out_t[...] = dot_tn(dh_low[...], mixed[...]).astype(BF)
        sums[...] = sums_in[...]

    slope = head_slope(t)
    keys_t = qkv[1].astype(F32).T.astype(BF)
    for start in reversed(range(0, length, QUERY_BLOCK)):
        rows = start + QUERY_BLOCK
        query = qkv[0, start:rows, :]
        above = upstream[t, start:rows, :]
        scores = scores_t(query, qkv[1, :rows, :], slope, start, rows)
        probs = jnp.exp(scores - lse[0, :, start:rows])
        prob_grad = dot_nt(qkv[2, :rows, :], above)
        weighted = probs * prob_grad
        centered = jnp.sum(weighted, axis=0, keepdims=True)
        score_grad = (weighted - probs * centered).astype(BF)
        query_grad = dot_nn(keys_t[:, :rows], score_grad) * scale
        grads[start:rows, :HEAD_DIM] = query_grad.T.astype(BF)
        key_part = dot_nn(score_grad, query)
        value_part = dot_nn(probs.astype(BF), above)
        if rows == length:
            dk[...] = key_part
            dv[...] = value_part
        else:
            dk[:rows, :] += key_part
            dv[:rows, :] += value_part
        tick((length - start) // QUERY_BLOCK)
    grads[:, HEAD_DIM : 2 * HEAD_DIM] = (dk[...] * scale).astype(BF)
    grads[:, 2 * HEAD_DIM :] = dv[...].astype(BF)
    totals = jnp.sum(grads[...].astype(F32), axis=0, keepdims=True)
    lanes = pl.ds(pl.multiple_of(t * HEAD_DIM, HEAD_DIM), HEAD_DIM)
    sums[2:3, lanes] = totals[:, :HEAD_DIM]
    sums[3:4, lanes] = totals[:, 2 * HEAD_DIM :]
    weight_grad = dot_tn(grads[...], acts[...]).astype(BF)
    for part in range(3):
        qkv_t[part] = weight_grad[part * HEAD_DIM : (part + 1) * HEAD_DIM, :]


def attend_backward(dh_low, weights, widths, mixed, acts, qkv, lse, sums, jobs, collective_id):
    tokens = acts.shape[0]
    return fused_call(
        attend_back_body,
        HEADS,
        [
            whole(dh_low),
            rows_of(weights, *widths),
            whole(mixed),
            whole(acts),
            block(qkv, (3, tokens, HEAD_DIM), lambda h: (0, 0, h)),
            block(lse, (1, 1, tokens), lambda h: (h, 0, 0)),
            whole(sums),
        ],
        [
            result((D, D), BF),
            result((3, D, D), BF, (3, HEAD_DIM, D), lambda h: (0, h, 0)),
            result(
                (HEADS, tokens, 3 * HEAD_DIM), BF, (1, tokens, 3 * HEAD_DIM), lambda h: (h, 0, 0)
            ),
            result((8, D), F32),
        ],
        [
            pltpu.VMEM((HEADS, tokens, HEAD_DIM), BF),
            pltpu.VMEM((tokens, HEAD_DIM), F32),
            pltpu.VMEM((tokens, HEAD_DIM), F32),
        ],
        jobs,
        collective_id,
        ticks=5,
        cost=(7, 5.4, 0),
        stagger=0.1,
    )


def input_body(t, tick, grads, wq, wk, wv, x, dh, vec, grad_in, sums, back):
    weights = jnp.concatenate([wq[...], wk[...], wv[...]], axis=0)
    accumulate(t, back, dot_nn(grads[0], weights))

    @pl.when(t == pl.num_programs(0) - 1)
    def _():
        sums[...] = jnp.zeros_like(sums)

        def leave(rows):
            normed, inverse = layer_norm(x[rows, :].astype(F32), 1.0, 0.0)[1:]
            change, gain, shift = norm_backward(back[rows, :], normed, inverse, vec[0:1, :])
            grad_in[rows, :] = (dh[rows, :] + change).astype(BF)
            sums[0:1, :] += gain[None]
            sums[1:2, :] += shift[None]

        chunks(x.shape[0], CHUNK, leave)


def input_part(grads, qkv_full, x, dh, vec):
    tokens = x.shape[0]
    head_rows = lambda part: block(qkv_full, (HEAD_DIM, D), lambda h: (part * HEADS + h, 0))
    return (
        input_body,
        [
            block(grads, (1, tokens, 3 * HEAD_DIM), lambda h: (h, 0, 0)),
            head_rows(0),
            head_rows(1),
            head_rows(2),
            whole(x),
            whole(dh),
            whole(vec),
        ],
        [result((tokens, D), BF), result((8, D), F32)],
        [pltpu.VMEM((tokens, D), F32)],
        (0, 2, 6),
    )


def owner_place(owner):
    return owner // 16, (owner // 8) % 2, (owner // 4) % 2, owner % 4


def forward_body(
    t, tick, gathered, x, dy, qkv, mixed, lse, acts_one, residual, acts, hidden, slope, down_t, vec,
    small, qkv_w, up_w, out_w, bias, small_sem, qkv_sem, up_sem, out_sem,
):
    small_all, qkv_all, up_all, _ = gathered
    length = x.shape[0]
    owned = qkv_w.shape[4]
    up_rows = up_w.shape[2]
    out_rows = out_w.shape[4]

    def load_up(n):
        dst = up_w.at[n % 2]
        src = up_all.at[n // 4, (n // 2) % 2, n % 2, :, pl.ds(0, up_rows)]
        return pltpu.make_async_copy(src, dst, up_sem.at[n % 2])

    def load_out():
        return pltpu.make_async_copy(
            up_all.at[:, :, :, :, pl.ds(up_rows, out_rows)], out_w, out_sem
        )

    @pl.when(t == 0)
    def _():
        weights = pltpu.make_async_copy(qkv_all, qkv_w, qkv_sem)
        vectors = pltpu.make_async_copy(small_all, small, small_sem)
        weights.start()
        vectors.start()
        vectors.wait()
        for group in range(8):
            total = jnp.zeros((8, 128), F32)
            for z in range(4):
                part = small[group // 4, (group // 2) % 2, group % 2, z].astype(F32)
                total = total + part[:8, :]
                at = (group * 4 + z) * 128
                bias[:, at : at + 128] = part[8:9, :]
            vec[:, group * 128 : (group + 1) * 128] = total

        def norm(rows):
            normed = layer_norm(x[rows, :].astype(F32), vec[0:1, :], vec[1:2, :])[0]
            acts_one[rows, :] = normed.astype(BF)

        chunks(length, CHUNK, norm)
        weights.wait()

    @pl.when(t < HEADS)
    def _():
        unit = math.gcd(owned, HEAD_DIM)
        pieces = []
        for part in range(3):
            for i in range(HEAD_DIM // unit):
                index = (part * HEADS + t) * (HEAD_DIM // unit) + i
                per_owner = owned // unit
                row = pl.multiple_of((index % per_owner) * unit, unit)
                pieces.append(qkv_w[(*owner_place(index // per_owner), pl.ds(row, unit))])
        lanes = pl.ds(pl.multiple_of(t * HEAD_DIM, HEAD_DIM), HEAD_DIM)
        projected = dot_nt(acts_one[...], jnp.concatenate(pieces, axis=0))
        qkv[0] = (projected[:, :HEAD_DIM] + vec[2:3, lanes]).astype(BF)
        qkv[1] = projected[:, HEAD_DIM : 2 * HEAD_DIM].astype(BF)
        values = projected[:, 2 * HEAD_DIM :] + vec[3:4, lanes]
        qkv[2] = values.astype(BF)
        values_t = values.T.astype(BF)
        tick(1, 0, HEADS)
        level = head_slope(t)
        for start in range(0, length, QUERY_BLOCK):
            rows = start + QUERY_BLOCK
            scores = scores_t(qkv[0, start:rows, :], qkv[1, :rows, :], level, start, rows)
            highest = jnp.max(scores, axis=0, keepdims=True)
            weights = jnp.exp(scores - highest)
            totals = jnp.sum(weights, axis=0, keepdims=True)
            mix = dot_nn(values_t[:, :rows], weights.astype(BF)) / totals
            mixed[start:rows, lanes] = mix.T.astype(BF)
            lse[0, :, start:rows] = highest + jnp.log(totals)
            if rows < length:
                tick(2 + start // QUERY_BLOCK, 0, HEADS)

    @pl.when(t == HEADS)
    def _():
        load_out().start()
        load_up(0).start()
        load_out().wait()

        def enter(rows):
            attended = dot_nt(mixed[rows, :], flat(out_w)) + vec[4:5, :]
            here = x[rows, :].astype(F32) + attended
            residual[rows, :] = here
            acts[rows, :] = layer_norm(here, vec[5:6, :], vec[6:7, :])[0].astype(BF)

        chunks(length, 2 * CHUNK, enter)

    @pl.when(t >= HEADS)
    def _():
        n = t - HEADS
        load_up(n).wait()

        @pl.when(t < pl.num_programs(0) - 1)
        def _():
            load_up(n + 1).start()

        weights = up_w.at[n % 2]
        lanes = pl.ds(pl.multiple_of(n * UNITS, UNITS), UNITS)
        for start in range(0, length, 256):
            rows = slice(start, start + 256)
            pre = dot_nt(acts[rows, :], flat(weights)) + bias[:, lanes]
            value, steep = gelu_pair(pre)
            hidden[rows, :] = value.astype(BF)
            slope[rows, :] = steep.astype(BF)
            tick(1 + start // 256, HEADS)
        down_t[...] = dot_tn(hidden[...], dy[...]).astype(BF)


def forward(x, dy, small, qkv_w, up_set, down_set, units_rows, out_rows, collective_id):
    tokens = x.shape[0]
    units = 32 * units_rows
    steps = HEADS + units // UNITS
    head = lambda t: jnp.minimum(t, HEADS - 1)
    unit = lambda t: jnp.maximum(t - HEADS, 0)
    jobs = [Gather(small), Gather(qkv_w), Gather(up_set), Gather(down_set)]

    def timeline(ends):
        spans = [(ends[1] + 4 + 3.5 * i, 3.5) for i in range(HEADS)]
        start = max(ends[1] + 4 + 3.5 * HEADS, ends[2])
        return spans + [(start + 5 * (i > 0) + 4 * i, 4) for i in range(steps - HEADS)]

    column = result((tokens, units), BF, (tokens, UNITS), lambda t: (0, unit(t)))
    return fused_call(
        forward_body,
        steps,
        [whole(x), whole(dy)],
        [
            result((3, tokens, D), BF, (3, tokens, HEAD_DIM), lambda t: (0, 0, head(t))),
            result((tokens, D), BF),
            result((HEADS, 1, tokens), F32, (1, 1, tokens), lambda t: (head(t), 0, 0)),
            result((tokens, D), BF),
            result((tokens, D), F32),
            result((tokens, D), BF),
            column,
            column,
            result((units, D), BF, (UNITS, D), lambda t: (unit(t), 0)),
            result((8, D), F32),
        ],
        [
            pltpu.VMEM(jobs[0].shape.shape, BF),
            pltpu.VMEM(jobs[1].shape.shape, BF),
            pltpu.VMEM((2, 4, units_rows, D), BF),
            pltpu.VMEM((2, 2, 2, 4, out_rows, D), BF),
            pltpu.VMEM((1, units), F32),
            pltpu.SemaphoreType.DMA,
            pltpu.SemaphoreType.DMA,
            pltpu.SemaphoreType.DMA((2,)),
            pltpu.SemaphoreType.DMA,
        ],
        jobs,
        collective_id,
        ticks=5,
        stagger=36.0,
        needs={0: 0, 1: 0, 2: HEADS, 3: steps},
        timeline=timeline,
    )


def renew_body(
    t, tick, own, full, root, n_stat, m_stat, m_root, weight, new_n, new_m, new_w, left, product
):
    last = pl.num_programs(0) - 1
    me = lax.axis_index("dp") * lax.axis_size("ffn") + lax.axis_index("ffn")
    rows_owned = m_stat.shape[0]
    share = 128 // rows_owned
    lanes = pl.ds(pl.multiple_of((me // share) * 128, 128), 128)
    here = flat(full)
    new_n[...] = decay_rate * n_stat[...] + (1.0 - decay_rate) * dot_nt(own[...], here)
    left_part = dot_tn(full[:, :, lanes].reshape(-1, 128), here)
    product_part = dot_nn(root[...].astype(BF), here)

    @pl.when(t == 0)
    def _():
        left[...] = left_part
        product[...] = product_part

    @pl.when(t > 0)
    def _():
        left[...] += left_part
        product[...] += product_part

    @pl.when(t == last)
    def _():
        mine = left[pl.ds(pl.multiple_of((me % share) * rows_owned, rows_owned), rows_owned), :]
        new_m[...] = decay_rate * m_stat[...] + (1.0 - decay_rate) * mine
        step = dot_nt(product[...].astype(BF), flat(m_root))
        new_w[...] = weight[...] - matrix_rate * step


def renew(
    own, gathered, at, n_root, n_stat, m_stat, roots, root_at, weight, jobs, collective_id, part=None
):
    rows, total = own.shape[0], n_stat.shape[1]
    rows_owned = m_stat.shape[0]
    body, ins, outs, scratch, more = part or (None, [], [], [], (0, 0, 0))
    if not on_fast_grid():
        extra = fused_call(body, 8, ins, outs, scratch, [], collective_id)[0] if part else []
        full = gathered[:, at : at + rows].reshape(-1, D)
        m_root = roots[:, root_at : root_at + rows_owned].reshape(-1, D)
        me = lax.axis_index("dp") * lax.axis_size("ffn") + lax.axis_index("ffn")
        new_n = decay_rate * n_stat + (1.0 - decay_rate) * dot_nt(own, full)
        mine = lax.dynamic_slice_in_dim(full, me * rows_owned, rows_owned, 1)
        new_m = decay_rate * m_stat + (1.0 - decay_rate) * dot_tn(mine, full)
        product = dot_nn(n_root.astype(BF), full)
        new_w = weight - matrix_rate * dot_nt(product.astype(BF), m_root)
        return [new_n, new_m, new_w] + extra, [job.plainly() for job in jobs]
    owners = {32: 32, 96: 8}.get(rows, 4)
    size = owners * rows
    column = lambda array: block(array, (rows, size), lambda n: (0, n))
    own_ins = [
        whole(own),
        block(gathered, (owners, rows, D), lambda n: (n, at // rows, 0)),
        column(n_root),
        column(n_stat),
        whole(m_stat),
        rows_of(roots, root_at, rows_owned),
        whole(weight),
    ]
    own_outs = [
        result((rows, total), F32, (rows, size), lambda n: (0, n)),
        result((rows_owned, D), F32),
        result((rows, D), F32),
    ]
    own_scratch = [pltpu.VMEM((128, D), F32), pltpu.VMEM((rows, D), F32)]
    sizes = [len(own_ins), len(ins), len(own_outs), len(outs), len(own_scratch), len(scratch)]

    def both(t, tick, *refs):
        cuts = [sum(sizes[:i]) for i in range(len(sizes) + 1)]
        groups = [refs[i:j] for i, j in zip(cuts, cuts[1:])]
        renew_body(t, tick, *groups[0], *groups[2], *groups[4])
        if part:
            tick(1)
            body(t, tick, *groups[1], *groups[3], *groups[5])

    return fused_call(
        both,
        total // size,
        own_ins + ins,
        own_outs + outs,
        own_scratch + scratch,
        jobs,
        collective_id,
        ticks=2 if part else 1,
        cost=(0, 1.6 + more[1], 1 + more[2]),
        stagger=0.1 if len(jobs) > 2 else 36.0,
    )


SMALL_ROWS = 32
SMALL_WIDTH = 128


def pack_small(vector_part, bias_part):
    owners = vector_part.shape[0]
    flat = jnp.concatenate([vector_part.reshape(owners, -1), bias_part.reshape(owners, -1)], axis=1)
    room = SMALL_ROWS * SMALL_WIDTH
    flat = jnp.pad(flat, ((0, 0), (0, room - flat.shape[1])))
    return flat.reshape(owners * SMALL_ROWS, SMALL_WIDTH)


def unpack_small(packed, columns, units):
    owners = packed.shape[0] // SMALL_ROWS
    flat = packed.reshape(owners, -1)
    vector_part = flat[:, : 8 * columns].reshape(owners, 8, columns)
    bias_part = flat[:, 8 * columns : 8 * columns + units]
    return vector_part, bias_part


def shards(
    block_input,
    cotangent,
    w_qkv,
    w_out,
    w_up,
    w_down,
    vectors,
    b_up,
    qkv_left,
    qkv_right,
    out_left,
    out_right,
    up_left,
    up_right,
    down_left,
    down_right,
    qkv_left_root,
    qkv_right_root,
    out_left_root,
    out_right_root,
    up_left_root,
    up_right_root,
    down_left_root,
    down_right_root,
    vector_stat,
    b_up_stat,
):
    owners = lax.axis_size("dp") * lax.axis_size("ffn")
    columns = vectors.shape[1]
    units = b_up.shape[0]
    qkv_w, out_w, up_w = w_qkv.T, w_out.T, w_up.T
    units_rows, qkv_rows, out_rows = units, qkv_w.shape[0], out_w.shape[0]
    root_rows = qkv_left_root.shape[0]

    def stack(*items):
        return Gather(jnp.concatenate([item.astype(BF) for item in items], axis=0))

    def by_owner(array):
        return array.reshape(owners, -1, D)

    up_block = [up_w, out_w]
    down_block = [w_down, out_left_root, qkv_left_root]
    if on_fast_grid():
        lane = (lax.axis_index("ffn") * columns).astype(jnp.int32)
        small = jnp.zeros((SMALL_ROWS, SMALL_WIDTH), BF)
        small = lax.dynamic_update_slice(small, vectors.astype(BF), (0, lane))
        small = lax.dynamic_update_slice(small, b_up.astype(BF)[None], (8, 0))
        results, gathered = forward(
            block_input,
            cotangent,
            small,
            qkv_w.astype(BF),
            stack(*up_block).array,
            stack(*down_block).array,
            units_rows,
            out_rows,
            1,
        )
        qkv, mixed, logsum, acts_one, residual, acts_two, hidden, slope, down_t, vector_rows = results
        _, qkv_full, up_set, down_set = gathered
        up_set, down_set = by_owner(up_set), by_owner(down_set)
    else:
        small = pack_small(vectors[None], b_up[None]).astype(BF)
        small_full, qkv_full = transfer([Gather(small), Gather(qkv_w.astype(BF))], 1)
        vector_low, bias_low = unpack_small(small_full, columns, units)
        vector_rows = vector_low.transpose(1, 0, 2).reshape(8, D).astype(F32)
        up_bias = bias_low.reshape(1, -1).astype(F32)
        (qkv, mixed, logsum, acts_one), (up_set,) = attend(
            block_input, vector_rows, qkv_full, [stack(*up_block)], 2
        )
        up_set = by_owner(up_set)
        (residual, acts_two, hidden, slope, down_t), (down_set,) = hidden_forward(
            block_input,
            mixed,
            up_set,
            (units_rows, out_rows),
            vector_rows,
            cotangent,
            up_bias,
            [stack(*down_block)],
            3,
        )
        down_set = by_owner(down_set)
    (up_t, bias_grad, dh, dh_low, sums), (down_g, down_mroot) = hidden_backward(
        cotangent,
        acts_two,
        residual,
        slope,
        down_set,
        up_set,
        units_rows,
        vector_rows,
        [Reduce(down_t), stack(down_right_root)],
        4,
    )
    down_low = down_g.astype(BF)
    (out_t, qkv_t, qkv_grads, sums), (up_g, down_all) = attend_backward(
        dh_low,
        up_set,
        (units_rows, out_rows),
        mixed,
        acts_one,
        qkv,
        logsum,
        sums,
        [Reduce(up_t), Gather(down_low)],
        5,
    )
    up_low = up_g.astype(BF)
    (new_down_n, new_down_m, new_w_down, input_grad, first_sums), (up_all, qkv_g, out_g) = renew(
        down_low,
        by_owner(down_all),
        0,
        down_left_root,
        down_left,
        down_right,
        by_owner(down_mroot),
        0,
        w_down,
        [stack(up_low, up_left_root), Reduce(qkv_t.reshape(-1, D)), Reduce(out_t)],
        6,
        input_part(qkv_grads, qkv_full, block_input, dh, vector_rows),
    )
    small_part = pack_small(
        (sums + first_sums).reshape(8, owners, columns).transpose(1, 0, 2),
        bias_grad.reshape(owners, units),
    ).astype(BF)
    qkv_low, out_low = qkv_g.astype(BF), out_g.astype(BF)
    up_all = by_owner(up_all)
    (new_up_n, new_up_m, new_w_up, block_output), (last_all, small_g) = renew(
        up_low,
        up_all,
        0,
        up_right_root,
        up_right,
        up_left,
        up_all,
        units_rows,
        up_w,
        [stack(qkv_low, out_low), Reduce(small_part)],
        7,
        output_part(hidden, down_set, units_rows, residual, vector_rows),
    )
    last_all = by_owner(last_all)
    new_qkv_n, new_qkv_m, new_w_qkv = renew(
        qkv_low,
        last_all,
        0,
        qkv_right_root,
        qkv_right,
        qkv_left,
        down_set,
        units_rows + root_rows,
        qkv_w,
        [],
        8,
    )[0]
    new_out_n, new_out_m, new_w_out = renew(
        out_low,
        last_all,
        qkv_rows,
        out_right_root,
        out_right,
        out_left,
        down_set,
        units_rows,
        out_w,
        [],
        8,
    )[0]
    new_m = [new_qkv_m, new_out_m, new_up_m, new_down_m]
    new_n = [new_qkv_n, new_out_n, new_up_n, new_down_n]
    new_w_qkv, new_w_out, new_w_up = new_w_qkv.T, new_w_out.T, new_w_up.T
    grads = [qkv_g, out_g, up_g, down_g]
    vector_grad, b_up_grad = unpack_small(small_g, columns, units)
    vector_grad, b_up_grad = vector_grad[0], b_up_grad[0]
    new_vector_stat = decay_rate * vector_stat + (1.0 - decay_rate) * vector_grad * vector_grad
    new_vectors = vectors - vector_rate * vector_grad * lax.rsqrt(new_vector_stat)
    new_b_up_stat = decay_rate * b_up_stat + (1.0 - decay_rate) * b_up_grad * b_up_grad
    new_b_up = b_up - vector_rate * b_up_grad * lax.rsqrt(new_b_up_stat)
    return (
        block_output,
        input_grad,
        grads[0].T,
        grads[1].T,
        grads[2].T,
        grads[3],
        vector_grad,
        b_up_grad,
        new_m[0],
        new_n[0],
        new_m[1],
        new_n[1],
        new_m[2],
        new_n[2],
        new_n[3],
        new_m[3],
        new_vector_stat,
        new_b_up_stat,
        new_w_qkv,
        new_w_out,
        new_w_up,
        new_w_down,
        new_vectors,
        new_b_up,
    )


def solution(mesh):
    return jax.shard_map(
        shards,
        mesh=mesh,
        in_specs=(
            P(("dp", "ffn"), None),
            P(("dp", "ffn"), None),
            P(None, ("dp", "ffn")),
            P(None, ("dp", "ffn")),
            P(None, ("dp", "ffn")),
            P(("dp", "ffn"), None),
            P(None, ("dp", "ffn")),
            P(("dp", "ffn")),
            P(("dp", "ffn"), None),
            P(("dp", "ffn"), None),
            P(("dp", "ffn"), None),
            P(("dp", "ffn"), None),
            P(("dp", "ffn"), None),
            P(("dp", "ffn"), None),
            P(("dp", "ffn"), None),
            P(("dp", "ffn"), None),
            P(("dp", "ffn"), None),
            P(("dp", "ffn"), None),
            P(("dp", "ffn"), None),
            P(("dp", "ffn"), None),
            P(("dp", "ffn"), None),
            P(("dp", "ffn"), None),
            P(("dp", "ffn"), None),
            P(("dp", "ffn"), None),
            P(None, ("dp", "ffn")),
            P(("dp", "ffn")),
        ),
        out_specs=(
            P(("dp", "ffn"), None),
            P(("dp", "ffn"), None),
            P(None, ("dp", "ffn")),
            P(None, ("dp", "ffn")),
            P(None, ("dp", "ffn")),
            P(("dp", "ffn"), None),
            P(None, ("dp", "ffn")),
            P(("dp", "ffn")),
            P(("dp", "ffn"), None),
            P(("dp", "ffn"), None),
            P(("dp", "ffn"), None),
            P(("dp", "ffn"), None),
            P(("dp", "ffn"), None),
            P(("dp", "ffn"), None),
            P(("dp", "ffn"), None),
            P(("dp", "ffn"), None),
            P(None, ("dp", "ffn")),
            P(("dp", "ffn")),
            P(None, ("dp", "ffn")),
            P(None, ("dp", "ffn")),
            P(None, ("dp", "ffn")),
            P(("dp", "ffn"), None),
            P(None, ("dp", "ffn")),
            P(("dp", "ffn")),
        ),
        check_vma=False,
    )
```

```python
import functools
import math

import jax
import jax.numpy as jnp
from jax import lax
from jax.experimental import pallas as pl
from jax.experimental.pallas import tpu as pltpu
from jax.sharding import PartitionSpec as P

D = 1024
HEADS = 8
HEAD_DIM = 128
MESH = pl.DeviceIdType.MESH
ALL = ("dp", "ffn")
BF = jnp.bfloat16
F32 = jnp.float32
MIB = 2**20

norm_epsilon = 1e-05
decay_rate = 0.5
matrix_rate = 0.5
vector_rate = 0.1
masked_score = -1e30


def layer_norm(values, gain, shift):
    center = values - jnp.mean(values, axis=-1, keepdims=True)
    inverse = lax.rsqrt(jnp.mean(center * center, axis=-1, keepdims=True) + norm_epsilon)
    normed = center * inverse
    return (normed * gain + shift, normed, inverse)


def norm_backward(grad, normed, inverse, gain):
    scaled = grad * gain
    inner = (
        scaled
        - jnp.mean(scaled, axis=-1, keepdims=True)
        - normed * jnp.mean(scaled * normed, axis=-1, keepdims=True)
    )
    return (inner * inverse, jnp.sum(grad * normed, axis=0), jnp.sum(grad, axis=0))


def dot_nt(left, right):
    return lax.dot_general(left, right, (((1,), (1,)), ((), ())), preferred_element_type=F32)


def dot_tn(left, right):
    return lax.dot_general(left, right, (((0,), (0,)), ((), ())), preferred_element_type=F32)


def dot_nn(left, right):
    return jnp.dot(left, right, preferred_element_type=F32)


def flip(value, mask):
    result = value
    bit = 1
    while bit <= mask:
        if mask & bit:
            result = result + bit - 2 * bit * ((result // bit) % 2)
        bit *= 2
    return result


class Copies:
    def __init__(self, send, recv):
        self.send, self.recv, self.made = send, recv, {}

    def copy(self, name):
        at, make = self.made[name]
        src, dst, device = make()
        return pltpu.make_async_remote_copy(
            src, dst, self.send.at[at], self.recv.at[at], device_id=device, device_id_type=MESH
        )

    def plan(self, name, make):
        self.made[name] = (len(self.made), make)

    def post(self, name):
        self.copy(name).start()

    def got(self, name):
        self.copy(name).wait_recv()

    def sent(self):
        for name in self.made:
            self.copy(name).wait_send()


class Place:
    def __init__(self):
        dp = lax.axis_index("dp")
        self.y, self.x, self.c, self.z = dp // 4, (dp // 2) % 2, dp % 2, lax.axis_index("ffn")

    def device(self, y=0, x=0, c=0, z=0):
        dp = (flip(self.y, y) * 2 + flip(self.x, x)) * 2 + flip(self.c, c)
        return dp, flip(self.z, z)

    def span(self, group):
        if len(group) == 1:
            return pl.ds(flip(self.z, group[0]), 1)
        if len(group) == 2:
            return pl.ds(flip(self.z // 2, group[0] // 2) * 2, 2)
        return pl.ds(0, 4)


def greet(place):
    barrier = pltpu.get_barrier_semaphore()
    steps = [dict(y=1), dict(x=1), dict(c=1), dict(z=1), dict(z=2), dict(z=3)]
    for step in steps:
        pl.semaphore_signal(
            barrier, inc=1, device_id=place.device(**step), device_id_type=MESH
        )
    pl.semaphore_wait(barrier, len(steps))


def one(index):
    return pl.ds(index, 1)


TURNS = (("x", "y"), ("y", "x"))


def gather_plan(place, shard, out, send, recv, local_sem):
    y, x, c, z = place.y, place.x, place.c, place.z
    half_rows = shard.shape[0] // 2
    copies = Copies(send, recv)

    def half(ref, h):
        return ref.at[pl.ds(h * half_rows, half_rows)]

    def local():
        return pltpu.make_async_copy(shard, out.at[y, x, c, z], local_sem)

    def along_z(k):
        return shard, out.at[y, x, c, z], place.device(z=k)

    def own(turn, k, h):
        dst = half(out.at[y, x, c, flip(z, k)], h)
        return (dst if k else half(shard, h)), dst, place.device(**{TURNS[h][turn]: 1})

    def relay(k, h):
        block = out.at[y, 1 - x, c, flip(z, k)] if h == 0 else out.at[1 - y, x, c, flip(z, k)]
        return half(block, h), half(block, h), place.device(**{TURNS[h][1]: 1})

    def across(k):
        piece = out.at[:, :, c, flip(z, k)]
        return piece, piece, place.device(c=1)

    do = functools.partial
    for k in range(4):
        if k:
            copies.plan(("z", k), do(along_z, k))
        for h in (0, 1):
            copies.plan(("first", k, h), do(own, 0, k, h))
            copies.plan(("second", k, h), do(own, 1, k, h))
            copies.plan(("relay", k, h), do(relay, k, h))
        copies.plan(("core", k), do(across, k))

    def spread(k):
        for name in ("first", "second"):
            for h in (0, 1):
                copies.post((name, k, h))

    def begin():
        copies.post(("z", 1))
        spread(0)
        local().start()

    def landed(k):
        copies.got(("z", k))
        if k < 3:
            copies.post(("z", k + 1))
        spread(k)

    def forward(k):
        for h in (0, 1):
            copies.got(("first", k, h))
            copies.post(("relay", k, h))

    def share(k):
        for h in (0, 1):
            copies.got(("second", k, h))
            copies.got(("relay", k, h))
        if k == 0:
            local().wait()
        copies.post(("core", k))

    def finish():
        for k in range(4):
            copies.got(("core", k))
        copies.sent()

    return [
        (0, 0, begin),
        (4, 1, do(forward, 0)),
        (6, 1, do(landed, 1)),
        (13, 2, do(share, 0)),
        (14, 2, do(forward, 1)),
        (18, 2, do(landed, 2)),
        (20, 3, do(share, 1)),
        (24, 3, do(forward, 2)),
        (30, 2, do(landed, 3)),
        (31, 3, do(share, 2)),
        (35, 3, do(forward, 3)),
        (39, 3, do(share, 3)),
        (40, 4, finish),
    ]


def gather_small_plan(place, shard, out, send, recv, local_sem):
    y, x, c, z = place.y, place.x, place.c, place.z
    rows = shard.shape[0]
    copies = Copies(send, recv)

    def half(h):
        return pl.ds(h * (rows // 2), rows // 2)

    def local():
        return pltpu.make_async_copy(shard, out.at[y, x, c, z], local_sem)

    def along_z(k):
        return shard, out.at[y, x, c, z], place.device(z=k)

    def first(h):
        piece = out.at[y, x, c, :, half(h)]
        return piece, piece, place.device(**{TURNS[h][0]: 1})

    def second(h):
        piece = out.at[y, :, c, :, half(h)] if h == 0 else out.at[:, x, c, :, half(h)]
        return piece, piece, place.device(**{TURNS[h][1]: 1})

    def across():
        piece = out.at[:, :, c]
        return piece, piece, place.device(c=1)

    do = functools.partial
    for k in (1, 2, 3):
        copies.plan(("z", k), do(along_z, k))
    for h in (0, 1):
        copies.plan(("first", h), do(first, h))
        copies.plan(("second", h), do(second, h))
    copies.plan("core", across)

    def begin():
        local().start()
        for k in (1, 2, 3):
            copies.post(("z", k))

    def start_first():
        for k in (1, 2, 3):
            copies.got(("z", k))
        local().wait()
        for h in (0, 1):
            copies.post(("first", h))

    def start_second():
        for h in (0, 1):
            copies.got(("first", h))
            copies.post(("second", h))

    def share():
        for h in (0, 1):
            copies.got(("second", h))
        copies.post("core")

    def finish():
        copies.got("core")
        copies.sent()

    return [
        (0, 0, begin),
        (24, 1, start_first),
        (36, 2, start_second),
        (60, 3, share),
        (62, 4, finish),
    ]


def gather_z_last_plan(place, shard, out, send, recv, local_sem):
    y, x, c, z = place.y, place.x, place.c, place.z
    rows = shard.shape[0]
    copies = Copies(send, recv)

    def half(h):
        return pl.ds(h * (rows // 2), rows // 2)

    def local():
        return pltpu.make_async_copy(shard, out.at[y, x, c, z], local_sem)

    def first(h):
        return shard.at[half(h)], out.at[y, x, c, z, half(h)], place.device(**{TURNS[h][0]: 1})

    def second(h):
        piece = out.at[y, :, c, z, half(h)] if h == 0 else out.at[:, x, c, z, half(h)]
        return piece, piece, place.device(**{TURNS[h][1]: 1})

    def along_z(k):
        piece = out.at[:, :, c, z]
        return piece, piece, place.device(z=k)

    def across():
        piece = out.at[:, :, c]
        return piece, piece, place.device(c=1)

    do = functools.partial
    for h in (0, 1):
        copies.plan(("first", h), do(first, h))
        copies.plan(("second", h), do(second, h))
    for k in (1, 2, 3):
        copies.plan(("z", k), do(along_z, k))
    copies.plan("core", across)

    def begin():
        local().start()
        for h in (0, 1):
            copies.post(("first", h))

    def start_second():
        local().wait()
        for h in (0, 1):
            copies.got(("first", h))
            copies.post(("second", h))

    def column():
        for h in (0, 1):
            copies.got(("second", h))
        for k in (1, 2, 3):
            copies.post(("z", k))

    def share():
        for k in (1, 2, 3):
            copies.got(("z", k))
        copies.post("core")

    def finish():
        copies.got("core")
        copies.sent()

    return [(0, 0, begin), (3, 1, start_second), (9, 2, column), (93, 3, share), (100, 4, finish)]


def reduce_plan(
    place, parts, out, held, from_core, from_second, from_first, from_z, send, recv, load
):
    y, x, c, z = place.y, place.x, place.c, place.z
    rows = parts.shape[-2]
    whole_first = rows < 64
    groups = [(0, 1, 2, 3)] if whole_first else [(3,), (2,), (1,), (0,)]
    copies = Copies(send, recv)

    def half(h):
        return pl.ds(h * (rows // 2), rows // 2)

    def local(group):
        span = place.span(group)
        return pltpu.make_async_copy(
            parts.at[:, :, c, span], held.at[:, :, span], load.at[groups.index(group)]
        )

    def core_route(group):
        span = place.span(group)
        return parts.at[:, :, 1 - c, span], from_core.at[:, :, span], place.device(c=1)

    def second_part(group, h, other):
        at = (1 - y if other else y) if h == 0 else (1 - x if other else x)
        if h == 0:
            return (at, slice(None), place.span(group), half(h))
        return (slice(None), at, place.span(group), half(h))

    def second_route(group, h):
        return (
            held.at[second_part(group, h, True)],
            from_second.at[h, :, place.span(group)],
            place.device(**{TURNS[h][1]: 1}),
        )

    def first_part(group, h):
        return (y, 1 - x, place.span(group), half(h)) if h == 0 else (1 - y, x, place.span(group), half(h))

    def first_route(group, h):
        return (
            held.at[first_part(group, h)],
            from_first.at[h, place.span(group)],
            place.device(**{TURNS[h][0]: 1}),
        )

    def z_route(k):
        return held.at[y, x, flip(z, k)], from_z.at[k - 1], place.device(z=k)

    do = functools.partial
    for group in groups:
        copies.plan(("core", group), do(core_route, group))
        for h in (0, 1):
            copies.plan(("second", group, h), do(second_route, group, h))
            copies.plan(("first", group, h), do(first_route, group, h))
        for k in group:
            if k:
                copies.plan(("z", k), do(z_route, k))

    def add(dst, *sources):
        if len(sources) == 1:
            dst[...] += sources[0][...]
            return
        total = dst[...].astype(F32)
        for source in sources:
            total = total + source[...].astype(F32)
        dst[...] = total.astype(BF)

    def to_core(group):
        copies.post(("core", group))
        local(group).start()

    def begin():
        to_core(groups[0])

    def cores(group):
        local(group).wait()
        copies.got(("core", group))
        at = groups.index(group)
        if at + 1 < len(groups):
            to_core(groups[at + 1])
        for other in (True, False):
            for h in (0, 1):
                part = second_part(group, h, other)
                add(held.at[part], from_core.at[part])
                if other:
                    copies.post(("second", group, h))

    def second(group):
        span = place.span(group)
        for h in (0, 1):
            copies.got(("second", group, h))
            away = 1 - x if h == 0 else 1 - y
            add(held.at[first_part(group, h)], from_second.at[h, away, span])
            copies.post(("first", group, h))

    def first(group):
        span = place.span(group)
        for h in (0, 1):
            copies.got(("first", group, h))
            mine = x if h == 0 else y
            add(held.at[y, x, span, half(h)], from_second.at[h, mine, span], from_first.at[h, span])
        for k in group:
            if k:
                copies.post(("z", k))

    def finish():
        for k in (1, 2, 3):
            copies.got(("z", k))
        total = held[y, x, z].astype(F32)
        for k in range(3):
            total = total + from_z[k].astype(F32)
        out[...] = total
        copies.sent()

    if whole_first:
        (group,) = groups
        return [
            (0, 0, begin),
            (7, 1, do(cores, group)),
            (31, 2, do(second, group)),
            (43, 3, do(first, group)),
            (67, 4, finish),
        ]
    a, b, d, e = groups
    return [
        (0, 0, begin),
        (2, 1, do(cores, a)),
        (4, 1.2, do(cores, b)),
        (6, 2, do(second, a)),
        (8, 2, do(cores, d)),
        (12, 3, do(first, a)),
        (15, 2, do(second, b)),
        (17, 2, do(cores, e)),
        (20, 3, do(first, b)),
        (24, 2, do(second, d)),
        (29, 3, do(first, d)),
        (33, 2, do(second, e)),
        (38, 3, do(first, e)),
        (42, 4, finish),
    ]


HOP_US = 2.0
FULL_BLOCK = 128 * 1024


def merge_plans(jobs, plans, stagger):
    timed = []
    start = 0.0
    for g, (job, plan) in enumerate(zip(jobs, plans)):
        size = job.rows * job.width / FULL_BLOCK
        own = 0.0 if job.beside else start
        at = 0.0
        for i, (volume, hops, step) in enumerate(plan):
            ahead = 0.0 if i else min(own, 20.0 * size)
            at = max(at, own - ahead + volume * size + hops * HOP_US)
            timed.append((at, g, i, step))
        if not job.beside:
            start += stagger * size
        else:
            start += 9.0 * size
    timed.sort(key=lambda item: item[:3])
    return [(at, step, g, i == len(plans[g]) - 1) for at, g, i, step in timed]


ANYWHERE = pl.BlockSpec(memory_space=pl.ANY)
COPIES = 31


class Gather:
    def __init__(self, shard, z_last=False):
        self.array = shard
        self.rows, self.width = shard.shape
        self.shape = jax.ShapeDtypeStruct((2, 2, 2, 4, self.rows, self.width), BF)
        self.spec = ANYWHERE
        sems = pltpu.SemaphoreType.DMA((COPIES,))
        self.scratch = [sems, sems, pltpu.SemaphoreType.DMA]
        self.beside = z_last
        self.plan = gather_plan if self.rows >= 64 else gather_small_plan
        if z_last:
            self.plan = gather_z_last_plan

    def finish(self, out):
        return out.reshape(-1, self.width)

    def plainly(self):
        return lax.all_gather(self.array, ALL, axis=0, tiled=True)


class Reduce:
    def __init__(self, parts):
        devices = lax.axis_size("dp") * lax.axis_size("ffn")
        self.parts = parts
        self.rows, width = parts.shape[0] // devices, parts.shape[1]
        self.width, self.beside = width, False
        self.shape = jax.ShapeDtypeStruct((self.rows, width), F32)
        self.spec = pl.BlockSpec((self.rows, width), lambda *_: (0, 0))
        sems = pltpu.SemaphoreType.DMA((COPIES,))
        rows = self.rows
        self.scratch = [
            pltpu.VMEM((2, 2, 4, rows, width), BF),
            pltpu.VMEM((2, 2, 4, rows, width), BF),
            pltpu.VMEM((2, 2, 4, rows // 2, width), BF),
            pltpu.VMEM((2, 4, rows // 2, width), BF),
            pltpu.VMEM((3, rows, width), BF),
            sems,
            sems,
            pltpu.SemaphoreType.DMA((4,)),
        ]
        self.plan = reduce_plan

    @property
    def array(self):
        return self.parts.reshape(2, 2, 2, 4, self.rows, self.parts.shape[1])

    def finish(self, out):
        return out

    def plainly(self):
        return lax.psum_scatter(self.parts, ALL, scatter_dimension=0, tiled=True).astype(F32)


def on_fast_grid():
    return lax.axis_size("dp") == 8 and lax.axis_size("ffn") == 4


def fused_call(
    body,
    steps,
    ins,
    outs,
    scratch,
    jobs,
    collective_id,
    ticks=1,
    cost=(0, 1, 0),
    stagger=28.0,
    needs=None,
    timeline=None,
):
    plainly = not (on_fast_grid() and all(job.rows % 32 == 0 for job in jobs))
    run = [] if plainly else jobs
    held = [i for i, item in enumerate(ins) if item[1] is None]
    counts = [len(ins), len(run), len(outs), len(run), len(scratch), len(held), len(held)]

    def kernel(*refs):
        groups = []
        at = 0
        for count in counts:
            groups.append(refs[at : at + count])
            at += count
        own_in, job_in, own_out, job_out, own_scratch, buffers, arrived = groups
        own_in = list(own_in)
        loads = []
        for i, buffer, sem in zip(held, buffers, arrived):
            loads.append((own_in[i], buffer, sem))
            own_in[i] = buffer
        t = pl.program_id(0)
        if loads:

            @pl.when(t == 0)
            def _():
                for load in loads:
                    pltpu.make_async_copy(*load).start()

        here = {}
        rest = []
        if run:
            place = Place()
            plans = []
            for job, src, dst in zip(run, job_in, job_out):
                plans.append(job.plan(place, src, dst, *refs[at : at + len(job.scratch)]))
                at += len(job.scratch)
            merged = merge_plans(run, plans, stagger)
            before, each_step, after = cost
            pace = min(1.0, (before + each_step * steps + after) / merged[-1][0])
            spans = [(before * (i > 0) + each_step * i, each_step) for i in range(steps)]
            if timeline:
                pace = 1.0
                spans = timeline({g: when for when, _, g, is_last in merged if is_last})
            clocks = [0.0]
            for start, length in spans:
                clocks += [start + length * j / ticks for j in range(ticks)]
            clocks = [0.0] + clocks[2:]
            limits = [(needs or {}).get(g, steps) * ticks if is_last else steps * ticks for _, _, g, is_last in merged]
            position = 0
            for i, (when, step, _, _) in enumerate(merged):
                while position < steps * ticks and clocks[position] < when * pace:
                    position += 1
                position = min([position] + limits[i:])
                if position < steps * ticks:
                    here.setdefault(position, []).append(step)
                else:
                    rest.append(step)
            here.setdefault(0, []).insert(0, functools.partial(greet, place))

        def tick(j, least=0, most=steps):
            for position in sorted(here):
                if position % ticks == j and least <= position // ticks < most:

                    @pl.when(t == position // ticks)
                    def _(now=here[position]):
                        for each in now:
                            each()

        tick(0)
        if loads:

            @pl.when(t == 0)
            def _():
                for load in loads:
                    pltpu.make_async_copy(*load).wait()

        if body is not None:
            shared = [job_out] if needs else []
            body(t, tick, *shared, *own_in, *own_out, *own_scratch)
        if rest:

            @pl.when(t == steps - 1)
            def _():
                for each in rest:
                    each()

    all_scratch = list(scratch)
    all_scratch += [pltpu.VMEM(ins[i][0].shape, ins[i][0].dtype) for i in held]
    all_scratch += [pltpu.SemaphoreType.DMA] * len(held)
    for job in run:
        all_scratch += job.scratch
    extra = dict(collective_id=collective_id, has_side_effects=True) if run else {}
    results = pl.pallas_call(
        kernel,
        grid=(steps,),
        out_shape=tuple(o[0] for o in outs) + tuple(job.shape for job in run),
        in_specs=[i[1] or ANYWHERE for i in ins] + [ANYWHERE] * len(run),
        out_specs=tuple(o[1] for o in outs) + tuple(job.spec for job in run),
        scratch_shapes=all_scratch,
        compiler_params=pltpu.CompilerParams(vmem_limit_bytes=60 * MIB, **extra),
    )(*[i[0] for i in ins], *[job.array for job in run])
    own = list(results[: len(outs)])
    if plainly:
        return own, [job.plainly() for job in jobs]
    return own, [job.finish(out) for job, out in zip(jobs, results[len(outs) :])]


def transfer(jobs, collective_id):
    if not (on_fast_grid() and all(job.rows % 32 == 0 for job in jobs)):
        return [job.plainly() for job in jobs]
    return fused_call(None, 1, [], [], [], jobs, collective_id)[1]


def whole(array):
    return array, None


def rows_of(array, first, count):
    if on_fast_grid() and count % 16 == 0 and first % count == 0:
        shape = (array.shape[0], count, D)
        at = first // count
        return array, pl.BlockSpec(shape, lambda t: (0, at, 0), pipeline_mode=pl.Buffered(1))
    return whole(array[:, first : first + count].reshape(-1, D))


def unit_rows(array, count, total):
    return array, pl.BlockSpec((total // count, count, D), lambda n: (n, 0, 0))


def flat(ref):
    return ref[...].reshape(-1, D)


def block(array, shape, at):
    return array, pl.BlockSpec(shape, at)


def result(shape, dtype, tile=None, at=None):
    rank = len(shape)
    if tile is None:
        return jax.ShapeDtypeStruct(shape, dtype), pl.BlockSpec(shape, lambda t: (0,) * rank)
    return jax.ShapeDtypeStruct(shape, dtype), pl.BlockSpec(tile, at)


def chunks(rows, size, body):
    @pl.loop(0, rows // size)
    def _(i):
        body(pl.ds(pl.multiple_of(i * size, size), size))


QUERY_BLOCK = 256
CHUNK = 128
UNITS = 512


def head_slope(head):
    level = head.astype(F32) + 1.0
    return jnp.exp2(jnp.full((1, 1), -8.0 / HEADS, F32) * level)


def scores_t(query, keys, slope, start, rows):
    at_key = lax.broadcasted_iota(jnp.int32, (rows, 1), 0).astype(F32)
    scores = dot_nt(keys, query) * HEAD_DIM ** (-0.5) + at_key * slope
    at_key = lax.broadcasted_iota(jnp.int32, (rows, QUERY_BLOCK), 0)
    at_query = lax.broadcasted_iota(jnp.int32, (rows, QUERY_BLOCK), 1) + start
    return jnp.where(at_key <= at_query, scores, masked_score)


def attend_body(t, tick, x, vec, wq, wk, wv, head_vec, qkv, mixed, lse, acts):
    length = x.shape[0]

    @pl.when(t == 0)
    def _():
        def norm(rows):
            normed = layer_norm(x[rows, :].astype(F32), vec[0:1, :], vec[1:2, :])[0]
            acts[rows, :] = normed.astype(BF)

        chunks(length, CHUNK, norm)

    weights = jnp.concatenate([wq[...], wk[...], wv[...]], axis=0)
    projected = dot_nt(acts[...], weights)
    qkv[0] = (projected[:, :HEAD_DIM] + head_vec[2:3, :]).astype(BF)
    qkv[1] = projected[:, HEAD_DIM : 2 * HEAD_DIM].astype(BF)
    values = projected[:, 2 * HEAD_DIM :] + head_vec[3:4, :]
    qkv[2] = values.astype(BF)
    values_t = values.T.astype(BF)
    tick(1)
    slope = head_slope(t)
    for start in range(0, length, QUERY_BLOCK):
        rows = start + QUERY_BLOCK
        scores = scores_t(qkv[0, start:rows, :], qkv[1, :rows, :], slope, start, rows)
        highest = jnp.max(scores, axis=0, keepdims=True)
        weights = jnp.exp(scores - highest)
        totals = jnp.sum(weights, axis=0, keepdims=True)
        mix = dot_nn(values_t[:, :rows], weights.astype(BF)) / totals
        mixed[start:rows, :] = mix.T.astype(BF)
        lse[0, :, start:rows] = highest + jnp.log(totals)
        if rows < length:
            tick(2 + start // QUERY_BLOCK)


def attend(x, vec, qkv_full, jobs, collective_id):
    tokens = x.shape[0]
    head_rows = lambda part: block(
        qkv_full, (HEAD_DIM, D), lambda h: (part * HEADS + h, 0)
    )
    return fused_call(
        attend_body,
        HEADS,
        [
            whole(x),
            whole(vec),
            head_rows(0),
            head_rows(1),
            head_rows(2),
            block(vec, (8, HEAD_DIM), lambda h: (0, h)),
        ],
        [
            result((3, tokens, D), BF, (3, tokens, HEAD_DIM), lambda h: (0, 0, h)),
            result((tokens, D), BF, (tokens, HEAD_DIM), lambda h: (0, h)),
            result((HEADS, 1, tokens), F32, (1, 1, tokens), lambda h: (h, 0, 0)),
            result((tokens, D), BF),
        ],
        [],
        jobs,
        collective_id,
        ticks=5,
        cost=(3, 3.4, 0),
    )


def gelu_pair(pre):
    half = 0.5 * (1.0 + lax.erf(pre * 0.7071067811865476))
    slope = half + pre * jnp.exp(-0.5 * pre * pre) * 0.3989422804014327
    return pre * half, slope


def hidden_body(t, tick, x, mixed, out_w, vec, dy, up, bias, residual, acts, hidden, slope, down_t):
    tokens = x.shape[0]

    @pl.when(t == 0)
    def _():
        def enter(rows):
            attended = dot_nt(mixed[rows, :], flat(out_w)) + vec[4:5, :]
            here = x[rows, :].astype(F32) + attended
            residual[rows, :] = here
            acts[rows, :] = layer_norm(here, vec[5:6, :], vec[6:7, :])[0].astype(BF)

        chunks(tokens, 2 * CHUNK, enter)

    for start in range(0, tokens, 256):
        rows = slice(start, start + 256)
        pre = dot_nt(acts[rows, :], flat(up)) + bias[...]
        value, steep = gelu_pair(pre)
        hidden[rows, :] = value.astype(BF)
        slope[rows, :] = steep.astype(BF)
        tick(1 + start // 256)
    down_t[...] = dot_tn(hidden[...], dy[...]).astype(BF)


def hidden_forward(x, mixed, weights, widths, vec, dy, bias, jobs, collective_id):
    tokens = x.shape[0]
    units = bias.shape[1]
    up_rows, out_rows = widths
    return fused_call(
        hidden_body,
        units // UNITS,
        [
            whole(x),
            whole(mixed),
            rows_of(weights, up_rows, out_rows),
            whole(vec),
            whole(dy),
            unit_rows(weights, up_rows, UNITS),
            block(bias, (1, UNITS), lambda n: (0, n)),
        ],
        [
            result((tokens, D), F32),
            result((tokens, D), BF),
            result((tokens, units), BF, (tokens, UNITS), lambda n: (0, n)),
            result((tokens, units), BF, (tokens, UNITS), lambda n: (0, n)),
            result((units, D), BF, (UNITS, D), lambda n: (n, 0)),
        ],
        [],
        jobs,
        collective_id,
        ticks=5,
        cost=(5, 4, 0),
    )


def accumulate(t, into, value):
    @pl.when(t == 0)
    def _():
        into[...] = value

    @pl.when(t > 0)
    def _():
        into[...] += value


def hidden_back_body(
    t, tick, dy, acts, residual, slope, down, up, vec, up_t, bias_sum, dh, dh_low, sums, back, du
):
    tokens = dy.shape[0]
    last = pl.num_programs(0) - 1
    du[...] = (dot_nt(dy[...], flat(down)) * slope[...].astype(F32)).astype(BF)
    bias_sum[...] = jnp.sum(du[...].astype(F32), axis=0, keepdims=True)
    tick(1)
    up_t[...] = dot_tn(du[...], acts[...]).astype(BF)
    tick(2)
    accumulate(t, back, dot_nn(du[...], flat(up)))

    @pl.when(t == last)
    def _():
        sums[...] = jnp.zeros_like(sums)

        def leave(rows):
            grad = back[rows, :]
            normed, inverse = layer_norm(residual[rows, :], 1.0, 0.0)[1:]
            change, gain, shift = norm_backward(grad, normed, inverse, vec[5:6, :])
            upstream = dy[rows, :].astype(F32)
            here = upstream + change
            dh[rows, :] = here
            low = here.astype(BF)
            dh_low[rows, :] = low
            bias = jnp.sum(low.astype(F32), axis=0)
            for row, value in enumerate((bias, gain, shift, jnp.sum(upstream, axis=0))):
                sums[4 + row : 5 + row, :] += value[None]

        chunks(tokens, CHUNK, leave)


def hidden_backward(
    dy, acts, residual, slope, down_weights, weights, unit_count, vec, jobs, collective_id
):
    tokens = dy.shape[0]
    units = slope.shape[1]
    return fused_call(
        hidden_back_body,
        units // UNITS,
        [
            whole(dy),
            whole(acts),
            whole(residual),
            block(slope, (tokens, UNITS), lambda n: (0, n)),
            unit_rows(down_weights, unit_count, UNITS),
            unit_rows(weights, unit_count, UNITS),
            whole(vec),
        ],
        [
            result((units, D), BF, (UNITS, D), lambda n: (n, 0)),
            result((1, units), F32, (1, UNITS), lambda n: (0, n)),
            result((tokens, D), F32),
            result((tokens, D), BF),
            result((8, D), F32),
        ],
        [pltpu.VMEM((tokens, D), F32), pltpu.VMEM((tokens, UNITS), BF)],
        jobs,
        collective_id,
        ticks=3,
        cost=(0, 5, 5),
        stagger=10.0,
    )


def output_body(t, tick, hidden, down, residual, vec, out, total):
    accumulate(t, total, dot_nn(hidden[...], flat(down)))

    @pl.when(t == pl.num_programs(0) - 1)
    def _():
        def leave(rows):
            out[rows, :] = (residual[rows, :] + total[rows, :] + vec[7:8, :]).astype(BF)

        chunks(hidden.shape[0], CHUNK, leave)


def output_part(hidden, down_weights, unit_count, residual, vec):
    tokens = hidden.shape[0]
    return (
        output_body,
        [
            block(hidden, (tokens, UNITS), lambda n: (0, n)),
            unit_rows(down_weights, unit_count, UNITS),
            whole(residual),
            whole(vec),
        ],
        [result((tokens, D), BF)],
        [pltpu.VMEM((tokens, D), F32)],
        (0, 1.7, 2),
    )


def attend_back_body(
    t, tick, dh_low, out_w, mixed, acts, qkv, lse, sums_in,
    out_t, qkv_t, grads_out, sums, upstream, dk, dv,
):
    length = acts.shape[0]
    scale = HEAD_DIM ** (-0.5)
    grads = grads_out.at[0]

    @pl.when(t == 0)
    def _():
        def enter(rows):
            value = dot_nn(dh_low[rows, :], flat(out_w)).astype(BF)
            for head in range(HEADS):
                upstream[head, rows, :] = value[:, head * HEAD_DIM : (head + 1) * HEAD_DIM]

        chunks(length, 2 * CHUNK, enter)
        out_t[...] = dot_tn(dh_low[...], mixed[...]).astype(BF)
        sums[...] = sums_in[...]

    slope = head_slope(t)
    keys_t = qkv[1].astype(F32).T.astype(BF)
    for start in reversed(range(0, length, QUERY_BLOCK)):
        rows = start + QUERY_BLOCK
        query = qkv[0, start:rows, :]
        above = upstream[t, start:rows, :]
        scores = scores_t(query, qkv[1, :rows, :], slope, start, rows)
        probs = jnp.exp(scores - lse[0, :, start:rows])
        prob_grad = dot_nt(qkv[2, :rows, :], above)
        weighted = probs * prob_grad
        centered = jnp.sum(weighted, axis=0, keepdims=True)
        score_grad = (weighted - probs * centered).astype(BF)
        query_grad = dot_nn(keys_t[:, :rows], score_grad) * scale
        grads[start:rows, :HEAD_DIM] = query_grad.T.astype(BF)
        key_part = dot_nn(score_grad, query)
        value_part = dot_nn(probs.astype(BF), above)
        if rows == length:
            dk[...] = key_part
            dv[...] = value_part
        else:
            dk[:rows, :] += key_part
            dv[:rows, :] += value_part
        tick((length - start) // QUERY_BLOCK)
    grads[:, HEAD_DIM : 2 * HEAD_DIM] = (dk[...] * scale).astype(BF)
    grads[:, 2 * HEAD_DIM :] = dv[...].astype(BF)
    totals = jnp.sum(grads[...].astype(F32), axis=0, keepdims=True)
    lanes = pl.ds(pl.multiple_of(t * HEAD_DIM, HEAD_DIM), HEAD_DIM)
    sums[2:3, lanes] = totals[:, :HEAD_DIM]
    sums[3:4, lanes] = totals[:, 2 * HEAD_DIM :]
    weight_grad = dot_tn(grads[...], acts[...]).astype(BF)
    for part in range(3):
        qkv_t[part] = weight_grad[part * HEAD_DIM : (part + 1) * HEAD_DIM, :]


def attend_backward(dh_low, weights, widths, mixed, acts, qkv, lse, sums, jobs, collective_id):
    tokens = acts.shape[0]
    return fused_call(
        attend_back_body,
        HEADS,
        [
            whole(dh_low),
            rows_of(weights, *widths),
            whole(mixed),
            whole(acts),
            block(qkv, (3, tokens, HEAD_DIM), lambda h: (0, 0, h)),
            block(lse, (1, 1, tokens), lambda h: (h, 0, 0)),
            whole(sums),
        ],
        [
            result((D, D), BF),
            result((3, D, D), BF, (3, HEAD_DIM, D), lambda h: (0, h, 0)),
            result(
                (HEADS, tokens, 3 * HEAD_DIM), BF, (1, tokens, 3 * HEAD_DIM), lambda h: (h, 0, 0)
            ),
            result((8, D), F32),
        ],
        [
            pltpu.VMEM((HEADS, tokens, HEAD_DIM), BF),
            pltpu.VMEM((tokens, HEAD_DIM), F32),
            pltpu.VMEM((tokens, HEAD_DIM), F32),
        ],
        jobs,
        collective_id,
        ticks=5,
        cost=(7, 5.4, 0),
        stagger=0.1,
    )


def input_body(t, tick, grads, wq, wk, wv, x, dh, vec, grad_in, sums, back):
    weights = jnp.concatenate([wq[...], wk[...], wv[...]], axis=0)
    accumulate(t, back, dot_nn(grads[0], weights))

    @pl.when(t == pl.num_programs(0) - 1)
    def _():
        sums[...] = jnp.zeros_like(sums)

        def leave(rows):
            normed, inverse = layer_norm(x[rows, :].astype(F32), 1.0, 0.0)[1:]
            change, gain, shift = norm_backward(back[rows, :], normed, inverse, vec[0:1, :])
            grad_in[rows, :] = (dh[rows, :] + change).astype(BF)
            sums[0:1, :] += gain[None]
            sums[1:2, :] += shift[None]

        chunks(x.shape[0], CHUNK, leave)


def input_part(grads, qkv_full, x, dh, vec):
    tokens = x.shape[0]
    head_rows = lambda part: block(qkv_full, (HEAD_DIM, D), lambda h: (part * HEADS + h, 0))
    return (
        input_body,
        [
            block(grads, (1, tokens, 3 * HEAD_DIM), lambda h: (h, 0, 0)),
            head_rows(0),
            head_rows(1),
            head_rows(2),
            whole(x),
            whole(dh),
            whole(vec),
        ],
        [result((tokens, D), BF), result((8, D), F32)],
        [pltpu.VMEM((tokens, D), F32)],
        (0, 2, 6),
    )


def owner_place(owner):
    return owner // 16, (owner // 8) % 2, (owner // 4) % 2, owner % 4


def forward_body(
    t, tick, gathered, x, dy, qkv, mixed, lse, acts_one, residual, acts, hidden, slope, down_t, vec,
    small, qkv_w, up_w, out_w, bias, small_sem, qkv_sem, up_sem, out_sem,
):
    small_all, qkv_all, up_all, _ = gathered
    length = x.shape[0]
    owned = qkv_w.shape[4]
    up_rows = up_w.shape[2]
    out_rows = out_w.shape[4]

    def load_up(n):
        dst = up_w.at[n % 2]
        src = up_all.at[n // 4, (n // 2) % 2, n % 2, :, pl.ds(0, up_rows)]
        return pltpu.make_async_copy(src, dst, up_sem.at[n % 2])

    def load_out():
        return pltpu.make_async_copy(
            up_all.at[:, :, :, :, pl.ds(up_rows, out_rows)], out_w, out_sem
        )

    @pl.when(t == 0)
    def _():
        weights = pltpu.make_async_copy(qkv_all, qkv_w, qkv_sem)
        vectors = pltpu.make_async_copy(small_all, small, small_sem)
        weights.start()
        vectors.start()
        vectors.wait()
        for group in range(8):
            total = jnp.zeros((8, 128), F32)
            for z in range(4):
                part = small[group // 4, (group // 2) % 2, group % 2, z].astype(F32)
                total = total + part[:8, :]
                at = (group * 4 + z) * 128
                bias[:, at : at + 128] = part[8:9, :]
            vec[:, group * 128 : (group + 1) * 128] = total

        def norm(rows):
            normed = layer_norm(x[rows, :].astype(F32), vec[0:1, :], vec[1:2, :])[0]
            acts_one[rows, :] = normed.astype(BF)

        chunks(length, CHUNK, norm)
        weights.wait()

    @pl.when(t < HEADS)
    def _():
        unit = math.gcd(owned, HEAD_DIM)
        pieces = []
        for part in range(3):
            for i in range(HEAD_DIM // unit):
                index = (part * HEADS + t) * (HEAD_DIM // unit) + i
                per_owner = owned // unit
                row = pl.multiple_of((index % per_owner) * unit, unit)
                pieces.append(qkv_w[(*owner_place(index // per_owner), pl.ds(row, unit))])
        lanes = pl.ds(pl.multiple_of(t * HEAD_DIM, HEAD_DIM), HEAD_DIM)
        projected = dot_nt(acts_one[...], jnp.concatenate(pieces, axis=0))
        qkv[0] = (projected[:, :HEAD_DIM] + vec[2:3, lanes]).astype(BF)
        qkv[1] = projected[:, HEAD_DIM : 2 * HEAD_DIM].astype(BF)
        values = projected[:, 2 * HEAD_DIM :] + vec[3:4, lanes]
        qkv[2] = values.astype(BF)
        values_t = values.T.astype(BF)
        tick(1, 0, HEADS)
        level = head_slope(t)
        for start in range(0, length, QUERY_BLOCK):
            rows = start + QUERY_BLOCK
            scores = scores_t(qkv[0, start:rows, :], qkv[1, :rows, :], level, start, rows)
            highest = jnp.max(scores, axis=0, keepdims=True)
            weights = jnp.exp(scores - highest)
            totals = jnp.sum(weights, axis=0, keepdims=True)
            mix = dot_nn(values_t[:, :rows], weights.astype(BF)) / totals
            mixed[start:rows, lanes] = mix.T.astype(BF)
            lse[0, :, start:rows] = highest + jnp.log(totals)
            if rows < length:
                tick(2 + start // QUERY_BLOCK, 0, HEADS)

    @pl.when(t == HEADS)
    def _():
        load_out().start()
        load_up(0).start()
        load_out().wait()

        def enter(rows):
            attended = dot_nt(mixed[rows, :], flat(out_w)) + vec[4:5, :]
            here = x[rows, :].astype(F32) + attended
            residual[rows, :] = here
            acts[rows, :] = layer_norm(here, vec[5:6, :], vec[6:7, :])[0].astype(BF)

        chunks(length, 2 * CHUNK, enter)

    @pl.when(t >= HEADS)
    def _():
        n = t - HEADS
        load_up(n).wait()

        @pl.when(t < pl.num_programs(0) - 1)
        def _():
            load_up(n + 1).start()

        weights = up_w.at[n % 2]
        lanes = pl.ds(pl.multiple_of(n * UNITS, UNITS), UNITS)
        for start in range(0, length, 256):
            rows = slice(start, start + 256)
            pre = dot_nt(acts[rows, :], flat(weights)) + bias[:, lanes]
            value, steep = gelu_pair(pre)
            hidden[rows, :] = value.astype(BF)
            slope[rows, :] = steep.astype(BF)
            tick(1 + start // 256, HEADS)
        down_t[...] = dot_tn(hidden[...], dy[...]).astype(BF)


def forward(x, dy, small, qkv_w, up_set, down_set, units_rows, out_rows, collective_id):
    tokens = x.shape[0]
    units = 32 * units_rows
    steps = HEADS + units // UNITS
    head = lambda t: jnp.minimum(t, HEADS - 1)
    unit = lambda t: jnp.maximum(t - HEADS, 0)
    jobs = [Gather(small), Gather(qkv_w), Gather(up_set), Gather(down_set)]

    def timeline(ends):
        spans = [(ends[1] + 4 + 3.5 * i, 3.5) for i in range(HEADS)]
        start = max(ends[1] + 4 + 3.5 * HEADS, ends[2])
        return spans + [(start + 5 * (i > 0) + 4 * i, 4) for i in range(steps - HEADS)]

    column = result((tokens, units), BF, (tokens, UNITS), lambda t: (0, unit(t)))
    return fused_call(
        forward_body,
        steps,
        [whole(x), whole(dy)],
        [
            result((3, tokens, D), BF, (3, tokens, HEAD_DIM), lambda t: (0, 0, head(t))),
            result((tokens, D), BF),
            result((HEADS, 1, tokens), F32, (1, 1, tokens), lambda t: (head(t), 0, 0)),
            result((tokens, D), BF),
            result((tokens, D), F32),
            result((tokens, D), BF),
            column,
            column,
            result((units, D), BF, (UNITS, D), lambda t: (unit(t), 0)),
            result((8, D), F32),
        ],
        [
            pltpu.VMEM(jobs[0].shape.shape, BF),
            pltpu.VMEM(jobs[1].shape.shape, BF),
            pltpu.VMEM((2, 4, units_rows, D), BF),
            pltpu.VMEM((2, 2, 2, 4, out_rows, D), BF),
            pltpu.VMEM((1, units), F32),
            pltpu.SemaphoreType.DMA,
            pltpu.SemaphoreType.DMA,
            pltpu.SemaphoreType.DMA((2,)),
            pltpu.SemaphoreType.DMA,
        ],
        jobs,
        collective_id,
        ticks=5,
        stagger=36.0,
        needs={0: 0, 1: 0, 2: HEADS, 3: steps},
        timeline=timeline,
    )


def renew_body(
    t, tick, own, full, root, n_stat, m_stat, m_root, weight, new_n, new_m, new_w, left, product
):
    last = pl.num_programs(0) - 1
    me = lax.axis_index("dp") * lax.axis_size("ffn") + lax.axis_index("ffn")
    rows_owned = m_stat.shape[0]
    share = 128 // rows_owned
    lanes = pl.ds(pl.multiple_of((me // share) * 128, 128), 128)
    here = flat(full)
    new_n[...] = decay_rate * n_stat[...] + (1.0 - decay_rate) * dot_nt(own[...], here)
    left_part = dot_tn(full[:, :, lanes].reshape(-1, 128), here)
    product_part = dot_nn(root[...].astype(BF), here)

    @pl.when(t == 0)
    def _():
        left[...] = left_part
        product[...] = product_part

    @pl.when(t > 0)
    def _():
        left[...] += left_part
        product[...] += product_part

    @pl.when(t == last)
    def _():
        mine = left[pl.ds(pl.multiple_of((me % share) * rows_owned, rows_owned), rows_owned), :]
        new_m[...] = decay_rate * m_stat[...] + (1.0 - decay_rate) * mine
        step = dot_nt(product[...].astype(BF), flat(m_root))
        new_w[...] = weight[...] - matrix_rate * step


def renew(
    own, gathered, at, n_root, n_stat, m_stat, roots, root_at, weight, jobs, collective_id, part=None
):
    rows, total = own.shape[0], n_stat.shape[1]
    rows_owned = m_stat.shape[0]
    body, ins, outs, scratch, more = part or (None, [], [], [], (0, 0, 0))
    if not on_fast_grid():
        extra = fused_call(body, 8, ins, outs, scratch, [], collective_id)[0] if part else []
        full = gathered[:, at : at + rows].reshape(-1, D)
        m_root = roots[:, root_at : root_at + rows_owned].reshape(-1, D)
        me = lax.axis_index("dp") * lax.axis_size("ffn") + lax.axis_index("ffn")
        new_n = decay_rate * n_stat + (1.0 - decay_rate) * dot_nt(own, full)
        mine = lax.dynamic_slice_in_dim(full, me * rows_owned, rows_owned, 1)
        new_m = decay_rate * m_stat + (1.0 - decay_rate) * dot_tn(mine, full)
        product = dot_nn(n_root.astype(BF), full)
        new_w = weight - matrix_rate * dot_nt(product.astype(BF), m_root)
        return [new_n, new_m, new_w] + extra, [job.plainly() for job in jobs]
    owners = 16 if rows == 32 else 4
    size = owners * rows
    column = lambda array: block(array, (rows, size), lambda n: (0, n))
    own_ins = [
        whole(own),
        block(gathered, (owners, rows, D), lambda n: (n, at // rows, 0)),
        column(n_root),
        column(n_stat),
        whole(m_stat),
        rows_of(roots, root_at, rows_owned),
        whole(weight),
    ]
    own_outs = [
        result((rows, total), F32, (rows, size), lambda n: (0, n)),
        result((rows_owned, D), F32),
        result((rows, D), F32),
    ]
    own_scratch = [pltpu.VMEM((128, D), F32), pltpu.VMEM((rows, D), F32)]
    sizes = [len(own_ins), len(ins), len(own_outs), len(outs), len(own_scratch), len(scratch)]

    def both(t, tick, *refs):
        cuts = [sum(sizes[:i]) for i in range(len(sizes) + 1)]
        groups = [refs[i:j] for i, j in zip(cuts, cuts[1:])]
        renew_body(t, tick, *groups[0], *groups[2], *groups[4])
        if part:
            tick(1)
            body(t, tick, *groups[1], *groups[3], *groups[5])

    return fused_call(
        both,
        total // size,
        own_ins + ins,
        own_outs + outs,
        own_scratch + scratch,
        jobs,
        collective_id,
        ticks=2 if part else 1,
        cost=(0, 1.6 + more[1], 1 + more[2]),
        stagger=0.1 if len(jobs) > 2 else 14.0,
    )


SMALL_ROWS = 32
SMALL_WIDTH = 128


def pack_small(vector_part, bias_part):
    owners = vector_part.shape[0]
    flat = jnp.concatenate([vector_part.reshape(owners, -1), bias_part.reshape(owners, -1)], axis=1)
    room = SMALL_ROWS * SMALL_WIDTH
    flat = jnp.pad(flat, ((0, 0), (0, room - flat.shape[1])))
    return flat.reshape(owners * SMALL_ROWS, SMALL_WIDTH)


def unpack_small(packed, columns, units):
    owners = packed.shape[0] // SMALL_ROWS
    flat = packed.reshape(owners, -1)
    vector_part = flat[:, : 8 * columns].reshape(owners, 8, columns)
    bias_part = flat[:, 8 * columns : 8 * columns + units]
    return vector_part, bias_part


def shards(
    block_input,
    cotangent,
    w_qkv,
    w_out,
    w_up,
    w_down,
    vectors,
    b_up,
    qkv_left,
    qkv_right,
    out_left,
    out_right,
    up_left,
    up_right,
    down_left,
    down_right,
    qkv_left_root,
    qkv_right_root,
    out_left_root,
    out_right_root,
    up_left_root,
    up_right_root,
    down_left_root,
    down_right_root,
    vector_stat,
    b_up_stat,
):
    owners = lax.axis_size("dp") * lax.axis_size("ffn")
    columns = vectors.shape[1]
    units = b_up.shape[0]
    qkv_w, out_w, up_w = w_qkv.T, w_out.T, w_up.T
    units_rows, qkv_rows, out_rows = units, qkv_w.shape[0], out_w.shape[0]
    root_rows = qkv_left_root.shape[0]

    def stack(*items):
        return Gather(jnp.concatenate([item.astype(BF) for item in items], axis=0))

    def by_owner(array):
        return array.reshape(owners, -1, D)

    up_block = [up_w, out_w]
    down_block = [w_down, out_left_root, qkv_left_root]
    if on_fast_grid():
        lane = (lax.axis_index("ffn") * columns).astype(jnp.int32)
        small = jnp.zeros((SMALL_ROWS, SMALL_WIDTH), BF)
        small = lax.dynamic_update_slice(small, vectors.astype(BF), (0, lane))
        small = lax.dynamic_update_slice(small, b_up.astype(BF)[None], (8, 0))
        results, gathered = forward(
            block_input,
            cotangent,
            small,
            qkv_w.astype(BF),
            stack(*up_block).array,
            stack(*down_block).array,
            units_rows,
            out_rows,
            1,
        )
        qkv, mixed, logsum, acts_one, residual, acts_two, hidden, slope, down_t, vector_rows = results
        _, qkv_full, up_set, down_set = gathered
        up_set, down_set = by_owner(up_set), by_owner(down_set)
    else:
        small = pack_small(vectors[None], b_up[None]).astype(BF)
        small_full, qkv_full = transfer([Gather(small), Gather(qkv_w.astype(BF))], 1)
        vector_low, bias_low = unpack_small(small_full, columns, units)
        vector_rows = vector_low.transpose(1, 0, 2).reshape(8, D).astype(F32)
        up_bias = bias_low.reshape(1, -1).astype(F32)
        (qkv, mixed, logsum, acts_one), (up_set,) = attend(
            block_input, vector_rows, qkv_full, [stack(*up_block)], 2
        )
        up_set = by_owner(up_set)
        (residual, acts_two, hidden, slope, down_t), (down_set,) = hidden_forward(
            block_input,
            mixed,
            up_set,
            (units_rows, out_rows),
            vector_rows,
            cotangent,
            up_bias,
            [stack(*down_block)],
            3,
        )
        down_set = by_owner(down_set)
    (up_t, bias_grad, dh, dh_low, sums), (down_g, down_mroot) = hidden_backward(
        cotangent,
        acts_two,
        residual,
        slope,
        down_set,
        up_set,
        units_rows,
        vector_rows,
        [Reduce(down_t), stack(down_right_root)],
        4,
    )
    down_low = down_g.astype(BF)
    (out_t, qkv_t, qkv_grads, sums), (up_g, down_all) = attend_backward(
        dh_low,
        up_set,
        (units_rows, out_rows),
        mixed,
        acts_one,
        qkv,
        logsum,
        sums,
        [Reduce(up_t), Gather(down_low)],
        5,
    )
    up_low = up_g.astype(BF)
    (new_down_n, new_down_m, new_w_down, input_grad, first_sums), (up_all, qkv_g, out_g) = renew(
        down_low,
        by_owner(down_all),
        0,
        down_left_root,
        down_left,
        down_right,
        by_owner(down_mroot),
        0,
        w_down,
        [stack(up_low, up_left_root), Reduce(qkv_t.reshape(-1, D)), Reduce(out_t)],
        6,
        input_part(qkv_grads, qkv_full, block_input, dh, vector_rows),
    )
    small_part = pack_small(
        (sums + first_sums).reshape(8, owners, columns).transpose(1, 0, 2),
        bias_grad.reshape(owners, units),
    ).astype(BF)
    qkv_low, out_low = qkv_g.astype(BF), out_g.astype(BF)
    up_all = by_owner(up_all)
    (new_up_n, new_up_m, new_w_up, block_output), (last_all, small_g) = renew(
        up_low,
        up_all,
        0,
        up_right_root,
        up_right,
        up_left,
        up_all,
        units_rows,
        up_w,
        [stack(qkv_low, out_low), Reduce(small_part)],
        7,
        output_part(hidden, down_set, units_rows, residual, vector_rows),
    )
    last_all = by_owner(last_all)
    new_qkv_n, new_qkv_m, new_w_qkv = renew(
        qkv_low,
        last_all,
        0,
        qkv_right_root,
        qkv_right,
        qkv_left,
        down_set,
        units_rows + root_rows,
        qkv_w,
        [],
        8,
    )[0]
    new_out_n, new_out_m, new_w_out = renew(
        out_low,
        last_all,
        qkv_rows,
        out_right_root,
        out_right,
        out_left,
        down_set,
        units_rows,
        out_w,
        [],
        8,
    )[0]
    new_m = [new_qkv_m, new_out_m, new_up_m, new_down_m]
    new_n = [new_qkv_n, new_out_n, new_up_n, new_down_n]
    new_w_qkv, new_w_out, new_w_up = new_w_qkv.T, new_w_out.T, new_w_up.T
    grads = [qkv_g, out_g, up_g, down_g]
    vector_grad, b_up_grad = unpack_small(small_g, columns, units)
    vector_grad, b_up_grad = vector_grad[0], b_up_grad[0]
    new_vector_stat = decay_rate * vector_stat + (1.0 - decay_rate) * vector_grad * vector_grad
    new_vectors = vectors - vector_rate * vector_grad * lax.rsqrt(new_vector_stat)
    new_b_up_stat = decay_rate * b_up_stat + (1.0 - decay_rate) * b_up_grad * b_up_grad
    new_b_up = b_up - vector_rate * b_up_grad * lax.rsqrt(new_b_up_stat)
    return (
        block_output,
        input_grad,
        grads[0].T,
        grads[1].T,
        grads[2].T,
        grads[3],
        vector_grad,
        b_up_grad,
        new_m[0],
        new_n[0],
        new_m[1],
        new_n[1],
        new_m[2],
        new_n[2],
        new_n[3],
        new_m[3],
        new_vector_stat,
        new_b_up_stat,
        new_w_qkv,
        new_w_out,
        new_w_up,
        new_w_down,
        new_vectors,
        new_b_up,
    )


def solution(mesh):
    return jax.shard_map(
        shards,
        mesh=mesh,
        in_specs=(
            P(("dp", "ffn"), None),
            P(("dp", "ffn"), None),
            P(None, ("dp", "ffn")),
            P(None, ("dp", "ffn")),
            P(None, ("dp", "ffn")),
            P(("dp", "ffn"), None),
            P(None, ("dp", "ffn")),
            P(("dp", "ffn")),
            P(("dp", "ffn"), None),
            P(("dp", "ffn"), None),
            P(("dp", "ffn"), None),
            P(("dp", "ffn"), None),
            P(("dp", "ffn"), None),
            P(("dp", "ffn"), None),
            P(("dp", "ffn"), None),
            P(("dp", "ffn"), None),
            P(("dp", "ffn"), None),
            P(("dp", "ffn"), None),
            P(("dp", "ffn"), None),
            P(("dp", "ffn"), None),
            P(("dp", "ffn"), None),
            P(("dp", "ffn"), None),
            P(("dp", "ffn"), None),
            P(("dp", "ffn"), None),
            P(None, ("dp", "ffn")),
            P(("dp", "ffn")),
        ),
        out_specs=(
            P(("dp", "ffn"), None),
            P(("dp", "ffn"), None),
            P(None, ("dp", "ffn")),
            P(None, ("dp", "ffn")),
            P(None, ("dp", "ffn")),
            P(("dp", "ffn"), None),
            P(None, ("dp", "ffn")),
            P(("dp", "ffn")),
            P(("dp", "ffn"), None),
            P(("dp", "ffn"), None),
            P(("dp", "ffn"), None),
            P(("dp", "ffn"), None),
            P(("dp", "ffn"), None),
            P(("dp", "ffn"), None),
            P(("dp", "ffn"), None),
            P(("dp", "ffn"), None),
            P(None, ("dp", "ffn")),
            P(("dp", "ffn")),
            P(None, ("dp", "ffn")),
            P(None, ("dp", "ffn")),
            P(None, ("dp", "ffn")),
            P(("dp", "ffn"), None),
            P(None, ("dp", "ffn")),
            P(("dp", "ffn")),
        ),
        check_vma=False,
    )
```
